256 devices in a mesh: seq: 32 (over z, y), ch: 8 (over x, core).
Axes of the slice: x: 4, y: 4, z: 8, core: 2. Of those that a mesh axis runs over, the one named last changes fastest.
Arguments:
- signal: bfloat16 [8192, 4, 768], P('seq', None, 'ch'), may hold values from -6 to 6
- filter_taps: float32 [8192, 768], P('seq', 'ch'), may hold values from -2 to 2
- skip_gain: float32 [768], P('ch'), may hold values from 0.5 to 1.5
- w_gate: bfloat16 [768, 768], P(None, 'ch'), may hold values from -0.21875 to 0.21875
- w_out: bfloat16 [768, 768], P('ch'), may hold values from -0.21875 to 0.21875
- catalogue: bfloat16 [524288, 768], P(('seq', 'ch')), may hold values from -6 to 6
- item_draw_counts: int32 [524288], P(('seq', 'ch')), may hold values from 1 to 8
- sampled_pos: int32 [4096], P('seq'), may hold values from 0 to 1023
- neg_owner: int32 [4096, 64, 1], P('seq'), may hold values from 0 to 255; in each aligned block of 8192 rows (0 to 8191, 8192 to 16383, ..., all dimensions but the last counted through in order) at most 64 rows name the same one
- neg_row: int32 [4096, 64], P('seq'), may hold values from 0 to 2047
- target_owner: int32 [4096, 1], P('seq'), may hold values from 0 to 255; in each aligned block of 128 rows (0 to 127, 128 to 255, ...) at most 2 rows name the same one
- target_row: int32 [4096], P('seq'), may hold values from 0 to 2047
Outputs:
- layer_out: bfloat16 [8192, 4, 768], P('seq', None, 'ch')
- sample_loss: float32 [4096], P('seq')
The draws below stay inside these ranges and needn't reach their ends.
Inputs may be any that keep to these rules, and one draw needn't show every extreme that they name: `neg_owner`: shard index, devices in seq-major order; of the 8192 samples of one device's positions at most 64 name one shard, a bound that some block reaches. `target_owner`: shard index, devices in seq-major order; of the 128 targets of one device's positions at most 2 name one shard, a bound that some block reaches.
All inputs are finite; a program needn't handle non-finite values.
Results may differ from the reference program's by a relative error of at most 0.007.
Values may be sent and summed in bfloat16 or wider, within the bound.
A program may use at most 128 MiB of HBM per device.

```python
import math
import jax
import jax.numpy as jnp
import numpy as np
from jax import lax

CHANNEL_COUNT = 768
SEQS = 4
TOK_DEV = 256
POS_DEV = 128
NEG = 64
CAT_DEV = 2048
L = 8192
POSITIONS = 4096
ITEMS = 524288
NEG_CAP = 64
TGT_CAP = 2
N_SEQ = 32
N_CH = 8
DEVICES = 256


def draw_filter_taps(key, part):
    key = jax.random.fold_in(key, 11)
    rate_key, noise_key = jax.random.split(key)
    rate = jnp.exp(jax.random.uniform(rate_key, (CHANNEL_COUNT,), jnp.float32, math.log(2.0 / L), math.log(1.0 / 40.0)))
    noise = jax.random.normal(noise_key, (L, CHANNEL_COUNT), jnp.float32)
    steps_idx = jnp.arange(L, dtype=jnp.float32)[:, None]
    return noise * jnp.sqrt(2.0 * rate) * jnp.exp(-rate * steps_idx)


def set_ends(values, stream_key, low, high):
    shape = values.shape
    index_at = [jax.random.randint(jax.random.fold_in(stream_key, axis), (), 0, shape[axis]) for axis in range(len(shape))]
    values = values.at[tuple(index_at)].set(low)
    longest = shape.index(max(shape))
    index_at[longest] = (index_at[longest] + 1) % shape[longest]
    return values.at[tuple(index_at)].set(high)


def level_of(rng, shape, cuts, low, high):
    loudness, own = 1.0, jax.random.fold_in(rng, 6)
    for dim, shards_of in cuts:
        draws = jnp.exp(jax.random.uniform(jax.random.fold_in(own, dim), (shards_of,), jnp.float32, low / len(cuts), high / len(cuts)))
        loudness = loudness * jnp.repeat(draws, shape[dim] // shards_of).reshape([-1 if axis == dim else 1 for axis in range(len(shape))])
    return loudness


def shared_out(key, own, number, rows, count, top, reach, lean):
    sequence = jax.random.permutation(key, count)
    crowded, usual = shares(count, rows * top, reach, lean, True), shares(count, rows * top, reach, lean, False)
    places = jnp.arange(count)

    def named(lengths, offset_by):
        used = int((lengths > 0).sum())
        fixed = max(1, used // 4)
        passed = fixed + (places - fixed + offset_by * (used - fixed)) % max(1, count - fixed)
        return jnp.zeros((count,), jnp.int32).at[sequence[jnp.where(places < fixed, places, passed)]].set(jnp.asarray(lengths, jnp.int32))

    lengths = jnp.where(number % 4 == 0, named(crowded, number // 4), named(usual, number - number // 4 - 1))
    mixed = jax.random.permutation(jax.random.fold_in(own, 3), count)
    giver, receiver = mixed[0:count // 2 * 2:2], mixed[1:count // 2 * 2:2]
    margin = jnp.minimum(lengths[giver] - 1, reach - lengths[receiver]) // 2
    margin = jnp.where((giver == sequence[0]) | (receiver == sequence[0]) | (lengths[receiver] == 0), 0, jnp.maximum(margin, 0))
    passed = jax.random.randint(jax.random.fold_in(own, 4), (count // 2,), 0, 1 << 20) % (margin + 1)
    lengths = lengths.at[giver].add(-passed).at[receiver].add(passed)
    labels = jnp.searchsorted(jnp.cumsum(lengths), jnp.arange(rows * top), side="right").astype(jnp.int32)
    listing = labels.reshape(top, rows).T
    listing = listing[jax.random.permutation(jax.random.fold_in(own, 1), rows)]
    offset_by = jax.random.randint(jax.random.fold_in(own, 2), (rows, 1), 0, top)
    return jnp.take_along_axis(listing, (jnp.arange(top)[None, :] + offset_by) % top, axis=1)


def shares(number_of, total, limit, skew, full):
    loads = [(1 << 20) // math.isqrt(rank ** skew) + 1 for rank in range(1, number_of + 1)]
    largest = limit if full else min(limit, max(-(-total // number_of), total * loads[0] // sum(loads)))
    least = 1 if total - largest >= number_of - 1 else 0
    given, rest = [largest] + [least] * (number_of - 1), total - largest - least * (number_of - 1)
    while rest > 0:
        candidates = [i for i in range(1, number_of) if given[i] < largest] or [i for i in range(1, number_of) if given[i] < limit]
        whole, left = sum([loads[i] for i in candidates]), rest
        for i in candidates:
            more = min(limit - given[i], max(1, left * loads[i] // whole), rest)
            given[i] = given[i] + more
            rest = rest - more
    return np.array(given)


def scatter_about(rng, shape, spread, bound, shards=(), kind=jnp.bfloat16):
    loudness = level_of(rng, shape, shards, -0.22, 0.18) if shards else 1.0
    drawn = jax.random.normal(rng, shape, jnp.float32) * spread * loudness
    return jnp.minimum(jnp.maximum(drawn, -bound), bound).astype(kind)


def setup_inputs(seed: int = 0) -> dict:
    key_of = jax.random.split(jax.random.key(seed), 13)
    signal = scatter_about(key_of[0], (L, SEQS, CHANNEL_COUNT), 1.0, 6.0, ((0, 32), (2, 8)))
    filter_taps = draw_filter_taps(jax.random.fold_in(key_of[12], 71), 0)
    skip_gain = jnp.clip(0.5 + 1.0 * jax.random.uniform(key_of[2], (CHANNEL_COUNT,), jnp.float32) ** level_of(key_of[2], (CHANNEL_COUNT,), ((0, 8),), -0.2, 0.2), 0.5, 1.5)
    w_gate = scatter_about(key_of[3], (CHANNEL_COUNT, CHANNEL_COUNT), CHANNEL_COUNT ** -0.5, 0.21875, ((1, 8),))
    w_out = scatter_about(key_of[4], (CHANNEL_COUNT, CHANNEL_COUNT), CHANNEL_COUNT ** -0.5, 0.21875, ((0, 8),))
    catalogue = scatter_about(key_of[5], (ITEMS, CHANNEL_COUNT), 1.0, 6.0, ((0, 256),))
    item_draw_counts = set_ends(jax.random.randint(key_of[6], (ITEMS,), 1, 9), jax.random.fold_in(key_of[6], 1), 1, 8).astype(jnp.int32)
    sampled_pos = set_ends(jax.random.randint(key_of[7], (POSITIONS,), 0, TOK_DEV * SEQS), jax.random.fold_in(key_of[7], 1), 0, (TOK_DEV * SEQS) - 1).astype(jnp.int32)
    neg_owner_keys = jax.random.split(jax.random.fold_in(key_of[8], 1), POSITIONS * NEG // (POS_DEV * NEG))
    neg_owner_turns = jax.random.permutation(jax.random.fold_in(key_of[8], 3), POSITIONS * NEG // (POS_DEV * NEG))
    neg_owner = jax.vmap(lambda own, number: shared_out(jax.random.fold_in(key_of[8], 2), own, number, POS_DEV * NEG, DEVICES, 1, NEG_CAP, 2))(neg_owner_keys, neg_owner_turns).reshape((POSITIONS, NEG, 1))
    neg_row = set_ends(jax.random.randint(key_of[9], (POSITIONS, NEG), 0, CAT_DEV), jax.random.fold_in(key_of[9], 1), 0, CAT_DEV - 1).astype(jnp.int32)
    target_owner_keys = jax.random.split(jax.random.fold_in(key_of[10], 1), POSITIONS // POS_DEV)
    target_owner_turns = jax.random.permutation(jax.random.fold_in(key_of[10], 3), POSITIONS // POS_DEV)
    target_owner = jax.vmap(lambda own, number: shared_out(jax.random.fold_in(key_of[10], 2), own, number, POS_DEV, DEVICES, 1, TGT_CAP, 1))(target_owner_keys, target_owner_turns).reshape((POSITIONS, 1))
    target_row = set_ends(jax.random.randint(key_of[11], (POSITIONS,), 0, CAT_DEV), jax.random.fold_in(key_of[11], 1), 0, CAT_DEV - 1).astype(jnp.int32)
    return {"signal": signal, "filter_taps": filter_taps, "skip_gain": skip_gain, "w_gate": w_gate, "w_out": w_out, "catalogue": catalogue, "item_draw_counts": item_draw_counts, "sampled_pos": sampled_pos, "neg_owner": neg_owner, "neg_row": neg_row, "target_owner": target_owner, "target_row": target_row}


SOFTMAX_TEMP = 0.02
EPSILON = 1e-06

def causal_conv(signal, filter_taps):
    length = signal.shape[0]
    lane = signal.shape[2] // N_CH
    sig_blocks = jnp.moveaxis(signal.reshape(length, SEQS, N_CH, lane), 2, 0)
    tap_blocks = jnp.moveaxis(filter_taps.reshape(length, N_CH, lane), 1, 0)

    def one_block(pair):
        sig_part, tap_part = pair
        sig_freq = jnp.fft.rfft(sig_part.astype(jnp.float32), n=2 * length, axis=0)
        tap_freq = jnp.fft.rfft(tap_part, n=2 * length, axis=0)
        joined = jnp.fft.irfft(sig_freq * tap_freq[:, None, :], n=2 * length, axis=0)
        return joined[:length].astype(jnp.float32)
    result = lax.map(one_block, (sig_blocks, tap_blocks))
    return jnp.moveaxis(result, 0, 2).reshape(length, SEQS, signal.shape[2])

def reference(signal, filter_taps, skip_gain, w_gate, w_out, catalogue, item_draw_counts, sampled_pos, neg_owner, neg_row, target_owner, target_row):
    convolved = causal_conv(signal, filter_taps)
    flat_signal = signal.reshape(L * SEQS, CHANNEL_COUNT)
    gate_sum = jnp.dot(flat_signal, w_gate, preferred_element_type=jnp.float32).reshape(L, SEQS, CHANNEL_COUNT)
    gated_mix = ((convolved + skip_gain * signal.astype(jnp.float32)) * gate_sum).astype(jnp.bfloat16)
    layer_out = jnp.dot(gated_mix.reshape(L * SEQS, CHANNEL_COUNT), w_out, preferred_element_type=jnp.float32).astype(jnp.bfloat16)
    neg_item = neg_owner[:, :, 0] * CAT_DEV + neg_row
    target_item = target_owner[:, 0] * CAT_DEV + target_row
    block_base = jnp.arange(POSITIONS, dtype=jnp.int32) // POS_DEV * (TOK_DEV * SEQS)
    queries = layer_out[block_base + sampled_pos]

    def one_block(parts):
        query_rows, negative_item_ids, target_item_ids = parts
        query_f = query_rows.astype(jnp.float32)
        neg_rows = catalogue[negative_item_ids].astype(jnp.float32)
        tgt_rows = catalogue[target_item_ids].astype(jnp.float32)
        query_norm_scale = lax.rsqrt(lax.optimization_barrier(jnp.sum(query_f * query_f, -1)) / CHANNEL_COUNT + EPSILON)
        negative_scale = lax.rsqrt(lax.optimization_barrier(jnp.sum(neg_rows * neg_rows, -1)) / CHANNEL_COUNT + EPSILON)
        target_scale = lax.rsqrt(lax.optimization_barrier(jnp.sum(tgt_rows * tgt_rows, -1)) / CHANNEL_COUNT + EPSILON)
        negative_products = jnp.einsum('pc,pkc->pk', query_f, neg_rows)
        target_products = lax.optimization_barrier(jnp.sum(query_f * tgt_rows, -1))
        negative_logit = negative_products * query_norm_scale[:, None] * negative_scale / (CHANNEL_COUNT * SOFTMAX_TEMP) - jnp.log(item_draw_counts[negative_item_ids].astype(jnp.float32))
        target_logit = target_products * query_norm_scale * target_scale / (CHANNEL_COUNT * SOFTMAX_TEMP) - jnp.log(item_draw_counts[target_item_ids].astype(jnp.float32))
        return jnp.log(jnp.exp(target_logit) + lax.optimization_barrier(jnp.sum(jnp.exp(negative_logit), -1))) - target_logit
    sample_loss = lax.map(one_block, (queries.reshape(N_SEQ, POS_DEV, CHANNEL_COUNT), neg_item.reshape(N_SEQ, POS_DEV, NEG), target_item.reshape(N_SEQ, POS_DEV)))
    return (layer_out.reshape(L, SEQS, CHANNEL_COUNT), sample_loss.reshape(POSITIONS))
```

```python
import jax
import jax.numpy as jnp
from jax import lax
from jax.experimental import pallas as pl
from jax.experimental.pallas import tpu as pltpu
from jax.sharding import PartitionSpec as P

SOFTMAX_TEMP = 0.02
EPSILON = 1e-06
MESH = pl.DeviceIdType.MESH
BF16 = jnp.bfloat16
F32 = jnp.float32
I32 = jnp.int32

S = 32
C = 8
LANE = 128
CH = 96
FULL = CH * C
TOK = 1024
NEG = 64
GROUPS = 16
SLOTS = (GROUPS + 1) * LANE
ITEMS = 2048

(
    X_CONV,
    X_REQ,
    X_BACK,
    X_QUERY,
    X_SUMS,
    X_SIG,
    X_WGATE,
    X_WOUT,
    X_TABLE,
    X_ROWS,
    X_MIX,
    X_OUT,
    X_PART,
    X_FIN,
) = range(14)


def iota(shape, dim):
    return lax.broadcasted_iota(I32, shape, dim)


def onehot(mask):
    return jnp.where(mask, 1.0, 0.0).astype(BF16)


def dot(a, b, ca=1, cb=0):
    return lax.dot_general(a, b, (((ca,), (cb,)), ((), ())), preferred_element_type=F32)


def split_parts(value, count):
    parts = []
    for _ in range(count):
        piece = value.astype(BF16)
        parts.append(piece)
        value = value - piece.astype(F32)
    return parts


def body(
    sig,
    taps,
    gain,
    w_gate,
    w_out,
    cat,
    cnt,
    spos,
    nown,
    nrow,
    town,
    trow,
    out_ref,
    loss_ref,
    perm,
    sig_send,
    sig_all,
    msgf,
    msg1,
    rcv1,
    rf,
    xpad,
    x4,
    acc,
    msg2,
    rcv2,
    wg_own,
    wg_all,
    wo_all,
    wo_t,
    gate_t,
    mix_send,
    mix_all,
    lo_send,
    lo_all,
    q_own,
    q_all,
    req_msg,
    req_all,
    ohs,
    inner,
    total,
    keys,
    vals,
    tab_own,
    tab_all,
    cat_t,
    rows_send,
    rows_all,
    row_scale,
    row_log,
    ohp,
    oht,
    part,
    part_all,
    sums,
    sums_all,
    fin,
    fin_all,
    send_sem,
    recv_sem,
):
    me_s = lax.axis_index("seq")
    me_c = lax.axis_index("ch")

    def seq_copy(x, peer, src, dst):
        return pltpu.make_async_remote_copy(
            src_ref=src,
            dst_ref=dst,
            send_sem=send_sem.at[x, peer],
            recv_sem=recv_sem.at[x, me_s],
            device_id=(peer, me_c),
            device_id_type=MESH,
        )

    def ch_copy(x, peer, src, dst):
        return pltpu.make_async_remote_copy(
            src_ref=src,
            dst_ref=dst,
            send_sem=send_sem.at[x, peer],
            recv_sem=recv_sem.at[x, me_c],
            device_id=(me_s, peer),
            device_id_type=MESH,
        )

    def over(n, me, fn):
        def step(d, carry):
            fn(lax.rem(me + d, n))
            return carry

        lax.fori_loop(1, n, step, 0)

    def start_seq(x, src_of, dst):
        over(S, me_s, lambda peer: seq_copy(x, peer, src_of(peer), dst.at[me_s]).start())

    def start_ch(x, src_of, dst):
        over(C, me_c, lambda peer: ch_copy(x, peer, src_of(peer), dst.at[me_c]).start())

    def wait_from(x, peer, src, dst, device):
        pltpu.make_async_remote_copy(
            src_ref=src,
            dst_ref=dst,
            send_sem=send_sem.at[x, peer],
            recv_sem=recv_sem.at[x, peer],
            device_id=device,
            device_id_type=MESH,
        ).wait_recv()

    def wait_seq(x, src_of, dst):
        over(S, me_s, lambda peer: wait_from(x, peer, src_of(peer), dst.at[peer], (peer, me_c)))

    def wait_ch(x, src_of, dst):
        over(C, me_c, lambda peer: wait_from(x, peer, src_of(peer), dst.at[peer], (me_s, peer)))

    def sent_seq(x, src_of, dst):
        over(S, me_s, lambda peer: seq_copy(x, peer, src_of(peer), dst.at[me_s]).wait_send())

    def sent_ch(x, src_of, dst):
        over(C, me_c, lambda peer: ch_copy(x, peer, src_of(peer), dst.at[me_c]).wait_send())

    barrier = pltpu.get_barrier_semaphore()

    def greet_seq(peer):
        pl.semaphore_signal(barrier, inc=1, device_id=(peer, me_c), device_id_type=MESH)

    def greet_ch(peer):
        pl.semaphore_signal(barrier, inc=1, device_id=(me_s, peer), device_id_type=MESH)

    over(S, me_s, greet_seq)
    over(C, me_c, greet_ch)

    col = iota((TOK, TOK), 1)
    token = ((col >> 9) * LANE + (col & 127)) * 4 + ((col >> 7) & 3)
    perm[...] = onehot(iota((TOK, TOK), 0) == token)
    sig_t = dot(sig[...], perm[...], 0, 0)
    eye = onehot(iota((256, 256), 0) == iota((256, 256), 1))
    taps_t = dot(taps[...].astype(BF16), eye, 0, 0)
    msgf[...] = jnp.zeros_like(msgf)
    for q in range(8):
        piece = sig_t[:, q * LANE : (q + 1) * LANE]
        sig_send[q] = piece.astype(BF16)
        for k in range(3):
            msgf[pl.ds(k * 8 + q, S, stride=32), :] = piece[k * 32 : (k + 1) * 32]
    for il in range(2):
        piece = taps_t[:, il * LANE : (il + 1) * LANE]
        for k in range(3):
            msgf[pl.ds(24 + 2 * k + il, S, stride=32), :] = piece[k * 32 : (k + 1) * 32]
    msg1[...] = msgf[...].reshape(S, 32, LANE).astype(BF16)

    pl.semaphore_wait(barrier, S - 1 + C - 1)

    start_seq(X_CONV, lambda p: msg1.at[p], rcv1)
    rcv1[me_s] = msg1[me_s]
    start_ch(X_SIG, lambda p: sig_send.at[p], sig_all)
    sig_all[me_c] = sig_send[me_c]
    wg_own[...] = w_gate[...].astype(F32).T.astype(BF16)
    start_ch(X_WGATE, lambda p: wg_own, wg_all)
    wg_all[me_c] = wg_own[...]
    start_ch(X_WOUT, lambda p: w_out, wo_all)
    wo_all[me_c] = w_out[...]

    upper = onehot(iota((LANE, LANE), 0) < iota((LANE, LANE), 1))
    ones = jnp.ones((LANE, LANE), BF16)
    owner_ids = iota((S, LANE), 0)

    def own_onehot(owners):
        mine = jnp.where((owners & 7) == me_c, owners >> 3, -1)
        return jnp.where(owner_ids == mine, 1.0, 0.0)

    def mark(m, carry):
        ohs[pl.ds(pl.multiple_of(m * S, S), S), :] = own_onehot(nown[pl.ds(m, 1), :]).astype(BF16)
        return carry

    lax.fori_loop(0, 64, mark, 0)
    inner[...] = dot(ohs[...], upper)
    total[...] = dot(ohs[...], ones)
    key_ids = iota((LANE, LANE), 0).astype(F32)
    lane_row = iota((1, LANE), 1)

    def key_of(hot, rank, offset):
        found = jnp.sum(hot * (rank + 1.0), axis=0, keepdims=True)
        place = jnp.where(found > 0.5, found - 1.0 + offset, -1.0)
        return jnp.where(key_ids == place, 1.0, 0.0).astype(BF16)

    def value_of(hot, rows, pos):
        high = (rows >> 8).astype(F32)
        low = (rows & 255).astype(F32)
        pieces = [hot * high, hot * low, hot * pos.astype(F32), hot]
        return jnp.concatenate(pieces, axis=0).astype(BF16)

    neg_offset = (lax.rem(me_s, 2) * NEG).astype(F32)

    def place(m, before):
        rows = pl.ds(pl.multiple_of(m * S, S), S)
        lanes = pl.ds(pl.multiple_of(m * LANE, LANE), LANE)
        hot = ohs[rows, :].astype(F32)
        keys[:, lanes] = key_of(hot, inner[rows, :] + before, neg_offset)
        vals[:, lanes] = value_of(hot, nrow[pl.ds(m, 1), :], 2 * m + (lane_row >> 6))
        return before + total[rows, :]

    lax.fori_loop(0, 64, place, jnp.zeros((S, LANE), F32))

    def packed(found):
        high, low, pos, filled = (found[i * S : (i + 1) * S].astype(I32) for i in range(4))
        return jnp.where(filled > 0, (high * 256 + low) * LANE + pos, -1)

    neg_table = packed(dot(vals[...], keys[...], 1, 1))
    hot = own_onehot(town[...])
    rank = dot(hot.astype(BF16), upper)
    tgt_table = packed(
        dot(
            value_of(hot, trow[...], lane_row),
            key_of(hot, rank, (2 * me_s).astype(F32)),
            1,
            1,
        )
    )
    req_msg[...] = jnp.full(req_msg.shape, -1, I32)
    req_msg[:, 0, :] = neg_table
    req_msg[:, 1, :] = tgt_table
    start_seq(X_REQ, lambda p: req_msg.at[p], req_all)
    req_all[me_s] = req_msg[me_s]

    def turn(i, carry):
        span = pl.ds(pl.multiple_of(i * 256, 256), 256)
        cat_t[0:FULL, span] = cat[span, :].T
        return carry

    lax.fori_loop(0, ITEMS // 256, turn, 0)
    cat_t[FULL : FULL + 16, :] = jnp.broadcast_to(cnt[...].astype(F32), (16, ITEMS)).astype(BF16)

    wait_seq(X_CONV, lambda p: msg1.at[p], rcv1)
    rf[...] = rcv1[...].astype(F32)
    xpad[0:16, :] = jnp.zeros((16, LANE), F32)
    later = iota((LANE, LANE), 1) >= iota((LANE, LANE), 0)
    msgf[...] = jnp.zeros_like(msgf)

    for k in range(3):
        xpad[16:272, :] = rf[:, k * 8 : (k + 1) * 8, :].reshape(256, LANE)
        x4[...] = jnp.concatenate(
            [xpad[16 - 4 * j : 272 - 4 * j, :] for j in range(4)], axis=1
        ).astype(BF16)
        acc[...] = jnp.zeros_like(acc)
        prev = jnp.zeros((LANE, LANE), F32)
        for e in range(16):
            tiles = []
            for j in range(4):
                d = 4 * e + j
                row = 24 + 2 * k + d % 2
                chunk = jnp.broadcast_to(rf[d // 2, row : row + 1, :], (LANE, LANE))
                turned = pltpu.roll(chunk, 0, 1, stride=1, stride_axis=0)
                tiles.append(jnp.where(later, turned, prev).astype(BF16))
                prev = turned
            taps_tile = jnp.concatenate(tiles, axis=0)
            acc[16 * e :, :] += dot(x4[0 : 256 - 16 * e, :], taps_tile)
        for s in range(S):
            msgf[s * 32 + k * 8 : s * 32 + k * 8 + 8, :] = acc[s * 8 : s * 8 + 8, :]
    msg2[...] = msgf[...].reshape(S, 32, LANE).astype(BF16)
    start_seq(X_BACK, lambda p: msg2.at[p], rcv2)
    rcv2[me_s] = msg2[me_s]

    wait_seq(X_REQ, lambda p: req_msg.at[p], req_all)
    asked = req_all[...]
    asked_neg = asked[:, 0, :].reshape(GROUPS, 2, LANE)
    lane16 = iota((GROUPS, LANE), 1)
    tab_own[...] = jnp.full(tab_own.shape, -1, I32)
    tab_own[0:GROUPS, :] = jnp.where(lane16 < NEG, asked_neg[:, 0, :], asked_neg[:, 1, :])
    tab_own[GROUPS : GROUPS + 1, :] = jnp.max(asked[:, 1, :], axis=0, keepdims=True)
    start_ch(X_TABLE, lambda p: tab_own, tab_all)
    tab_all[me_c] = tab_own[...]
    row_scale[...] = jnp.zeros_like(row_scale)
    row_log[...] = jnp.zeros_like(row_log)
    item_ids = iota((ITEMS, LANE), 0)

    def picked(group):
        return onehot(item_ids == (tab_own[pl.ds(group, 1), :] >> 7))

    def keep(found, lane0, width, group0):
        for c in range(C):
            rows_send[c, :, pl.ds(lane0, width)] = found[c * CH : (c + 1) * CH].astype(BF16)
        square = jnp.sum(found[0:FULL] * found[0:FULL], axis=0, keepdims=True)
        scale = lax.rsqrt(square / FULL + EPSILON) / (FULL * SOFTMAX_TEMP)
        logs = jnp.log(jnp.maximum(found[FULL : FULL + 1], 1.0))
        for i in range(width // LANE):
            row_scale[pl.ds(group0 + i, 1), :] = scale[:, i * LANE : (i + 1) * LANE]
            row_log[pl.ds(group0 + i, 1), :] = logs[:, i * LANE : (i + 1) * LANE]

    def fetch(h, carry):
        hot = jnp.concatenate([picked(2 * h), picked(2 * h + 1)], axis=1)
        keep(dot(cat_t[...], hot), pl.multiple_of(h * 256, 256), 256, 2 * h)
        return carry

    lax.fori_loop(0, GROUPS // 2, fetch, 0)
    keep(dot(cat_t[...], picked(GROUPS)), GROUPS * LANE, LANE, GROUPS)
    start_ch(X_ROWS, lambda p: rows_send.at[p], rows_all)
    rows_all[me_c] = rows_send[me_c]

    wait_ch(X_SIG, lambda p: sig_send.at[p], sig_all)
    wait_ch(X_WGATE, lambda p: wg_own, wg_all)
    gate_t[...] = dot(wg_all[...].reshape(FULL, FULL), sig_all[...].reshape(FULL, LANE))
    wait_ch(X_WOUT, lambda p: w_out, wo_all)
    wo_t[...] = wo_all[...].reshape(FULL, FULL).T

    wait_seq(X_BACK, lambda p: msg2.at[p], rcv2)
    rf[...] = rcv2[...].astype(F32)
    msgf[...] = rf[...].reshape(S * 32, LANE)
    diag = iota((CH, CH), 0) == iota((CH, CH), 1)
    gain_col = jnp.sum(jnp.where(diag, gain[...], 0.0), axis=1, keepdims=True)
    for q in range(8):
        conv = jnp.concatenate(
            [msgf[pl.ds(k * 8 + q, S, stride=32), :] for k in range(3)], axis=0
        )
        mix_send[q] = (conv + gain_col * sig_send[q].astype(F32)).astype(BF16)
    start_ch(X_MIX, lambda p: mix_send.at[p], mix_all)
    mix_all[me_c] = mix_send[me_c]
    wait_ch(X_MIX, lambda p: mix_send.at[p], mix_all)
    mix = mix_all[...].reshape(FULL, LANE).astype(F32) * gate_t[...]
    lo_send[...] = dot(wo_t[...], mix.astype(BF16)).astype(BF16).reshape(C, CH, LANE)
    start_ch(X_OUT, lambda p: lo_send.at[p], lo_all)
    lo_all[me_c] = lo_send[me_c]

    tok_pos = spos[...]
    pos_in = tok_pos >> 2
    where_in = ((pos_in >> 7) * 4 + (tok_pos & 3)) * LANE + (pos_in & 127)
    pick = onehot(iota((TOK, LANE), 0) == where_in)

    wait_ch(X_OUT, lambda p: lo_send.at[p], lo_all)
    lo_t = jnp.concatenate([lo_all[q] for q in range(8)], axis=1)
    q_own[...] = dot(lo_t, pick).astype(BF16)
    start_seq(X_QUERY, lambda p: q_own, q_all)
    q_all[me_s] = q_own[...]
    out_ref[...] = dot(perm[...], lo_t, 1, 1).astype(BF16)

    wait_ch(X_TABLE, lambda p: tab_own, tab_all)
    pair_ids = iota((2 * LANE, LANE), 0)
    block_ids = iota((LANE, LANE), 0)

    def slots(g, carry):
        for c in range(C):
            entry = tab_all[c, pl.ds(g, 1), :]
            target = jnp.where(entry < 0, -1, (entry & 127) + jnp.where(lane_row < NEG, 0, LANE))
            ohp[g, :, c * LANE : (c + 1) * LANE] = onehot(pair_ids == target)
        return carry

    lax.fori_loop(0, GROUPS, slots, 0)

    def target_slots(b, carry):
        rows = pl.ds(pl.multiple_of(b * LANE, LANE), LANE)
        for c in range(C):
            entry = tab_all[c, GROUPS : GROUPS + 1, :]
            ours = (entry >= 0) & ((lane_row >> 1) == b)
            target = jnp.where(ours, entry & 127, -1)
            oht[rows, c * LANE : (c + 1) * LANE] = onehot(block_ids == target)
        return carry

    lax.fori_loop(0, S, target_slots, 0)

    wait_ch(X_ROWS, lambda p: rows_send.at[p], rows_all)
    wait_seq(X_QUERY, lambda p: q_own, q_all)
    part[...] = jnp.zeros_like(part)

    def score(query, lane0, group):
        for c in range(C):
            one = query[:, c * LANE : (c + 1) * LANE]
            rows = rows_all[c, :, pl.ds(lane0, LANE)].astype(F32)
            part[c, pl.ds(group, 1), :] = jnp.sum(one * rows, axis=0, keepdims=True)
            part[c, pl.ds(24 + group, 1), :] = jnp.sum(one * one, axis=0, keepdims=True)

    def pair(g, carry):
        both = jnp.concatenate([q_all[2 * g], q_all[2 * g + 1]], axis=1)
        score(dot(both, ohp[g]), pl.multiple_of(g * LANE, LANE), g)
        return carry

    lax.fori_loop(0, GROUPS, pair, 0)

    def gather_targets(g, held):
        both = jnp.concatenate([q_all[2 * g], q_all[2 * g + 1]], axis=1)
        return held + dot(both, oht[pl.ds(pl.multiple_of(g * 256, 256), 256), :])

    score(
        lax.fori_loop(0, S // 2, gather_targets, jnp.zeros((CH, C * LANE), F32)),
        GROUPS * LANE,
        GROUPS,
    )
    start_ch(X_PART, lambda p: part.at[p], part_all)
    part_all[me_c] = part[me_c]
    wait_ch(X_PART, lambda p: part.at[p], part_all)
    whole = jnp.sum(part_all[...], axis=0)
    query_scale = lax.rsqrt(whole[24:48] / FULL + EPSILON)
    logit = whole[0:24] * query_scale * row_scale[...] - row_log[...]
    filled = tab_own[...] >= 0
    exp_parts = jnp.concatenate(
        split_parts(jnp.where(filled, jnp.exp(logit), 0.0)[0:GROUPS], 2), axis=0
    )
    tgt_parts = jnp.concatenate(
        split_parts(
            jnp.broadcast_to(jnp.where(filled, logit, 0.0)[GROUPS : GROUPS + 1], (16, LANE)), 3
        ),
        axis=0,
    )
    sums[...] = jnp.zeros_like(sums)
    own_lanes = pl.ds(pl.multiple_of(me_c * LANE, LANE), LANE)
    row32 = iota((2 * GROUPS, 1), 0)

    def totals(g, carry):
        found = dot(exp_parts, ohp[g, :, own_lanes], 1, 1)
        both = jnp.sum(jnp.where((row32 & 15) == g, found, 0.0), axis=0, keepdims=True)
        sums[2 * g, 0:1, :] = both[:, 0:LANE]
        sums[2 * g + 1, 0:1, :] = both[:, LANE:]
        targets = dot(
            tgt_parts, oht[pl.ds(pl.multiple_of(g * 256, 256), 256), own_lanes], 1, 1
        )
        joined = targets[0:1] + targets[16:17] + targets[32:33]
        sums[2 * g, 1:2, :] = joined[:, 0:LANE]
        sums[2 * g + 1, 1:2, :] = joined[:, LANE:]
        return carry

    lax.fori_loop(0, GROUPS, totals, 0)
    start_seq(X_SUMS, lambda p: sums.at[p], sums_all)
    sums_all[me_s] = sums[me_s]
    wait_seq(X_SUMS, lambda p: sums.at[p], sums_all)
    fin[...] = jnp.sum(sums_all[...], axis=0)
    start_ch(X_FIN, lambda p: fin, fin_all)
    fin_all[me_c] = fin[...]
    wait_ch(X_FIN, lambda p: fin, fin_all)
    last = jnp.sum(fin_all[...], axis=0)
    target_logit = last[1:2]
    loss_ref[...] = jnp.log(jnp.exp(target_logit) + last[0:1]) - target_logit

    sent_seq(X_CONV, lambda p: msg1.at[p], rcv1)
    sent_seq(X_REQ, lambda p: req_msg.at[p], req_all)
    sent_seq(X_BACK, lambda p: msg2.at[p], rcv2)
    sent_seq(X_QUERY, lambda p: q_own, q_all)
    sent_seq(X_SUMS, lambda p: sums.at[p], sums_all)
    sent_ch(X_SIG, lambda p: sig_send.at[p], sig_all)
    sent_ch(X_WGATE, lambda p: wg_own, wg_all)
    sent_ch(X_WOUT, lambda p: w_out, wo_all)
    sent_ch(X_TABLE, lambda p: tab_own, tab_all)
    sent_ch(X_ROWS, lambda p: rows_send.at[p], rows_all)
    sent_ch(X_MIX, lambda p: mix_send.at[p], mix_all)
    sent_ch(X_OUT, lambda p: lo_send.at[p], lo_all)
    sent_ch(X_PART, lambda p: part.at[p], part_all)
    sent_ch(X_FIN, lambda p: fin, fin_all)


def per_device(
    signal,
    filter_taps,
    skip_gain,
    w_gate,
    w_out,
    catalogue,
    item_draw_counts,
    sampled_pos,
    neg_owner,
    neg_row,
    target_owner,
    target_row,
):
    vmem = pl.BlockSpec(memory_space=pltpu.VMEM)
    scratch = [
        ((TOK, TOK), BF16),
        ((C, CH, LANE), BF16),
        ((C, CH, LANE), BF16),
        ((S * 32, LANE), F32),
        ((S, 32, LANE), BF16),
        ((S, 32, LANE), BF16),
        ((S, 32, LANE), F32),
        ((272, LANE), F32),
        ((256, 512), BF16),
        ((256, LANE), F32),
        ((S, 32, LANE), BF16),
        ((S, 32, LANE), BF16),
        ((CH, FULL), BF16),
        ((C, CH, FULL), BF16),
        ((C, CH, FULL), BF16),
        ((FULL, FULL), BF16),
        ((FULL, LANE), F32),
        ((C, CH, LANE), BF16),
        ((C, CH, LANE), BF16),
        ((C, CH, LANE), BF16),
        ((C, CH, LANE), BF16),
        ((CH, LANE), BF16),
        ((S, CH, LANE), BF16),
        ((S, 8, LANE), I32),
        ((S, 8, LANE), I32),
        ((64 * S, LANE), BF16),
        ((64 * S, LANE), F32),
        ((64 * S, LANE), F32),
        ((LANE, 64 * LANE), BF16),
        ((LANE, 64 * LANE), BF16),
        ((24, LANE), I32),
        ((C, 24, LANE), I32),
        ((FULL + 16, ITEMS), BF16),
        ((C, CH, SLOTS), BF16),
        ((C, CH, SLOTS), BF16),
        ((24, LANE), F32),
        ((24, LANE), F32),
        ((GROUPS, 2 * LANE, C * LANE), BF16),
        ((S * LANE, C * LANE), BF16),
        ((C, 48, LANE), F32),
        ((C, 48, LANE), F32),
        ((S, 8, LANE), F32),
        ((S, 8, LANE), F32),
        ((8, LANE), F32),
        ((C, 8, LANE), F32),
    ]
    layer_out, loss = pl.pallas_call(
        body,
        out_shape=(
            jax.ShapeDtypeStruct((TOK, CH), BF16),
            jax.ShapeDtypeStruct((1, LANE), F32),
        ),
        in_specs=[vmem] * 12,
        out_specs=(vmem, vmem),
        scratch_shapes=[pltpu.VMEM(shape, kind) for shape, kind in scratch]
        + [pltpu.SemaphoreType.DMA((14, S)), pltpu.SemaphoreType.DMA((14, S))],
        compiler_params=pltpu.CompilerParams(
            collective_id=0, has_side_effects=True, vmem_limit_bytes=60 * 1024 * 1024
        ),
        cost_estimate=pl.CostEstimate(
            flops=20_000_000_000, bytes_accessed=5_000_000, transcendentals=10_000
        ),
    )(
        signal.reshape(TOK, CH),
        filter_taps,
        skip_gain.reshape(1, CH),
        w_gate,
        w_out,
        catalogue,
        item_draw_counts.reshape(1, ITEMS),
        sampled_pos.reshape(1, LANE),
        neg_owner.reshape(64, LANE),
        neg_row.reshape(64, LANE),
        target_owner.reshape(1, LANE),
        target_row.reshape(1, LANE),
    )
    return layer_out.reshape(256, 4, CH), loss.reshape(LANE)


def solution(mesh):
    placed = (
        P("seq", None, "ch"),
        P("seq", "ch"),
        P("ch"),
        P(None, "ch"),
        P("ch", None),
        P(("seq", "ch"), None),
        P(("seq", "ch")),
        P("seq"),
        P("seq", None, None),
        P("seq", None),
        P("seq", None),
        P("seq"),
    )
    return jax.shard_map(
        per_device,
        mesh=mesh,
        in_specs=placed,
        out_specs=(P("seq", None, "ch"), P("seq")),
        check_vma=False,
    )
```

```python
import jax
import jax.numpy as jnp
from jax import lax
from jax.experimental import pallas as pl
from jax.experimental.pallas import tpu as pltpu
from jax.sharding import PartitionSpec as P

SOFTMAX_TEMP = 0.02
EPSILON = 1e-06
MESH = pl.DeviceIdType.MESH
BF16 = jnp.bfloat16
F32 = jnp.float32
I32 = jnp.int32

S = 32
C = 8
LANE = 128
CH = 96
FULL = CH * C
TOK = 1024
NEG = 64
GROUPS = 16
SLOTS = (GROUPS + 1) * LANE
ITEMS = 2048

(
    X_CONV,
    X_BACK,
    X_QUERY,
    X_FORWARD,
    X_SUMS,
    X_SIG,
    X_WGATE,
    X_WOUT,
    X_WGATE_MATE,
    X_WOUT_MATE,
    X_TABLE,
    X_MIX,
    X_OUT,
    X_PART,
    X_FIN,
    X_ROWS,
) = range(16)
CHUNKS = GROUPS // 2 + 1
EXCHANGES = X_ROWS + CHUNKS
SIDE = 4
TGT_LANES = (0, 16, 64, 80)
TGT_BLOCKS = tuple(tuple(range(first, first + 16, 2)) for first in (1, 17, 0, 16))


def iota(shape, dim):
    return lax.broadcasted_iota(I32, shape, dim)


def onehot(mask):
    return jnp.where(mask, 1.0, 0.0).astype(BF16)


def dot(a, b, ca=1, cb=0):
    return lax.dot_general(a, b, (((ca,), (cb,)), ((), ())), preferred_element_type=F32)


def split_parts(value, count):
    parts = []
    for _ in range(count):
        piece = value.astype(BF16)
        parts.append(piece)
        value = value - piece.astype(F32)
    return parts


def body(
    sig,
    taps_t,
    gain,
    wg_own,
    w_out,
    cat_hbm,
    cnt,
    spos,
    nown,
    nrow,
    town,
    trow,
    out_ref,
    loss_ref,
    cat,
    sig_send,
    sig_all,
    msgf,
    msg1,
    rcv1,
    rf,
    xpad,
    x4,
    acc,
    msg2,
    rcv2,
    wg_all,
    wo_all,
    wo_t,
    gate_t,
    mix_send,
    mix_all,
    lo_send,
    lo_all,
    q_own,
    q_all,
    ohs,
    inner,
    total,
    keys,
    vals,
    tab_own,
    tab_all,
    tab_t,
    cat_t,
    rows_send,
    rows_all,
    row_scale,
    row_log,
    ohp,
    oht,
    slot_pos,
    part,
    part_all,
    sums,
    sums_all,
    fin,
    fin_all,
    send_sem,
    recv_sem,
    cat_sem,
):
    me_s = lax.axis_index("seq")
    me_c = lax.axis_index("ch")

    def seq_copy(x, peer, src, dst):
        return pltpu.make_async_remote_copy(
            src_ref=src,
            dst_ref=dst,
            send_sem=send_sem.at[x, peer],
            recv_sem=recv_sem.at[x, me_s],
            device_id=(peer, me_c),
            device_id_type=MESH,
        )

    def ch_copy(x, peer, src, dst):
        return pltpu.make_async_remote_copy(
            src_ref=src,
            dst_ref=dst,
            send_sem=send_sem.at[x, peer],
            recv_sem=recv_sem.at[x, me_c],
            device_id=(me_s, peer),
            device_id_type=MESH,
        )

    def over(n, me, fn):
        def step(d, carry):
            fn(lax.rem(me + d, n))
            return carry

        lax.fori_loop(1, n, step, 0)

    def start_seq(x, src_of, dst):
        over(S, me_s, lambda peer: seq_copy(x, peer, src_of(peer), dst.at[me_s]).start())

    def start_ch(x, src_of, dst):
        over(C, me_c, lambda peer: ch_copy(x, peer, src_of(peer), dst.at[me_c]).start())

    def wait_from(x, peer, src, dst, device):
        pltpu.make_async_remote_copy(
            src_ref=src,
            dst_ref=dst,
            send_sem=send_sem.at[x, peer],
            recv_sem=recv_sem.at[x, peer],
            device_id=device,
            device_id_type=MESH,
        ).wait_recv()

    def wait_seq(x, src_of, dst):
        over(S, me_s, lambda peer: wait_from(x, peer, src_of(peer), dst.at[peer], (peer, me_c)))

    def wait_ch(x, src_of, dst):
        over(C, me_c, lambda peer: wait_from(x, peer, src_of(peer), dst.at[peer], (me_s, peer)))

    def sent_seq(x, src_of, dst):
        over(S, me_s, lambda peer: seq_copy(x, peer, src_of(peer), dst.at[me_s]).wait_send())

    def sent_ch(x, src_of, dst):
        over(C, me_c, lambda peer: ch_copy(x, peer, src_of(peer), dst.at[me_c]).wait_send())

    barrier = pltpu.get_barrier_semaphore()

    def greet_seq(peer):
        pl.semaphore_signal(barrier, inc=1, device_id=(peer, me_c), device_id_type=MESH)

    def greet_ch(peer):
        pl.semaphore_signal(barrier, inc=1, device_id=(me_s, peer), device_id_type=MESH)

    over(S, me_s, greet_seq)
    over(C, me_c, greet_ch)

    cat_copy = pltpu.make_async_copy(cat_hbm, cat, cat_sem)
    cat_copy.start()

    upper = onehot(iota((LANE, LANE), 0) < iota((LANE, LANE), 1))
    ones = jnp.ones((LANE, LANE), BF16)
    owner_ids = iota((S, LANE), 0)

    def own_onehot(owners):
        mine = jnp.where((owners & 7) == me_c, owners >> 3, -1)
        return jnp.where(owner_ids == mine, 1.0, 0.0)

    def mark(m, carry):
        ohs[pl.ds(pl.multiple_of(m * S, S), S), :] = own_onehot(nown[m]).astype(BF16)
        return carry

    lax.fori_loop(0, 64, mark, 0, unroll=4)
    inner[...] = dot(ohs[...], upper)
    total[...] = dot(ohs[...], ones)
    key_ids = iota((LANE, LANE), 0).astype(F32)
    lane_row = iota((1, LANE), 1)

    def key_of(hot, rank, offset):
        found = jnp.sum(hot * (rank + 1.0), axis=0, keepdims=True)
        place = jnp.where(found > 0.5, found - 1.0 + offset, -1.0)
        return jnp.where(key_ids == place, 1.0, 0.0).astype(BF16)

    def value_of(hot, rows):
        high = (rows >> 8).astype(F32)
        low = (rows & 255).astype(F32)
        pieces = [hot * high, hot * low, hot * lane_row.astype(F32), hot]
        return jnp.concatenate(pieces, axis=0).astype(BF16)

    odd = lax.rem(me_s, 2)
    neg_offset = (odd * NEG).astype(F32)
    tgt_offset = ((1 - odd) * NEG + me_s - odd).astype(F32)

    def place(m, before):
        rows = pl.ds(pl.multiple_of(m * S, S), S)
        lanes = pl.ds(pl.multiple_of(m * LANE, LANE), LANE)
        hot = ohs[rows, :].astype(F32)
        keys[:, lanes] = key_of(hot, inner[rows, :] + before, neg_offset)
        vals[:, lanes] = value_of(hot, nrow[pl.ds(m, 1), :])
        return before + total[rows, :]

    lax.fori_loop(0, 64, place, jnp.zeros((S, LANE), F32), unroll=4)
    hot = own_onehot(town[...])
    rank = dot(hot.astype(BF16), upper)
    found = dot(vals[...], keys[...], 1, 1) + dot(
        value_of(hot, trow[...]), key_of(hot, rank, tgt_offset), 1, 1
    )
    high, low, pos, filled = (found[i * S : (i + 1) * S].astype(I32) for i in range(4))
    entry = (high * 256 + low) * LANE + pos
    entry_high = jnp.where(filled > 0, (entry >> 9) - 256, 1024).astype(F32)
    entry_low = jnp.where(filled > 0, (entry & 511) - 256, 0).astype(F32)

    for q in range(8):
        piece = sig[q % 4, :, (q // 4) * LANE : (q // 4 + 1) * LANE]
        sig_send[q] = piece
        for k in range(3):
            msgf[pl.ds(k * 8 + q, S, stride=32), :] = piece[k * 32 : (k + 1) * 32].astype(F32)
    for il in range(2):
        for k in range(3):
            msgf[pl.ds(24 + 2 * k + il, S, stride=32), :] = taps_t[
                k * 32 : (k + 1) * 32, il * LANE : (il + 1) * LANE
            ]
    msgf[pl.ds(30, S, stride=32), :] = entry_high
    msgf[pl.ds(31, S, stride=32), :] = entry_low
    msg1[...] = msgf[...].reshape(S, 32, LANE).astype(BF16)

    pl.semaphore_wait(barrier, S - 1 + C - 1)

    start_seq(X_CONV, lambda p: msg1.at[p], rcv1)
    rcv1[me_s] = msg1[me_s]
    start_ch(X_SIG, lambda p: sig_send.at[p], sig_all)
    sig_all[me_c] = sig_send[me_c]

    core = lax.rem(me_c, 2)
    mate = me_c + 1 - 2 * core

    def over_x(fn):
        def step(d, carry):
            fn(lax.rem(me_c + 2 * d, C))
            return carry

        lax.fori_loop(1, SIDE, step, 0)

    def start_weight(x, src, dst):
        over_x(lambda peer: ch_copy(x, peer, src, dst.at[me_c]).start())
        ch_copy(x, mate, src, dst.at[me_c]).start()
        dst[me_c] = src[...]

    def mate_copy(x, x_mate, peer, dst):
        return pltpu.make_async_remote_copy(
            src_ref=dst.at[peer],
            dst_ref=dst.at[peer],
            send_sem=send_sem.at[x_mate, peer],
            recv_sem=recv_sem.at[x, peer],
            device_id=(me_s, mate),
            device_id_type=MESH,
        )

    def pass_weight(x, x_mate, src, dst):
        def fn(peer):
            wait_from(x, peer, src, dst.at[peer], (me_s, peer))
            mate_copy(x, x_mate, peer, dst).start()

        over_x(fn)

    def wait_weight(x, src, dst):
        wait_from(x, mate, src, dst.at[mate], (me_s, mate))

        def fn(peer):
            other = peer + 1 - 2 * core
            wait_from(x, other, src, dst.at[other], (me_s, mate))

        over_x(fn)

    def sent_weight(x, x_mate, src, dst):
        over_x(lambda peer: ch_copy(x, peer, src, dst.at[me_c]).wait_send())
        ch_copy(x, mate, src, dst.at[me_c]).wait_send()
        over_x(lambda peer: mate_copy(x, x_mate, peer, dst).wait_send())

    start_weight(X_WGATE, wg_own, wg_all)
    start_weight(X_WOUT, w_out, wo_all)

    cat_copy.wait()

    def turn(i, carry):
        span = pl.ds(pl.multiple_of(i * 256, 256), 256)
        cat_t[0:FULL, span] = cat[span, :].T
        return carry

    lax.fori_loop(0, ITEMS // 256, turn, 0)
    cat_t[FULL : FULL + 16, :] = jnp.broadcast_to(cnt[...].astype(F32), (16, ITEMS)).astype(BF16)

    wait_seq(X_CONV, lambda p: msg1.at[p], rcv1)
    rf[...] = rcv1[...].astype(F32)
    xpad[0:16, :] = jnp.zeros((16, LANE), F32)
    later = iota((LANE, LANE), 1) >= iota((LANE, LANE), 0)
    for k in range(3):
        xpad[16:272, :] = rf[:, k * 8 : (k + 1) * 8, :].reshape(256, LANE)
        x4[...] = jnp.concatenate(
            [xpad[16 - 4 * j : 272 - 4 * j, :] for j in range(4)], axis=1
        ).astype(BF16)
        acc[...] = jnp.zeros_like(acc)
        prev = jnp.zeros((LANE, LANE), F32)
        for e in range(16):
            tiles = []
            for j in range(4):
                d = 4 * e + j
                row = 24 + 2 * k + d % 2
                chunk = jnp.broadcast_to(rf[d // 2, row : row + 1, :], (LANE, LANE))
                turned = pltpu.roll(chunk, 0, 1, stride=1, stride_axis=0)
                tiles.append(jnp.where(later, turned, prev).astype(BF16))
                prev = turned
            taps_tile = jnp.concatenate(tiles, axis=0)
            acc[16 * e :, :] += dot(x4[0 : 256 - 16 * e, :], taps_tile)
        for s in range(S):
            msgf[s * 32 + k * 8 : s * 32 + k * 8 + 8, :] = acc[s * 8 : s * 8 + 8, :]
    msg2[...] = msgf[...].reshape(S, 32, LANE).astype(BF16)
    start_seq(X_BACK, lambda p: msg2.at[p], rcv2)
    rcv2[me_s] = msg2[me_s]

    asked_high = rf[:, 30, :].astype(I32)
    asked_low = rf[:, 31, :].astype(I32)
    asked = jnp.where(asked_high < 512, (asked_high + 256) * 512 + asked_low + 256, -1)
    asked = asked.reshape(GROUPS, 2, LANE)
    even_half, odd_half = asked[:, 0, :], asked[:, 1, :]
    first_half = iota((GROUPS, LANE), 1) < NEG
    tab_own[...] = jnp.full(tab_own.shape, -1, I32)
    tab_own[0:GROUPS, :] = jnp.where(first_half, even_half, odd_half)
    tab_own[GROUPS : GROUPS + 1, :] = jnp.max(
        jnp.where(first_half, odd_half, even_half), axis=0, keepdims=True
    )
    start_ch(X_TABLE, lambda p: tab_own, tab_all)
    tab_all[me_c] = tab_own[...]
    row_scale[...] = jnp.zeros_like(row_scale)
    row_log[...] = jnp.zeros_like(row_log)
    item_ids = iota((ITEMS, LANE), 0)

    def picked(group):
        return onehot(item_ids == (tab_own[pl.ds(group, 1), :] >> 7))

    def keep(found, width, group0):
        for i in range(width // LANE):
            lanes = slice(i * LANE, (i + 1) * LANE)
            for c in range(C):
                rows_send[group0 + i, c] = found[c * CH : (c + 1) * CH, lanes].astype(BF16)
            rows_all[group0 + i, me_c] = rows_send[group0 + i, me_c]
        square = jnp.sum(found[0:FULL] * found[0:FULL], axis=0, keepdims=True)
        scale = lax.rsqrt(square / FULL + EPSILON) / (FULL * SOFTMAX_TEMP)
        logs = jnp.log(jnp.maximum(found[FULL : FULL + 1], 1.0))
        for i in range(width // LANE):
            row_scale[pl.ds(group0 + i, 1), :] = scale[:, i * LANE : (i + 1) * LANE]
            row_log[pl.ds(group0 + i, 1), :] = logs[:, i * LANE : (i + 1) * LANE]

    def chunk_copy(h, peer):
        span = pl.ds(2 * h, 2)
        return ch_copy(X_ROWS + h, peer, rows_send.at[span, peer], rows_all.at[span, me_c])

    def target_copy(peer):
        x = X_ROWS + CHUNKS - 1
        return ch_copy(x, peer, rows_send.at[GROUPS, peer], rows_all.at[GROUPS, me_c])

    def fetch(first, last):
        def step(h, carry):
            hot = jnp.concatenate([picked(2 * h), picked(2 * h + 1)], axis=1)
            keep(dot(cat_t[...], hot), 256, 2 * h)
            over(C, me_c, lambda peer: chunk_copy(h, peer).start())
            return carry

        lax.fori_loop(first, last, step, 0)

    def fetch_targets():
        keep(dot(cat_t[...], picked(GROUPS)), LANE, GROUPS)
        over(C, me_c, lambda peer: target_copy(peer).start())

    def wait_rows():
        def step(h, carry):
            span = pl.ds(2 * h, 2)

            def fn(peer):
                src, dst = rows_send.at[span, peer], rows_all.at[span, peer]
                wait_from(X_ROWS + h, peer, src, dst, (me_s, peer))

            over(C, me_c, fn)
            return carry

        lax.fori_loop(0, CHUNKS - 1, step, 0)

        def last(peer):
            src, dst = rows_send.at[GROUPS, peer], rows_all.at[GROUPS, peer]
            wait_from(X_ROWS + CHUNKS - 1, peer, src, dst, (me_s, peer))

        over(C, me_c, last)

    def sent_rows():
        def step(h, carry):
            over(C, me_c, lambda peer: chunk_copy(h, peer).wait_send())
            return carry

        lax.fori_loop(0, CHUNKS - 1, step, 0)
        over(C, me_c, lambda peer: target_copy(peer).wait_send())

    fetch(0, 4)
    pass_weight(X_WGATE, X_WGATE_MATE, wg_own, wg_all)
    wait_ch(X_SIG, lambda p: sig_send.at[p], sig_all)

    wait_seq(X_BACK, lambda p: msg2.at[p], rcv2)
    rf[...] = rcv2[...].astype(F32)
    msgf[...] = rf[...].reshape(S * 32, LANE)
    diag = iota((CH, CH), 0) == iota((CH, CH), 1)
    gain_col = jnp.sum(jnp.where(diag, gain[...], 0.0), axis=1, keepdims=True)
    for q in range(8):
        conv = jnp.concatenate(
            [msgf[pl.ds(k * 8 + q, S, stride=32), :] for k in range(3)], axis=0
        )
        mix_send[q] = (conv + gain_col * sig_send[q].astype(F32)).astype(BF16)
    start_ch(X_MIX, lambda p: mix_send.at[p], mix_all)
    mix_all[me_c] = mix_send[me_c]
    pass_weight(X_WOUT, X_WOUT_MATE, w_out, wo_all)

    wait_weight(X_WGATE, wg_own, wg_all)
    gate_t[...] = dot(wg_all[...].reshape(FULL, FULL), sig_all[...].reshape(FULL, LANE))
    fetch(4, 6)
    wait_weight(X_WOUT, w_out, wo_all)
    wo_t[...] = wo_all[...].reshape(FULL, FULL).T
    wait_ch(X_MIX, lambda p: mix_send.at[p], mix_all)
    mix = mix_all[...].reshape(FULL, LANE).astype(F32) * gate_t[...]
    lo_send[...] = dot(wo_t[...], mix.astype(BF16)).astype(BF16).reshape(C, CH, LANE)
    start_ch(X_OUT, lambda p: lo_send.at[p], lo_all)
    lo_all[me_c] = lo_send[me_c]

    fetch(6, 8)
    tok_pos = spos[...]
    pos_in = tok_pos >> 2
    where_in = ((pos_in >> 7) * 4 + (tok_pos & 3)) * LANE + (pos_in & 127)
    pick = onehot(iota((TOK, LANE), 0) == where_in)

    wait_ch(X_OUT, lambda p: lo_send.at[p], lo_all)
    lo_t = jnp.concatenate([lo_all[q] for q in range(8)], axis=1)
    q_own[...] = dot(lo_t, pick).astype(BF16)

    me_z, me_y = me_s // SIDE, lax.rem(me_s, SIDE)
    layers = S // SIDE

    def block_to(x, slot, peer, src, block):
        return pltpu.make_async_remote_copy(
            src_ref=src,
            dst_ref=q_all.at[block],
            send_sem=send_sem.at[x, slot],
            recv_sem=recv_sem.at[X_QUERY, block],
            device_id=(peer, me_c),
            device_id_type=MESH,
        )

    def along_z(fn):
        def step(d, carry):
            fn(lax.rem(me_z + d, layers) * SIDE + me_y)
            return carry

        lax.fori_loop(1, layers, step, 0)

    def along_y(block, src, fn):
        def step(d, carry):
            peer = me_z * SIDE + lax.rem(me_y + d, SIDE)
            fn(block_to(X_FORWARD, d * layers + block // SIDE, peer, src, block))
            return carry

        lax.fori_loop(1, SIDE, step, 0)

    def take_block(block):
        wait_from(X_QUERY, block, q_own, q_all.at[block], (block, me_c))

    along_z(lambda peer: block_to(X_QUERY, peer, peer, q_own, me_s).start())
    along_y(me_s, q_own, lambda copy: copy.start())
    q_all[me_s] = q_own[...]
    for q in range(8):
        out_ref[q % 4, :, (q // 4) * LANE : (q // 4 + 1) * LANE] = lo_all[q]

    def go_on(block):
        take_block(block)
        along_y(block, q_all.at[block], lambda copy: copy.start())

    along_z(go_on)
    fetch_targets()

    wait_ch(X_TABLE, lambda p: tab_own, tab_all)
    pair_ids = iota((2 * LANE, LANE), 0)

    def slots(g, carry):
        for c in range(C):
            entry = tab_all[c, pl.ds(g, 1), :]
            target = jnp.where(entry < 0, -1, (entry & 127) + jnp.where(lane_row < NEG, 0, LANE))
            ohp[g, :, c * LANE : (c + 1) * LANE] = onehot(pair_ids == target)
        return carry

    lax.fori_loop(0, GROUPS, slots, 0)
    wide_ids = iota((8 * LANE, LANE), 0)
    part_of = lane_row >> 4
    for o, lane0 in enumerate(TGT_LANES):
        entry = jnp.full((1, LANE), -1, I32)
        for c in range(C):
            turned = pltpu.roll(tab_all[c, GROUPS : GROUPS + 1, :], (16 * c - lane0) % LANE, 1)
            entry = jnp.where(part_of == c, turned, entry)
        target = jnp.where(entry < 0, -1, ((lane_row & 15) >> 1) * LANE + (entry & 127))
        oht[o] = onehot(wide_ids == target)
    tab_t[...] = jnp.full(tab_t.shape, -1.0, F32)
    tab_t[0:24, :] = jnp.where(tab_own[...] < 0, -1, tab_own[...] & 127).astype(F32)
    columns = tab_t[...].T
    pos_ids = iota((LANE, LANE), 1).astype(F32)
    for g in range(GROUPS + 1):
        slot_pos[g] = onehot(columns[:, g : g + 1] == pos_ids)

    wait_rows()
    tgt_rows = []
    for lane0 in TGT_LANES:
        rows = jnp.zeros((CH, LANE), F32)
        for c in range(C):
            turned = pltpu.roll(rows_all[GROUPS, c].astype(F32), (16 * c - lane0) % LANE, 1)
            rows = jnp.where(part_of == c, turned, rows)
        tgt_rows.append(rows)
    part[...] = jnp.zeros_like(part)

    def rest_of_blocks(d, carry):
        y = lax.rem(me_y + d, SIDE)

        def step(z, inside):
            take_block(z * SIDE + y)
            return inside

        lax.fori_loop(0, layers, step, 0)
        return carry

    lax.fori_loop(1, SIDE, rest_of_blocks, 0)

    def pair(g, carry):
        both = jnp.concatenate([q_all[2 * g], q_all[2 * g + 1]], axis=1)
        query = dot(both, ohp[g])
        for c in range(C):
            one = query[:, c * LANE : (c + 1) * LANE]
            rows = rows_all[g, c].astype(F32)
            part[c, pl.ds(g, 1), :] = jnp.sum(one * rows, axis=0, keepdims=True)
            part[c, pl.ds(24 + g, 1), :] = jnp.sum(one * one, axis=0, keepdims=True)
        return carry

    lax.fori_loop(0, GROUPS, pair, 0, unroll=2)
    tgt_part = [[jnp.zeros((1, LANE), F32) for _ in range(2)] for _ in range(C)]
    for o, lane0 in enumerate(TGT_LANES):
        wide = jnp.concatenate([q_all[b] for b in TGT_BLOCKS[o]], axis=1)
        one = dot(wide, oht[o])
        for i, rows in enumerate((tgt_rows[o], one)):
            both = jnp.sum(one * rows, axis=0, keepdims=True)
            for c in range(C):
                turned = pltpu.roll(both, (lane0 - 16 * c) % LANE, 1)
                ours = (lane_row >= lane0) & (lane_row < lane0 + 16)
                tgt_part[c][i] = jnp.where(ours, turned, tgt_part[c][i])
    for c in range(C):
        part[c, GROUPS : GROUPS + 1, :] = tgt_part[c][0]
        part[c, 24 + GROUPS : 25 + GROUPS, :] = tgt_part[c][1]
    start_ch(X_PART, lambda p: part.at[p], part_all)
    part_all[me_c] = part[me_c]
    wait_ch(X_PART, lambda p: part.at[p], part_all)
    whole = jnp.sum(part_all[...], axis=0)
    query_scale = lax.rsqrt(whole[24:48] / FULL + EPSILON)
    logit = whole[0:24] * query_scale * row_scale[...] - row_log[...]
    filled = tab_own[...] >= 0
    exp_neg = jnp.where(filled, jnp.exp(logit), 0.0)[0:GROUPS]
    halves = [jnp.where(first_half, exp_neg, 0.0), jnp.where(first_half, 0.0, exp_neg)]
    exp_parts = jnp.concatenate([p for half in halves for p in split_parts(half, 2)], axis=0)
    tgt_logit = jnp.where(filled, logit, 0.0)[GROUPS : GROUPS + 1]
    block_of = 2 * ((lane_row & 63) >> 1) + jnp.where(lane_row < NEG, 1, 0)
    by_block = jnp.where(iota((S, LANE), 0) == block_of, tgt_logit, 0.0)
    tgt_parts = jnp.concatenate(split_parts(by_block, 3), axis=0)
    targets = dot(tgt_parts, slot_pos[GROUPS])
    targets = targets[0:S] + targets[S : 2 * S] + targets[2 * S : 3 * S]
    sums[...] = jnp.zeros_like(sums)
    sums[:, 1, :] = targets
    for g in range(GROUPS):
        found = dot(exp_parts, slot_pos[g])
        sums[2 * g, 0:1, :] = found[g : g + 1] + found[16 + g : 17 + g]
        sums[2 * g + 1, 0:1, :] = found[32 + g : 33 + g] + found[48 + g : 49 + g]
    start_seq(X_SUMS, lambda p: sums.at[p], sums_all)
    sums_all[me_s] = sums[me_s]
    wait_seq(X_SUMS, lambda p: sums.at[p], sums_all)
    fin[...] = jnp.sum(sums_all[...], axis=0)
    start_ch(X_FIN, lambda p: fin, fin_all)
    fin_all[me_c] = fin[...]
    wait_ch(X_FIN, lambda p: fin, fin_all)
    last = jnp.sum(fin_all[...], axis=0)
    target_logit = last[1:2]
    loss_ref[...] = jnp.log(jnp.exp(target_logit) + last[0:1]) - target_logit

    sent_seq(X_CONV, lambda p: msg1.at[p], rcv1)
    sent_seq(X_BACK, lambda p: msg2.at[p], rcv2)
    along_z(lambda peer: block_to(X_QUERY, peer, peer, q_own, me_s).wait_send())
    along_y(me_s, q_own, lambda copy: copy.wait_send())
    along_z(lambda block: along_y(block, q_all.at[block], lambda copy: copy.wait_send()))
    sent_seq(X_SUMS, lambda p: sums.at[p], sums_all)
    sent_ch(X_SIG, lambda p: sig_send.at[p], sig_all)
    sent_weight(X_WGATE, X_WGATE_MATE, wg_own, wg_all)
    sent_weight(X_WOUT, X_WOUT_MATE, w_out, wo_all)
    sent_ch(X_TABLE, lambda p: tab_own, tab_all)
    sent_rows()
    sent_ch(X_MIX, lambda p: mix_send.at[p], mix_all)
    sent_ch(X_OUT, lambda p: lo_send.at[p], lo_all)
    sent_ch(X_PART, lambda p: part.at[p], part_all)
    sent_ch(X_FIN, lambda p: fin, fin_all)


def per_device(
    signal,
    filter_taps,
    skip_gain,
    w_gate,
    w_out,
    catalogue,
    item_draw_counts,
    sampled_pos,
    neg_owner,
    neg_row,
    target_owner,
    target_row,
):
    vmem = pl.BlockSpec(memory_space=pltpu.VMEM)
    scratch = [
        ((ITEMS, FULL), BF16),
        ((C, CH, LANE), BF16),
        ((C, CH, LANE), BF16),
        ((S * 32, LANE), F32),
        ((S, 32, LANE), BF16),
        ((S, 32, LANE), BF16),
        ((S, 32, LANE), F32),
        ((272, LANE), F32),
        ((256, 512), BF16),
        ((256, LANE), F32),
        ((S, 32, LANE), BF16),
        ((S, 32, LANE), BF16),
        ((C, CH, FULL), BF16),
        ((C, CH, FULL), BF16),
        ((FULL, FULL), BF16),
        ((FULL, LANE), F32),
        ((C, CH, LANE), BF16),
        ((C, CH, LANE), BF16),
        ((C, CH, LANE), BF16),
        ((C, CH, LANE), BF16),
        ((CH, LANE), BF16),
        ((S, CH, LANE), BF16),
        ((64 * S, LANE), BF16),
        ((64 * S, LANE), F32),
        ((64 * S, LANE), F32),
        ((LANE, 64 * LANE), BF16),
        ((LANE, 64 * LANE), BF16),
        ((24, LANE), I32),
        ((C, 24, LANE), I32),
        ((LANE, LANE), F32),
        ((FULL + 16, ITEMS), BF16),
        ((GROUPS + 1, C, CH, LANE), BF16),
        ((GROUPS + 1, C, CH, LANE), BF16),
        ((24, LANE), F32),
        ((24, LANE), F32),
        ((GROUPS, 2 * LANE, C * LANE), BF16),
        ((len(TGT_LANES), 8 * LANE, LANE), BF16),
        ((GROUPS + 1, LANE, LANE), BF16),
        ((C, 48, LANE), F32),
        ((C, 48, LANE), F32),
        ((S, 8, LANE), F32),
        ((S, 8, LANE), F32),
        ((8, LANE), F32),
        ((C, 8, LANE), F32),
    ]
    layer_out, loss = pl.pallas_call(
        body,
        out_shape=(
            jax.ShapeDtypeStruct((4, CH, 256), BF16),
            jax.ShapeDtypeStruct((1, LANE), F32),
        ),
        in_specs=[vmem] * 5 + [pl.BlockSpec(memory_space=pl.ANY)] + [vmem] * 6,
        out_specs=(vmem, vmem),
        scratch_shapes=[pltpu.VMEM(shape, kind) for shape, kind in scratch]
        + [pltpu.SemaphoreType.DMA((EXCHANGES, S))] * 2
        + [pltpu.SemaphoreType.DMA(())],
        compiler_params=pltpu.CompilerParams(
            collective_id=0, has_side_effects=True, vmem_limit_bytes=60 * 1024 * 1024
        ),
        cost_estimate=pl.CostEstimate(
            flops=20_000_000_000, bytes_accessed=5_000_000, transcendentals=10_000
        ),
    )(
        signal.transpose(1, 2, 0),
        filter_taps.T,
        skip_gain.reshape(1, CH),
        w_gate.T,
        w_out,
        catalogue,
        item_draw_counts.reshape(1, ITEMS),
        sampled_pos.reshape(1, LANE),
        neg_owner.transpose(1, 2, 0),
        neg_row.T,
        target_owner.reshape(1, LANE),
        target_row.reshape(1, LANE),
    )
    return layer_out.transpose(2, 0, 1), loss.reshape(LANE)


def solution(mesh):
    placed = (
        P("seq", None, "ch"),
        P("seq", "ch"),
        P("ch"),
        P(None, "ch"),
        P("ch", None),
        P(("seq", "ch"), None),
        P(("seq", "ch")),
        P("seq"),
        P("seq", None, None),
        P("seq", None),
        P("seq", None),
        P("seq"),
    )
    return jax.shard_map(
        per_device,
        mesh=mesh,
        in_specs=placed,
        out_specs=(P("seq", None, "ch"), P("seq")),
        check_vma=False,
    )
```

```python
import jax
import jax.numpy as jnp
from jax import lax
from jax.experimental import pallas as pl
from jax.experimental.pallas import tpu as pltpu
from jax.sharding import PartitionSpec as P

SOFTMAX_TEMP = 0.02
EPSILON = 1e-06
MESH = pl.DeviceIdType.MESH
BF16 = jnp.bfloat16
F32 = jnp.float32
I32 = jnp.int32

S = 32
C = 8
LANE = 128
CH = 96
FULL = CH * C
TOK = 1024
NEG = 64
GROUPS = 16
SLOTS = (GROUPS + 1) * LANE
ITEMS = 2048

(
    X_CONV,
    X_BACK,
    X_QUERY,
    X_FORWARD,
    X_SUMS,
    X_SIG,
    X_WGATE,
    X_WOUT,
    X_WGATE_MATE,
    X_WOUT_MATE,
    X_TABLE,
    X_MIX,
    X_OUT,
    X_PART,
    X_FIN,
    X_ROWS,
) = range(16)
X_LAYER = X_ROWS + GROUPS // 2 + 1
CHUNKS = GROUPS // 2 + 1
EXCHANGES = X_LAYER + 8
SIDE = 4
TGT_LANES = (0, 16, 64, 80)
TGT_BLOCKS = tuple(tuple(range(first, first + 16, 2)) for first in (1, 17, 0, 16))


def iota(shape, dim):
    return lax.broadcasted_iota(I32, shape, dim)


def onehot(mask):
    return jnp.where(mask, 1.0, 0.0).astype(BF16)


def dot(a, b, ca=1, cb=0):
    return lax.dot_general(a, b, (((ca,), (cb,)), ((), ())), preferred_element_type=F32)


def split_parts(value, count):
    parts = []
    for _ in range(count):
        piece = value.astype(BF16)
        parts.append(piece)
        value = value - piece.astype(F32)
    return parts


def body(
    sig,
    taps_t,
    gain,
    wg_own,
    w_out,
    cat_hbm,
    cnt,
    spos,
    nown,
    nrow,
    town,
    trow,
    out_ref,
    loss_ref,
    cat,
    sig_send,
    sig_all,
    msgf,
    msg1,
    rcv1,
    rf,
    xpad,
    x4,
    acc,
    msg2,
    rcv2,
    wg_all,
    wo_all,
    wo_t,
    gate_t,
    mix_send,
    mix_all,
    lo_send,
    lo_all,
    q_own,
    q_all,
    ohs,
    inner,
    total,
    keys,
    vals,
    tab_own,
    tab_all,
    tab_t,
    cat_t,
    rows_send,
    rows_all,
    row_scale,
    row_log,
    ohp,
    oht,
    slot_pos,
    part,
    part_all,
    sums,
    sums_all,
    fin,
    fin_all,
    send_sem,
    recv_sem,
    cat_sem,
):
    me_s = lax.axis_index("seq")
    me_c = lax.axis_index("ch")

    def copy_to(x, device, src, dst, x_recv=None):
        return pltpu.make_async_remote_copy(
            src_ref=src,
            dst_ref=dst,
            send_sem=send_sem.at[x],
            recv_sem=recv_sem.at[x if x_recv is None else x_recv],
            device_id=device,
            device_id_type=MESH,
        )

    def arrived(x, like):
        copy_to(x, (me_s, me_c), like, like).wait_recv()

    def sent(x, like):
        copy_to(x, (me_s, me_c), like, like).wait_send()

    def over(n, me, fn):
        def step(d, carry):
            fn(lax.rem(me + d, n))
            return carry

        lax.fori_loop(1, n, step, 0)

    def start_seq(x, src_of, dst):
        over(S, me_s, lambda p: copy_to(x, (p, me_c), src_of(p), dst.at[me_s]).start())

    def start_ch(x, src_of, dst):
        over(C, me_c, lambda p: copy_to(x, (me_s, p), src_of(p), dst.at[me_c]).start())

    def wait_seq(x, dst):
        arrived(x, dst.at[pl.ds(0, S - 1)])

    def wait_ch(x, dst):
        arrived(x, dst.at[pl.ds(0, C - 1)])

    def sent_seq(x, dst):
        sent(x, dst.at[pl.ds(0, S - 1)])

    def sent_ch(x, dst):
        sent(x, dst.at[pl.ds(0, C - 1)])

    barrier = pltpu.get_barrier_semaphore()

    def greet_seq(peer):
        pl.semaphore_signal(barrier, inc=1, device_id=(peer, me_c), device_id_type=MESH)

    def greet_ch(peer):
        pl.semaphore_signal(barrier, inc=1, device_id=(me_s, peer), device_id_type=MESH)

    over(S, me_s, greet_seq)
    over(C, me_c, greet_ch)

    cat_copy = pltpu.make_async_copy(cat_hbm, cat, cat_sem)
    cat_copy.start()

    upper = onehot(iota((LANE, LANE), 0) < iota((LANE, LANE), 1))
    ones = jnp.ones((LANE, LANE), BF16)
    owner_ids = iota((S, LANE), 0)

    def own_onehot(owners):
        mine = jnp.where((owners & 7) == me_c, owners >> 3, -1)
        return jnp.where(owner_ids == mine, 1.0, 0.0)

    def mark(m, carry):
        ohs[pl.ds(pl.multiple_of(m * S, S), S), :] = own_onehot(nown[m]).astype(BF16)
        return carry

    lax.fori_loop(0, 64, mark, 0, unroll=4)
    inner[...] = dot(ohs[...], upper)
    total[...] = dot(ohs[...], ones)
    key_ids = iota((LANE, LANE), 0).astype(F32)
    lane_row = iota((1, LANE), 1)

    def key_of(hot, rank, offset):
        found = jnp.sum(hot * (rank + 1.0), axis=0, keepdims=True)
        place = jnp.where(found > 0.5, found - 1.0 + offset, -1.0)
        return jnp.where(key_ids == place, 1.0, 0.0).astype(BF16)

    def value_of(hot, rows):
        high = (rows >> 8).astype(F32)
        low = (rows & 255).astype(F32)
        pieces = [hot * high, hot * low, hot * lane_row.astype(F32), hot]
        return jnp.concatenate(pieces, axis=0).astype(BF16)

    odd = lax.rem(me_s, 2)
    neg_offset = (odd * NEG).astype(F32)
    tgt_offset = ((1 - odd) * NEG + me_s - odd).astype(F32)

    def place(m, before):
        rows = pl.ds(pl.multiple_of(m * S, S), S)
        lanes = pl.ds(pl.multiple_of(m * LANE, LANE), LANE)
        hot = ohs[rows, :].astype(F32)
        keys[:, lanes] = key_of(hot, inner[rows, :] + before, neg_offset)
        vals[:, lanes] = value_of(hot, nrow[pl.ds(m, 1), :])
        return before + total[rows, :]

    lax.fori_loop(0, 64, place, jnp.zeros((S, LANE), F32), unroll=4)
    hot = own_onehot(town[...])
    rank = dot(hot.astype(BF16), upper)
    found = dot(vals[...], keys[...], 1, 1) + dot(
        value_of(hot, trow[...]), key_of(hot, rank, tgt_offset), 1, 1
    )
    high, low, pos, filled = (found[i * S : (i + 1) * S].astype(I32) for i in range(4))
    entry = (high * 256 + low) * LANE + pos
    entry_high = jnp.where(filled > 0, (entry >> 9) - 256, 1024).astype(F32)
    entry_low = jnp.where(filled > 0, (entry & 511) - 256, 0).astype(F32)

    for q in range(8):
        piece = sig[q % 4, :, (q // 4) * LANE : (q // 4 + 1) * LANE]
        sig_send[q] = piece
        for k in range(3):
            msgf[pl.ds(k * 8 + q, S, stride=32), :] = piece[k * 32 : (k + 1) * 32].astype(F32)
    for il in range(2):
        for k in range(3):
            msgf[pl.ds(24 + 2 * k + il, S, stride=32), :] = taps_t[
                k * 32 : (k + 1) * 32, il * LANE : (il + 1) * LANE
            ]
    msgf[pl.ds(30, S, stride=32), :] = entry_high
    msgf[pl.ds(31, S, stride=32), :] = entry_low
    msg1[...] = msgf[...].reshape(S, 32, LANE).astype(BF16)

    pl.semaphore_wait(barrier, S - 1 + C - 1)

    start_seq(X_CONV, lambda p: msg1.at[p], rcv1)
    rcv1[me_s] = msg1[me_s]
    start_ch(X_SIG, lambda p: sig_send.at[p], sig_all)
    sig_all[me_c] = sig_send[me_c]

    core = lax.rem(me_c, 2)
    mate = me_c + 1 - 2 * core

    def over_x(fn):
        def step(d, carry):
            fn(lax.rem(me_c + 2 * d, C))
            return carry

        lax.fori_loop(1, SIDE, step, 0)

    def start_weight(x, x_mate, src, dst):
        over_x(lambda p: copy_to(x, (me_s, p), src, dst.at[me_c]).start())
        copy_to(x, (me_s, mate), src, dst.at[me_c], x_mate).start()
        dst[me_c] = src[...]

    def pass_weight(x, x_mate, dst):
        arrived(x, dst.at[pl.ds(0, SIDE - 1)])
        over_x(lambda p: copy_to(x_mate, (me_s, mate), dst.at[p], dst.at[p]).start())

    def wait_weight(x_mate, dst):
        arrived(x_mate, dst.at[pl.ds(0, SIDE)])

    def sent_weight(x, x_mate, dst):
        sent(x, dst.at[pl.ds(0, SIDE)])
        sent(x_mate, dst.at[pl.ds(0, SIDE - 1)])

    start_weight(X_WGATE, X_WGATE_MATE, wg_own, wg_all)
    start_weight(X_WOUT, X_WOUT_MATE, w_out, wo_all)

    cat_copy.wait()

    def turn(i, carry):
        span = pl.ds(pl.multiple_of(i * 256, 256), 256)
        cat_t[0:FULL, span] = cat[span, :].T
        return carry

    lax.fori_loop(0, ITEMS // 256, turn, 0)
    cat_t[FULL : FULL + 16, :] = jnp.broadcast_to(cnt[...].astype(F32), (16, ITEMS)).astype(BF16)

    wait_seq(X_CONV, rcv1)
    rf[...] = rcv1[...].astype(F32)
    xpad[0:16, :] = jnp.zeros((16, LANE), F32)
    later = iota((LANE, LANE), 1) >= iota((LANE, LANE), 0)
    for k in range(3):
        xpad[16:272, :] = rf[:, k * 8 : (k + 1) * 8, :].reshape(256, LANE)
        x4[...] = jnp.concatenate(
            [xpad[16 - 4 * j : 272 - 4 * j, :] for j in range(4)], axis=1
        ).astype(BF16)
        acc[...] = jnp.zeros_like(acc)
        prev = jnp.zeros((LANE, LANE), F32)
        for e in range(16):
            tiles = []
            for j in range(4):
                d = 4 * e + j
                row = 24 + 2 * k + d % 2
                chunk = jnp.broadcast_to(rf[d // 2, row : row + 1, :], (LANE, LANE))
                turned = pltpu.roll(chunk, 0, 1, stride=1, stride_axis=0)
                tiles.append(jnp.where(later, turned, prev).astype(BF16))
                prev = turned
            taps_tile = jnp.concatenate(tiles, axis=0)
            acc[16 * e :, :] += dot(x4[0 : 256 - 16 * e, :], taps_tile)
        for s in range(S):
            msgf[s * 32 + k * 8 : s * 32 + k * 8 + 8, :] = acc[s * 8 : s * 8 + 8, :]
    msg2[...] = msgf[...].reshape(S, 32, LANE).astype(BF16)
    start_seq(X_BACK, lambda p: msg2.at[p], rcv2)
    rcv2[me_s] = msg2[me_s]

    asked_high = rf[:, 30, :].astype(I32)
    asked_low = rf[:, 31, :].astype(I32)
    asked = jnp.where(asked_high < 512, (asked_high + 256) * 512 + asked_low + 256, -1)
    asked = asked.reshape(GROUPS, 2, LANE)
    even_half, odd_half = asked[:, 0, :], asked[:, 1, :]
    first_half = iota((GROUPS, LANE), 1) < NEG
    tab_own[...] = jnp.full(tab_own.shape, -1, I32)
    tab_own[0:GROUPS, :] = jnp.where(first_half, even_half, odd_half)
    tab_own[GROUPS : GROUPS + 1, :] = jnp.max(
        jnp.where(first_half, odd_half, even_half), axis=0, keepdims=True
    )
    start_ch(X_TABLE, lambda p: tab_own, tab_all)
    tab_all[me_c] = tab_own[...]
    row_scale[...] = jnp.zeros_like(row_scale)
    row_log[...] = jnp.zeros_like(row_log)
    item_ids = iota((ITEMS, LANE), 0)

    def picked(group):
        return onehot(item_ids == (tab_own[pl.ds(group, 1), :] >> 7))

    def keep(found, width, group0):
        for i in range(width // LANE):
            lanes = slice(i * LANE, (i + 1) * LANE)
            for c in range(C):
                rows_send[group0 + i, c] = found[c * CH : (c + 1) * CH, lanes].astype(BF16)
            rows_all[group0 + i, me_c] = rows_send[group0 + i, me_c]
        square = jnp.sum(found[0:FULL] * found[0:FULL], axis=0, keepdims=True)
        scale = lax.rsqrt(square / FULL + EPSILON) / (FULL * SOFTMAX_TEMP)
        logs = jnp.log(jnp.maximum(found[FULL : FULL + 1], 1.0))
        for i in range(width // LANE):
            row_scale[pl.ds(group0 + i, 1), :] = scale[:, i * LANE : (i + 1) * LANE]
            row_log[pl.ds(group0 + i, 1), :] = logs[:, i * LANE : (i + 1) * LANE]

    def chunk_copy(h, peer):
        span = pl.ds(2 * h, 2)
        src, dst = rows_send.at[span, peer], rows_all.at[span, me_c]
        return copy_to(X_ROWS + h, (me_s, peer), src, dst)

    def target_copy(peer):
        src, dst = rows_send.at[GROUPS, peer], rows_all.at[GROUPS, me_c]
        return copy_to(X_ROWS + CHUNKS - 1, (me_s, peer), src, dst)

    def fetch(first, last):
        def step(h, carry):
            hot = jnp.concatenate([picked(2 * h), picked(2 * h + 1)], axis=1)
            keep(dot(cat_t[...], hot), 256, 2 * h)
            over(C, me_c, lambda peer: chunk_copy(h, peer).start())
            return carry

        lax.fori_loop(first, last, step, 0)

    def fetch_targets():
        keep(dot(cat_t[...], picked(GROUPS)), LANE, GROUPS)
        over(C, me_c, lambda peer: target_copy(peer).start())

    def each_chunk(fn):
        def step(h, carry):
            fn(X_ROWS + h, rows_all.at[pl.ds(2 * h, 2), pl.ds(0, C - 1)])
            return carry

        lax.fori_loop(0, CHUNKS - 1, step, 0)
        fn(X_ROWS + CHUNKS - 1, rows_all.at[GROUPS, pl.ds(0, C - 1)])

    fetch(0, 4)
    pass_weight(X_WGATE, X_WGATE_MATE, wg_all)
    wait_ch(X_SIG, sig_all)

    wait_seq(X_BACK, rcv2)
    rf[...] = rcv2[...].astype(F32)
    msgf[...] = rf[...].reshape(S * 32, LANE)
    diag = iota((CH, CH), 0) == iota((CH, CH), 1)
    gain_col = jnp.sum(jnp.where(diag, gain[...], 0.0), axis=1, keepdims=True)
    for q in range(8):
        conv = jnp.concatenate(
            [msgf[pl.ds(k * 8 + q, S, stride=32), :] for k in range(3)], axis=0
        )
        mix_send[q] = (conv + gain_col * sig_send[q].astype(F32)).astype(BF16)
    start_ch(X_MIX, lambda p: mix_send.at[p], mix_all)
    mix_all[me_c] = mix_send[me_c]
    pass_weight(X_WOUT, X_WOUT_MATE, wo_all)

    wait_weight(X_WGATE_MATE, wg_all)
    gate_t[...] = dot(wg_all[...].reshape(FULL, FULL), sig_all[...].reshape(FULL, LANE))
    fetch(4, 6)
    wait_weight(X_WOUT_MATE, wo_all)
    wo_t[...] = wo_all[...].reshape(FULL, FULL).T
    wait_ch(X_MIX, mix_all)
    mix = mix_all[...].reshape(FULL, LANE).astype(F32) * gate_t[...]
    lo_send[...] = dot(wo_t[...], mix.astype(BF16)).astype(BF16).reshape(C, CH, LANE)
    start_ch(X_OUT, lambda p: lo_send.at[p], lo_all)
    lo_all[me_c] = lo_send[me_c]

    fetch(6, 8)
    tok_pos = spos[...]
    pos_in = tok_pos >> 2
    where_in = ((pos_in >> 7) * 4 + (tok_pos & 3)) * LANE + (pos_in & 127)
    pick = onehot(iota((TOK, LANE), 0) == where_in)

    wait_ch(X_OUT, lo_all)
    lo_t = jnp.concatenate([lo_all[q] for q in range(8)], axis=1)
    q_own[...] = dot(lo_t, pick).astype(BF16)

    me_z, me_y = me_s // SIDE, lax.rem(me_s, SIDE)
    layers = S // SIDE

    def along_z(fn):
        def step(d, carry):
            fn(lax.rem(me_z + d, layers))
            return carry

        lax.fori_loop(1, layers, step, 0)

    def along_y(block, src):
        def step(d, carry):
            peer = me_z * SIDE + lax.rem(me_y + d, SIDE)
            copy_to(X_FORWARD, (peer, me_c), src, q_all.at[block]).start()
            return carry

        lax.fori_loop(1, SIDE, step, 0)

    along_z(
        lambda z: copy_to(
            X_QUERY, (z * SIDE + me_y, me_c), q_own, q_all.at[me_s], X_LAYER + me_z
        ).start()
    )
    along_y(me_s, q_own)
    q_all[me_s] = q_own[...]
    for q in range(8):
        out_ref[q % 4, :, (q // 4) * LANE : (q // 4 + 1) * LANE] = lo_all[q]

    def go_on(z):
        block = z * SIDE + me_y
        arrived(X_LAYER + z, q_own)
        along_y(block, q_all.at[block])

    along_z(go_on)
    fetch_targets()

    wait_ch(X_TABLE, tab_all)
    pair_ids = iota((2 * LANE, LANE), 0)

    def slots(g, carry):
        for c in range(C):
            entry = tab_all[c, pl.ds(g, 1), :]
            target = jnp.where(entry < 0, -1, (entry & 127) + jnp.where(lane_row < NEG, 0, LANE))
            ohp[g, :, c * LANE : (c + 1) * LANE] = onehot(pair_ids == target)
        return carry

    lax.fori_loop(0, GROUPS, slots, 0)
    wide_ids = iota((8 * LANE, LANE), 0)
    part_of = lane_row >> 4
    for o, lane0 in enumerate(TGT_LANES):
        entry = jnp.full((1, LANE), -1, I32)
        for c in range(C):
            turned = pltpu.roll(tab_all[c, GROUPS : GROUPS + 1, :], (16 * c - lane0) % LANE, 1)
            entry = jnp.where(part_of == c, turned, entry)
        target = jnp.where(entry < 0, -1, ((lane_row & 15) >> 1) * LANE + (entry & 127))
        oht[o] = onehot(wide_ids == target)
    tab_t[...] = jnp.full(tab_t.shape, -1.0, F32)
    tab_t[0:24, :] = jnp.where(tab_own[...] < 0, -1, tab_own[...] & 127).astype(F32)
    columns = tab_t[...].T
    pos_ids = iota((LANE, LANE), 1).astype(F32)
    for g in range(GROUPS + 1):
        slot_pos[g] = onehot(columns[:, g : g + 1] == pos_ids)

    each_chunk(arrived)
    tgt_rows = []
    for lane0 in TGT_LANES:
        rows = jnp.zeros((CH, LANE), F32)
        for c in range(C):
            turned = pltpu.roll(rows_all[GROUPS, c].astype(F32), (16 * c - lane0) % LANE, 1)
            rows = jnp.where(part_of == c, turned, rows)
        tgt_rows.append(rows)
    part[...] = jnp.zeros_like(part)

    arrived(X_FORWARD, q_all.at[pl.ds(0, S - layers)])

    def pair(g, carry):
        both = jnp.concatenate([q_all[2 * g], q_all[2 * g + 1]], axis=1)
        query = dot(both, ohp[g])
        for c in range(C):
            one = query[:, c * LANE : (c + 1) * LANE]
            rows = rows_all[g, c].astype(F32)
            part[c, pl.ds(g, 1), :] = jnp.sum(one * rows, axis=0, keepdims=True)
            part[c, pl.ds(24 + g, 1), :] = jnp.sum(one * one, axis=0, keepdims=True)
        return carry

    lax.fori_loop(0, GROUPS, pair, 0, unroll=2)
    tgt_part = [[jnp.zeros((1, LANE), F32) for _ in range(2)] for _ in range(C)]
    for o, lane0 in enumerate(TGT_LANES):
        wide = jnp.concatenate([q_all[b] for b in TGT_BLOCKS[o]], axis=1)
        one = dot(wide, oht[o])
        for i, rows in enumerate((tgt_rows[o], one)):
            both = jnp.sum(one * rows, axis=0, keepdims=True)
            for c in range(C):
                turned = pltpu.roll(both, (lane0 - 16 * c) % LANE, 1)
                ours = (lane_row >= lane0) & (lane_row < lane0 + 16)
                tgt_part[c][i] = jnp.where(ours, turned, tgt_part[c][i])
    for c in range(C):
        part[c, GROUPS : GROUPS + 1, :] = tgt_part[c][0]
        part[c, 24 + GROUPS : 25 + GROUPS, :] = tgt_part[c][1]
    start_ch(X_PART, lambda p: part.at[p], part_all)
    part_all[me_c] = part[me_c]
    wait_ch(X_PART, part_all)
    whole = jnp.sum(part_all[...], axis=0)
    query_scale = lax.rsqrt(whole[24:48] / FULL + EPSILON)
    logit = whole[0:24] * query_scale * row_scale[...] - row_log[...]
    filled = tab_own[...] >= 0
    exp_neg = jnp.where(filled, jnp.exp(logit), 0.0)[0:GROUPS]
    halves = [jnp.where(first_half, exp_neg, 0.0), jnp.where(first_half, 0.0, exp_neg)]
    exp_parts = jnp.concatenate([p for half in halves for p in split_parts(half, 2)], axis=0)
    tgt_logit = jnp.where(filled, logit, 0.0)[GROUPS : GROUPS + 1]
    block_of = 2 * ((lane_row & 63) >> 1) + jnp.where(lane_row < NEG, 1, 0)
    by_block = jnp.where(iota((S, LANE), 0) == block_of, tgt_logit, 0.0)
    tgt_parts = jnp.concatenate(split_parts(by_block, 3), axis=0)
    targets = dot(tgt_parts, slot_pos[GROUPS])
    targets = targets[0:S] + targets[S : 2 * S] + targets[2 * S : 3 * S]
    sums[...] = jnp.zeros_like(sums)
    sums[:, 1, :] = targets
    for g in range(GROUPS):
        found = dot(exp_parts, slot_pos[g])
        sums[2 * g, 0:1, :] = found[g : g + 1] + found[16 + g : 17 + g]
        sums[2 * g + 1, 0:1, :] = found[32 + g : 33 + g] + found[48 + g : 49 + g]
    start_seq(X_SUMS, lambda p: sums.at[p], sums_all)
    sums_all[me_s] = sums[me_s]
    wait_seq(X_SUMS, sums_all)
    fin[...] = jnp.sum(sums_all[...], axis=0)
    start_ch(X_FIN, lambda p: fin, fin_all)
    fin_all[me_c] = fin[...]
    wait_ch(X_FIN, fin_all)
    last = jnp.sum(fin_all[...], axis=0)
    target_logit = last[1:2]
    loss_ref[...] = jnp.log(jnp.exp(target_logit) + last[0:1]) - target_logit

    sent_seq(X_CONV, rcv1)
    sent_seq(X_BACK, rcv2)
    sent(X_QUERY, q_all.at[pl.ds(0, layers - 1)])
    sent(X_FORWARD, q_all.at[pl.ds(0, S - layers)])
    sent_seq(X_SUMS, sums_all)
    sent_ch(X_SIG, sig_all)
    sent_weight(X_WGATE, X_WGATE_MATE, wg_all)
    sent_weight(X_WOUT, X_WOUT_MATE, wo_all)
    sent_ch(X_TABLE, tab_all)
    each_chunk(sent)
    sent_ch(X_MIX, mix_all)
    sent_ch(X_OUT, lo_all)
    sent_ch(X_PART, part_all)
    sent_ch(X_FIN, fin_all)


def per_device(
    signal,
    filter_taps,
    skip_gain,
    w_gate,
    w_out,
    catalogue,
    item_draw_counts,
    sampled_pos,
    neg_owner,
    neg_row,
    target_owner,
    target_row,
):
    vmem = pl.BlockSpec(memory_space=pltpu.VMEM)
    scratch = [
        ((ITEMS, FULL), BF16),
        ((C, CH, LANE), BF16),
        ((C, CH, LANE), BF16),
        ((S * 32, LANE), F32),
        ((S, 32, LANE), BF16),
        ((S, 32, LANE), BF16),
        ((S, 32, LANE), F32),
        ((272, LANE), F32),
        ((256, 512), BF16),
        ((256, LANE), F32),
        ((S, 32, LANE), BF16),
        ((S, 32, LANE), BF16),
        ((C, CH, FULL), BF16),
        ((C, CH, FULL), BF16),
        ((FULL, FULL), BF16),
        ((FULL, LANE), F32),
        ((C, CH, LANE), BF16),
        ((C, CH, LANE), BF16),
        ((C, CH, LANE), BF16),
        ((C, CH, LANE), BF16),
        ((CH, LANE), BF16),
        ((S, CH, LANE), BF16),
        ((64 * S, LANE), BF16),
        ((64 * S, LANE), F32),
        ((64 * S, LANE), F32),
        ((LANE, 64 * LANE), BF16),
        ((LANE, 64 * LANE), BF16),
        ((24, LANE), I32),
        ((C, 24, LANE), I32),
        ((LANE, LANE), F32),
        ((FULL + 16, ITEMS), BF16),
        ((GROUPS + 1, C, CH, LANE), BF16),
        ((GROUPS + 1, C, CH, LANE), BF16),
        ((24, LANE), F32),
        ((24, LANE), F32),
        ((GROUPS, 2 * LANE, C * LANE), BF16),
        ((len(TGT_LANES), 8 * LANE, LANE), BF16),
        ((GROUPS + 1, LANE, LANE), BF16),
        ((C, 48, LANE), F32),
        ((C, 48, LANE), F32),
        ((S, 8, LANE), F32),
        ((S, 8, LANE), F32),
        ((8, LANE), F32),
        ((C, 8, LANE), F32),
    ]
    layer_out, loss = pl.pallas_call(
        body,
        out_shape=(
            jax.ShapeDtypeStruct((4, CH, 256), BF16),
            jax.ShapeDtypeStruct((1, LANE), F32),
        ),
        in_specs=[vmem] * 5 + [pl.BlockSpec(memory_space=pl.ANY)] + [vmem] * 6,
        out_specs=(vmem, vmem),
        scratch_shapes=[pltpu.VMEM(shape, kind) for shape, kind in scratch]
        + [pltpu.SemaphoreType.DMA((EXCHANGES,))] * 2
        + [pltpu.SemaphoreType.DMA(())],
        compiler_params=pltpu.CompilerParams(
            collective_id=0, has_side_effects=True, vmem_limit_bytes=60 * 1024 * 1024
        ),
        cost_estimate=pl.CostEstimate(
            flops=20_000_000_000, bytes_accessed=5_000_000, transcendentals=10_000
        ),
    )(
        signal.transpose(1, 2, 0),
        filter_taps.T,
        skip_gain.reshape(1, CH),
        w_gate.T,
        w_out,
        catalogue,
        item_draw_counts.reshape(1, ITEMS),
        sampled_pos.reshape(1, LANE),
        neg_owner.transpose(1, 2, 0),
        neg_row.T,
        target_owner.reshape(1, LANE),
        target_row.reshape(1, LANE),
    )
    return layer_out.transpose(2, 0, 1), loss.reshape(LANE)


def solution(mesh):
    placed = (
        P("seq", None, "ch"),
        P("seq", "ch"),
        P("ch"),
        P(None, "ch"),
        P("ch", None),
        P(("seq", "ch"), None),
        P(("seq", "ch")),
        P("seq"),
        P("seq", None, None),
        P("seq", None),
        P("seq", None),
        P("seq"),
    )
    return jax.shard_map(
        per_device,
        mesh=mesh,
        in_specs=placed,
        out_specs=(P("seq", None, "ch"), P("seq")),
        check_vma=False,
    )
```

```python
import jax
import jax.numpy as jnp
from jax import lax
from jax.experimental import pallas as pl
from jax.experimental.pallas import tpu as pltpu
from jax.sharding import PartitionSpec as P

SOFTMAX_TEMP = 0.02
EPSILON = 1e-06
MESH = pl.DeviceIdType.MESH
BF16 = jnp.bfloat16
F32 = jnp.float32
I32 = jnp.int32

S = 32
C = 8
LANE = 128
CH = 96
FULL = CH * C
TOK = 1024
NEG = 64
GROUPS = 16
SLOTS = (GROUPS + 1) * LANE
ITEMS = 2048

(
    X_CONV,
    X_BACK,
    X_QUERY,
    X_FORWARD,
    X_ACROSS,
    X_SUMS,
    X_SIG,
    X_WGATE,
    X_WOUT,
    X_WGATE_MATE,
    X_WOUT_MATE,
    X_TABLE,
    X_TABLE_Y,
    X_MIX,
    X_OUT,
    X_PART,
    X_PART_Y,
    X_FIN,
    X_ROWS,
) = range(19)
X_LAYER = X_ROWS + GROUPS // 2 + 2
CHUNKS = GROUPS // 2
HALF = GROUPS // 2
EXCHANGES = X_LAYER + 8
SIDE = 4
TGT_LANES = (0, 16, 64, 80)
TGT_BLOCKS = tuple(tuple(range(first, first + 16, 2)) for first in (1, 17, 0, 16))


def iota(shape, dim):
    return lax.broadcasted_iota(I32, shape, dim)


def onehot(mask):
    return jnp.where(mask, 1.0, 0.0).astype(BF16)


def dot(a, b, ca=1, cb=0):
    return lax.dot_general(a, b, (((ca,), (cb,)), ((), ())), preferred_element_type=F32)


def split_parts(value, count):
    parts = []
    for _ in range(count):
        piece = value.astype(BF16)
        parts.append(piece)
        value = value - piece.astype(F32)
    return parts


def body(
    sig,
    taps_t,
    gain,
    wg_own,
    w_out,
    cat_hbm,
    cnt,
    spos,
    nown,
    nrow,
    town,
    trow,
    out_ref,
    loss_ref,
    cat,
    sig_send,
    sig_all,
    msgf,
    msg1,
    rcv1,
    rf,
    xpad,
    x4,
    acc,
    msg2,
    rcv2,
    wg_all,
    wo_all,
    wo_t,
    gate_t,
    mix_send,
    mix_all,
    lo_send,
    lo_all,
    q_own,
    q_stage,
    q_all,
    ohs,
    inner,
    total,
    keys,
    vals,
    tab_own,
    tab_all,
    tab_t,
    cat_t,
    rows_send,
    rows_all,
    row_scale,
    row_log,
    ohp,
    oht,
    slot_pos,
    part,
    part_all,
    sums,
    sums_all,
    fin,
    fin_all,
    send_sem,
    recv_sem,
    cat_sem,
):
    me_s = lax.axis_index("seq")
    me_c = lax.axis_index("ch")
    me_z, me_y = me_s // SIDE, lax.rem(me_s, SIDE)
    me_x, core = me_c // 2, lax.rem(me_c, 2)
    me_v = me_y * 2 + core
    layers = S // SIDE

    def beside(y, x):
        return (me_z * SIDE + y, x * 2 + core)

    def split_peer(along_x, p):
        seq = jnp.where(along_x, me_s, me_z * SIDE + p // 2)
        return (seq, jnp.where(along_x, p, me_x * 2 + lax.rem(p, 2)))

    def copy_to(x, device, src, dst, x_recv=None):
        return pltpu.make_async_remote_copy(
            src_ref=src,
            dst_ref=dst,
            send_sem=send_sem.at[x],
            recv_sem=recv_sem.at[x if x_recv is None else x_recv],
            device_id=device,
            device_id_type=MESH,
        )

    def arrived(x, like):
        copy_to(x, (me_s, me_c), like, like).wait_recv()

    def sent(x, like):
        copy_to(x, (me_s, me_c), like, like).wait_send()

    def over(n, me, fn):
        def step(d, carry):
            fn(lax.rem(me + d, n))
            return carry

        lax.fori_loop(1, n, step, 0)

    def start_seq(x, src_of, dst):
        over(S, me_s, lambda p: copy_to(x, (p, me_c), src_of(p), dst.at[me_s]).start())

    def start_ch(x, src_of, dst):
        over(C, me_c, lambda p: copy_to(x, (me_s, p), src_of(p), dst.at[me_c]).start())

    def wait_seq(x, dst):
        arrived(x, dst.at[pl.ds(0, S - 1)])

    def wait_ch(x, dst):
        arrived(x, dst.at[pl.ds(0, C - 1)])

    def sent_seq(x, dst):
        sent(x, dst.at[pl.ds(0, S - 1)])

    def sent_ch(x, dst):
        sent(x, dst.at[pl.ds(0, C - 1)])

    barrier = pltpu.get_barrier_semaphore()

    def greet_seq(peer):
        pl.semaphore_signal(barrier, inc=1, device_id=(peer, me_c), device_id_type=MESH)

    def greet_ch(peer):
        pl.semaphore_signal(barrier, inc=1, device_id=(me_s, peer), device_id_type=MESH)

    over(S, me_s, greet_seq)
    over(C, me_c, greet_ch)
    for y in range(SIDE):

        @pl.when(me_y != y)
        def _():
            other = (me_z * SIDE + y, me_x * 2 + 1 - core)
            pl.semaphore_signal(barrier, inc=1, device_id=other, device_id_type=MESH)

        @pl.when((me_y != y) | (me_x != me_y))
        def _():
            pl.semaphore_signal(barrier, inc=1, device_id=beside(y, me_y), device_id_type=MESH)

    on_diagonal = me_x == me_y

    cat_copy = pltpu.make_async_copy(cat_hbm, cat, cat_sem)
    cat_copy.start()

    upper = onehot(iota((LANE, LANE), 0) < iota((LANE, LANE), 1))
    ones = jnp.ones((LANE, LANE), BF16)
    owner_ids = iota((S, LANE), 0)

    def own_onehot(owners):
        mine = jnp.where((owners & 7) == me_c, owners >> 3, -1)
        return jnp.where(owner_ids == mine, 1.0, 0.0)

    def mark(m, carry):
        ohs[pl.ds(pl.multiple_of(m * S, S), S), :] = own_onehot(nown[m]).astype(BF16)
        return carry

    lax.fori_loop(0, 64, mark, 0, unroll=4)
    inner[...] = dot(ohs[...], upper)
    total[...] = dot(ohs[...], ones)
    key_ids = iota((LANE, LANE), 0).astype(F32)
    lane_row = iota((1, LANE), 1)

    def key_of(hot, rank, offset):
        found = jnp.sum(hot * (rank + 1.0), axis=0, keepdims=True)
        place = jnp.where(found > 0.5, found - 1.0 + offset, -1.0)
        return jnp.where(key_ids == place, 1.0, 0.0).astype(BF16)

    def value_of(hot, rows):
        high = (rows >> 8).astype(F32)
        low = (rows & 255).astype(F32)
        pieces = [hot * high, hot * low, hot * lane_row.astype(F32), hot]
        return jnp.concatenate(pieces, axis=0).astype(BF16)

    odd = lax.rem(me_s, 2)
    neg_offset = (odd * NEG).astype(F32)
    tgt_offset = ((1 - odd) * NEG + me_s - odd).astype(F32)

    def place(m, before):
        rows = pl.ds(pl.multiple_of(m * S, S), S)
        lanes = pl.ds(pl.multiple_of(m * LANE, LANE), LANE)
        hot = ohs[rows, :].astype(F32)
        keys[:, lanes] = key_of(hot, inner[rows, :] + before, neg_offset)
        vals[:, lanes] = value_of(hot, nrow[pl.ds(m, 1), :])
        return before + total[rows, :]

    lax.fori_loop(0, 64, place, jnp.zeros((S, LANE), F32), unroll=4)
    hot = own_onehot(town[...])
    rank = dot(hot.astype(BF16), upper)
    found = dot(vals[...], keys[...], 1, 1) + dot(
        value_of(hot, trow[...]), key_of(hot, rank, tgt_offset), 1, 1
    )
    high, low, pos, filled = (found[i * S : (i + 1) * S].astype(I32) for i in range(4))
    entry = (high * 256 + low) * LANE + pos
    entry_high = jnp.where(filled > 0, (entry >> 9) - 256, 1024).astype(F32)
    entry_low = jnp.where(filled > 0, (entry & 511) - 256, 0).astype(F32)

    for q in range(8):
        piece = sig[q % 4, :, (q // 4) * LANE : (q // 4 + 1) * LANE]
        sig_send[q] = piece
        for k in range(3):
            msgf[pl.ds(k * 8 + q, S, stride=32), :] = piece[k * 32 : (k + 1) * 32].astype(F32)
    for il in range(2):
        for k in range(3):
            msgf[pl.ds(24 + 2 * k + il, S, stride=32), :] = taps_t[
                k * 32 : (k + 1) * 32, il * LANE : (il + 1) * LANE
            ]
    msgf[pl.ds(30, S, stride=32), :] = entry_high
    msgf[pl.ds(31, S, stride=32), :] = entry_low
    msg1[...] = msgf[...].reshape(S, 32, LANE).astype(BF16)

    extra = SIDE - 1 + SIDE - jnp.where(on_diagonal, 1, 0)
    pl.semaphore_wait(barrier, S - 1 + C - 1 + extra)

    start_seq(X_CONV, lambda p: msg1.at[p], rcv1)
    rcv1[me_s] = msg1[me_s]
    start_ch(X_SIG, lambda p: sig_send.at[p], sig_all)
    sig_all[me_c] = sig_send[me_c]

    mate = me_c + 1 - 2 * core

    def over_x(fn):
        def step(d, carry):
            fn(lax.rem(me_c + 2 * d, C))
            return carry

        lax.fori_loop(1, SIDE, step, 0)

    def start_weight(x, x_mate, src, dst):
        over_x(lambda p: copy_to(x, (me_s, p), src, dst.at[me_c]).start())
        copy_to(x, (me_s, mate), src, dst.at[me_c], x_mate).start()
        dst[me_c] = src[...]

    def pass_weight(x, x_mate, dst):
        arrived(x, dst.at[pl.ds(0, SIDE - 1)])
        over_x(lambda p: copy_to(x_mate, (me_s, mate), dst.at[p], dst.at[p]).start())

    def wait_weight(x_mate, dst):
        arrived(x_mate, dst.at[pl.ds(0, SIDE)])

    def sent_weight(x, x_mate, dst):
        sent(x, dst.at[pl.ds(0, SIDE)])
        sent(x_mate, dst.at[pl.ds(0, SIDE - 1)])

    start_weight(X_WGATE, X_WGATE_MATE, wg_own, wg_all)
    start_weight(X_WOUT, X_WOUT_MATE, w_out, wo_all)

    cat_copy.wait()

    def turn(i, carry):
        span = pl.ds(pl.multiple_of(i * 256, 256), 256)
        cat_t[0:FULL, span] = cat[span, :].T
        return carry

    lax.fori_loop(0, ITEMS // 256, turn, 0)
    cat_t[FULL : FULL + 16, :] = jnp.broadcast_to(cnt[...].astype(F32), (16, ITEMS)).astype(BF16)

    wait_seq(X_CONV, rcv1)
    rf[...] = rcv1[...].astype(F32)
    xpad[0:16, :] = jnp.zeros((16, LANE), F32)
    later = iota((LANE, LANE), 1) >= iota((LANE, LANE), 0)
    for k in range(3):
        xpad[16:272, :] = rf[:, k * 8 : (k + 1) * 8, :].reshape(256, LANE)
        x4[...] = jnp.concatenate(
            [xpad[16 - 4 * j : 272 - 4 * j, :] for j in range(4)], axis=1
        ).astype(BF16)
        acc[...] = jnp.zeros_like(acc)
        prev = jnp.zeros((LANE, LANE), F32)
        for e in range(16):
            tiles = []
            for j in range(4):
                d = 4 * e + j
                row = 24 + 2 * k + d % 2
                chunk = jnp.broadcast_to(rf[d // 2, row : row + 1, :], (LANE, LANE))
                turned = pltpu.roll(chunk, 0, 1, stride=1, stride_axis=0)
                tiles.append(jnp.where(later, turned, prev).astype(BF16))
                prev = turned
            taps_tile = jnp.concatenate(tiles, axis=0)
            acc[16 * e :, :] += dot(x4[0 : 256 - 16 * e, :], taps_tile)
        for s in range(S):
            msgf[s * 32 + k * 8 : s * 32 + k * 8 + 8, :] = acc[s * 8 : s * 8 + 8, :]
    msg2[...] = msgf[...].reshape(S, 32, LANE).astype(BF16)
    start_seq(X_BACK, lambda p: msg2.at[p], rcv2)
    rcv2[me_s] = msg2[me_s]

    asked_high = rf[:, 30, :].astype(I32)
    asked_low = rf[:, 31, :].astype(I32)
    asked = jnp.where(asked_high < 512, (asked_high + 256) * 512 + asked_low + 256, -1)
    asked = asked.reshape(GROUPS, 2, LANE)
    even_half, odd_half = asked[:, 0, :], asked[:, 1, :]
    first_half = iota((GROUPS, LANE), 1) < NEG
    tab_own[...] = jnp.full(tab_own.shape, -1, I32)
    tab_own[0:GROUPS, :] = jnp.where(first_half, even_half, odd_half)
    tab_own[GROUPS : GROUPS + 1, :] = jnp.max(
        jnp.where(first_half, odd_half, even_half), axis=0, keepdims=True
    )
    start_ch(X_TABLE, lambda p: tab_own, tab_all.at[0])
    tab_all[0, me_c] = tab_own[...]

    def table_along_y(p):
        copy_to(X_TABLE_Y, split_peer(False, p), tab_own, tab_all.at[1, me_v]).start()

    over(C, me_v, table_along_y)
    tab_all[1, me_v] = tab_own[...]
    row_scale[...] = jnp.zeros_like(row_scale)
    row_log[...] = jnp.zeros_like(row_log)
    item_ids = iota((ITEMS, LANE), 0)

    def picked(group):
        return onehot(item_ids == (tab_own[pl.ds(group, 1), :] >> 7))

    def keep(found, width, group0):
        for i in range(width // LANE):
            lanes = slice(i * LANE, (i + 1) * LANE)
            for c in range(C):
                rows_send[group0 + i, c] = found[c * CH : (c + 1) * CH, lanes].astype(BF16)
            if width > LANE:
                mine = jnp.where(group0 < HALF, me_c, me_v)
                rows_all[group0 + i, mine] = rows_send[group0 + i, mine]
        square = jnp.sum(found[0:FULL] * found[0:FULL], axis=0, keepdims=True)
        scale = lax.rsqrt(square / FULL + EPSILON) / (FULL * SOFTMAX_TEMP)
        logs = jnp.log(jnp.maximum(found[FULL : FULL + 1], 1.0))
        for i in range(width // LANE):
            row_scale[pl.ds(group0 + i, 1), :] = scale[:, i * LANE : (i + 1) * LANE]
            row_log[pl.ds(group0 + i, 1), :] = logs[:, i * LANE : (i + 1) * LANE]

    def send_rows(x, span, to, along_x):
        mine = jnp.where(along_x, me_c, me_v)

        def fn(p):
            src, dst = rows_send.at[span, p], rows_all.at[to, mine]
            copy_to(x, split_peer(along_x, p), src, dst).start()

        over(C, mine, fn)

    def fetch(first, last):
        def step(i, carry):
            h = lax.rem(i, 2) * (CHUNKS // 2) + i // 2
            hot = jnp.concatenate([picked(2 * h), picked(2 * h + 1)], axis=1)
            keep(dot(cat_t[...], hot), 256, 2 * h)
            send_rows(X_ROWS + h, pl.ds(2 * h, 2), pl.ds(2 * h, 2), h < CHUNKS // 2)
            return carry

        lax.fori_loop(first, last, step, 0)

    def fetch_targets():
        keep(dot(cat_t[...], picked(GROUPS)), LANE, GROUPS)
        rows_all[GROUPS, me_c] = rows_send[GROUPS, me_c]
        rows_all[GROUPS + 1, me_v] = rows_send[GROUPS, me_v]
        send_rows(X_ROWS + CHUNKS, GROUPS, GROUPS, True)
        send_rows(X_ROWS + CHUNKS + 1, GROUPS, GROUPS + 1, False)

    def each_chunk(fn):
        def step(h, carry):
            fn(X_ROWS + h, rows_all.at[pl.ds(2 * h, 2), pl.ds(0, C - 1)])
            return carry

        lax.fori_loop(0, CHUNKS, step, 0)
        for i in range(2):
            fn(X_ROWS + CHUNKS + i, rows_all.at[GROUPS + i, pl.ds(0, C - 1)])

    fetch(0, 4)
    pass_weight(X_WGATE, X_WGATE_MATE, wg_all)
    wait_ch(X_SIG, sig_all)

    wait_seq(X_BACK, rcv2)
    rf[...] = rcv2[...].astype(F32)
    msgf[...] = rf[...].reshape(S * 32, LANE)
    diag = iota((CH, CH), 0) == iota((CH, CH), 1)
    gain_col = jnp.sum(jnp.where(diag, gain[...], 0.0), axis=1, keepdims=True)
    for q in range(8):
        conv = jnp.concatenate(
            [msgf[pl.ds(k * 8 + q, S, stride=32), :] for k in range(3)], axis=0
        )
        mix_send[q] = (conv + gain_col * sig_send[q].astype(F32)).astype(BF16)
    start_ch(X_MIX, lambda p: mix_send.at[p], mix_all)
    mix_all[me_c] = mix_send[me_c]
    pass_weight(X_WOUT, X_WOUT_MATE, wo_all)

    wait_weight(X_WGATE_MATE, wg_all)
    gate_t[...] = dot(wg_all[...].reshape(FULL, FULL), sig_all[...].reshape(FULL, LANE))
    fetch(4, 6)
    wait_weight(X_WOUT_MATE, wo_all)
    wo_t[...] = wo_all[...].reshape(FULL, FULL).T
    wait_ch(X_MIX, mix_all)
    mix = mix_all[...].reshape(FULL, LANE).astype(F32) * gate_t[...]
    lo_send[...] = dot(wo_t[...], mix.astype(BF16)).astype(BF16).reshape(C, CH, LANE)
    start_ch(X_OUT, lambda p: lo_send.at[p], lo_all)
    lo_all[me_c] = lo_send[me_c]

    fetch(6, 8)
    tok_pos = spos[...]
    pos_in = tok_pos >> 2
    where_in = ((pos_in >> 7) * 4 + (tok_pos & 3)) * LANE + (pos_in & 127)
    pick = onehot(iota((TOK, LANE), 0) == where_in)

    wait_ch(X_OUT, lo_all)
    lo_t = jnp.concatenate([lo_all[q] for q in range(8)], axis=1)
    q_own[...] = dot(lo_t, pick).astype(BF16)

    def along_z(fn):
        def step(d, carry):
            fn(lax.rem(me_z + d, layers))
            return carry

        lax.fori_loop(1, layers, step, 0)

    def go_on(z):
        block = z * SIDE + me_y
        first = z < layers // 2
        src = q_stage.at[z]

        def step(j, carry):
            y = jnp.where(first, j, me_x)
            x = jnp.where(first, me_x, j)
            here = (y == me_y) & (x == me_x)

            @pl.when(jnp.logical_not(here))
            def _():
                way = jnp.where(first, X_FORWARD, X_ACROSS)
                copy_to(way, beside(y, x), src, q_all.at[block]).start()

            @pl.when(here)
            def _():
                q_all[block] = q_stage[z]

            return carry

        lax.fori_loop(0, SIDE, step, 0)

    q_stage[me_z] = q_own[...]
    along_z(
        lambda z: copy_to(
            X_QUERY, (z * SIDE + me_y, me_c), q_own, q_stage.at[me_z], X_LAYER + me_z
        ).start()
    )
    go_on(me_z)
    for q in range(8):
        out_ref[q % 4, :, (q // 4) * LANE : (q // 4 + 1) * LANE] = lo_all[q]

    def take_layer(z):
        arrived(X_LAYER + z, q_own)
        go_on(z)

    along_z(take_layer)

    def each_way(fn):
        fn(X_FORWARD, q_all.at[pl.ds(0, 12)])

        @pl.when(on_diagonal)
        def _():
            fn(X_ACROSS, q_all.at[pl.ds(0, 12)])

        @pl.when(jnp.logical_not(on_diagonal))
        def _():
            fn(X_ACROSS, q_all.at[pl.ds(0, 16)])

    fetch_targets()

    wait_ch(X_TABLE, tab_all.at[0])
    wait_ch(X_TABLE_Y, tab_all.at[1])
    pair_ids = iota((2 * LANE, LANE), 0)

    def slots(g, carry):
        for c in range(C):
            entry = tab_all[g // HALF, c, pl.ds(g, 1), :]
            target = jnp.where(entry < 0, -1, (entry & 127) + jnp.where(lane_row < NEG, 0, LANE))
            ohp[g, :, c * LANE : (c + 1) * LANE] = onehot(pair_ids == target)
        return carry

    lax.fori_loop(0, GROUPS, slots, 0)
    wide_ids = iota((8 * LANE, LANE), 0)
    part_of = lane_row >> 4
    for o, lane0 in enumerate(TGT_LANES):
        entry = jnp.full((1, LANE), -1, I32)
        for c in range(C):
            listed = tab_all[o % 2, c, GROUPS : GROUPS + 1, :]
            turned = pltpu.roll(listed, (16 * c - lane0) % LANE, 1)
            entry = jnp.where(part_of == c, turned, entry)
        target = jnp.where(entry < 0, -1, ((lane_row & 15) >> 1) * LANE + (entry & 127))
        oht[o] = onehot(wide_ids == target)
    tab_t[...] = jnp.full(tab_t.shape, -1.0, F32)
    tab_t[0:24, :] = jnp.where(tab_own[...] < 0, -1, tab_own[...] & 127).astype(F32)
    columns = tab_t[...].T
    pos_ids = iota((LANE, LANE), 1).astype(F32)
    for g in range(GROUPS + 1):
        slot_pos[g] = onehot(columns[:, g : g + 1] == pos_ids)

    each_chunk(arrived)
    tgt_rows = []
    for o, lane0 in enumerate(TGT_LANES):
        rows = jnp.zeros((CH, LANE), F32)
        for c in range(C):
            there = rows_all[GROUPS + o % 2, c].astype(F32)
            turned = pltpu.roll(there, (16 * c - lane0) % LANE, 1)
            rows = jnp.where(part_of == c, turned, rows)
        tgt_rows.append(rows)
    part[...] = jnp.zeros_like(part)

    each_way(arrived)

    def pair(g, carry):
        both = jnp.concatenate([q_all[2 * g], q_all[2 * g + 1]], axis=1)
        query = dot(both, ohp[g])
        for c in range(C):
            one = query[:, c * LANE : (c + 1) * LANE]
            rows = rows_all[g, c].astype(F32)
            place = pl.ds(lax.rem(g, HALF), 1)
            square_place = pl.ds(16 + lax.rem(g, HALF), 1)
            part[g // HALF, c, place, :] = jnp.sum(one * rows, axis=0, keepdims=True)
            part[g // HALF, c, square_place, :] = jnp.sum(one * one, axis=0, keepdims=True)
        return carry

    lax.fori_loop(0, GROUPS, pair, 0, unroll=2)
    tgt_part = [[[jnp.zeros((1, LANE), F32)] * 2 for _ in range(C)] for _ in range(2)]
    for o, lane0 in enumerate(TGT_LANES):
        wide = jnp.concatenate([q_all[b] for b in TGT_BLOCKS[o]], axis=1)
        one = dot(wide, oht[o])
        for i, rows in enumerate((tgt_rows[o], one)):
            both = jnp.sum(one * rows, axis=0, keepdims=True)
            for c in range(C):
                turned = pltpu.roll(both, (lane0 - 16 * c) % LANE, 1)
                ours = (lane_row >= lane0) & (lane_row < lane0 + 16)
                tgt_part[o % 2][c][i] = jnp.where(ours, turned, tgt_part[o % 2][c][i])
    for way in range(2):
        for c in range(C):
            part[way, c, HALF : HALF + 1, :] = tgt_part[way][c][0]
            part[way, c, 16 + HALF : 17 + HALF, :] = tgt_part[way][c][1]
    start_ch(X_PART, lambda p: part.at[0, p], part_all.at[0])
    part_all[0, me_c] = part[0, me_c]

    def part_along_y(p):
        copy_to(X_PART_Y, split_peer(False, p), part.at[1, p], part_all.at[1, me_v]).start()

    over(C, me_v, part_along_y)
    part_all[1, me_v] = part[1, me_v]
    wait_ch(X_PART, part_all.at[0])
    wait_ch(X_PART_Y, part_all.at[1])
    by_x, by_y = jnp.sum(part_all[0], axis=0), jnp.sum(part_all[1], axis=0)
    whole = jnp.concatenate(
        [
            piece
            for i in (0, 16)
            for piece in (by_x[i : i + 8], by_y[i : i + 8], by_x[i + 8 : i + 16] + by_y[i + 8 : i + 16])
        ],
        axis=0,
    )
    query_scale = lax.rsqrt(whole[24:48] / FULL + EPSILON)
    logit = whole[0:24] * query_scale * row_scale[...] - row_log[...]
    filled = tab_own[...] >= 0
    exp_neg = jnp.where(filled, jnp.exp(logit), 0.0)[0:GROUPS]
    halves = [jnp.where(first_half, exp_neg, 0.0), jnp.where(first_half, 0.0, exp_neg)]
    exp_parts = jnp.concatenate([p for half in halves for p in split_parts(half, 2)], axis=0)
    tgt_logit = jnp.where(filled, logit, 0.0)[GROUPS : GROUPS + 1]
    block_of = 2 * ((lane_row & 63) >> 1) + jnp.where(lane_row < NEG, 1, 0)
    by_block = jnp.where(iota((S, LANE), 0) == block_of, tgt_logit, 0.0)
    tgt_parts = jnp.concatenate(split_parts(by_block, 3), axis=0)
    targets = dot(tgt_parts, slot_pos[GROUPS])
    targets = targets[0:S] + targets[S : 2 * S] + targets[2 * S : 3 * S]
    sums[...] = jnp.zeros_like(sums)
    sums[:, 1, :] = targets
    for g in range(GROUPS):
        found = dot(exp_parts, slot_pos[g])
        sums[2 * g, 0:1, :] = found[g : g + 1] + found[16 + g : 17 + g]
        sums[2 * g + 1, 0:1, :] = found[32 + g : 33 + g] + found[48 + g : 49 + g]
    start_seq(X_SUMS, lambda p: sums.at[p], sums_all)
    sums_all[me_s] = sums[me_s]
    wait_seq(X_SUMS, sums_all)
    fin[...] = jnp.sum(sums_all[...], axis=0)
    start_ch(X_FIN, lambda p: fin, fin_all)
    fin_all[me_c] = fin[...]
    wait_ch(X_FIN, fin_all)
    last = jnp.sum(fin_all[...], axis=0)
    target_logit = last[1:2]
    loss_ref[...] = jnp.log(jnp.exp(target_logit) + last[0:1]) - target_logit

    sent_seq(X_CONV, rcv1)
    sent_seq(X_BACK, rcv2)
    sent(X_QUERY, q_all.at[pl.ds(0, layers - 1)])
    each_way(sent)
    sent_seq(X_SUMS, sums_all)
    sent_ch(X_SIG, sig_all)
    sent_weight(X_WGATE, X_WGATE_MATE, wg_all)
    sent_weight(X_WOUT, X_WOUT_MATE, wo_all)
    sent_ch(X_TABLE, tab_all.at[0])
    sent_ch(X_TABLE_Y, tab_all.at[1])
    each_chunk(sent)
    sent_ch(X_MIX, mix_all)
    sent_ch(X_OUT, lo_all)
    sent_ch(X_PART, part_all.at[0])
    sent_ch(X_PART_Y, part_all.at[1])
    sent_ch(X_FIN, fin_all)


def per_device(
    signal,
    filter_taps,
    skip_gain,
    w_gate,
    w_out,
    catalogue,
    item_draw_counts,
    sampled_pos,
    neg_owner,
    neg_row,
    target_owner,
    target_row,
):
    vmem = pl.BlockSpec(memory_space=pltpu.VMEM)
    scratch = [
        ((ITEMS, FULL), BF16),
        ((C, CH, LANE), BF16),
        ((C, CH, LANE), BF16),
        ((S * 32, LANE), F32),
        ((S, 32, LANE), BF16),
        ((S, 32, LANE), BF16),
        ((S, 32, LANE), F32),
        ((272, LANE), F32),
        ((256, 512), BF16),
        ((256, LANE), F32),
        ((S, 32, LANE), BF16),
        ((S, 32, LANE), BF16),
        ((C, CH, FULL), BF16),
        ((C, CH, FULL), BF16),
        ((FULL, FULL), BF16),
        ((FULL, LANE), F32),
        ((C, CH, LANE), BF16),
        ((C, CH, LANE), BF16),
        ((C, CH, LANE), BF16),
        ((C, CH, LANE), BF16),
        ((CH, LANE), BF16),
        ((S // SIDE, CH, LANE), BF16),
        ((S, CH, LANE), BF16),
        ((64 * S, LANE), BF16),
        ((64 * S, LANE), F32),
        ((64 * S, LANE), F32),
        ((LANE, 64 * LANE), BF16),
        ((LANE, 64 * LANE), BF16),
        ((24, LANE), I32),
        ((2, C, 24, LANE), I32),
        ((LANE, LANE), F32),
        ((FULL + 16, ITEMS), BF16),
        ((GROUPS + 1, C, CH, LANE), BF16),
        ((GROUPS + 2, C, CH, LANE), BF16),
        ((24, LANE), F32),
        ((24, LANE), F32),
        ((GROUPS, 2 * LANE, C * LANE), BF16),
        ((len(TGT_LANES), 8 * LANE, LANE), BF16),
        ((GROUPS + 1, LANE, LANE), BF16),
        ((2, C, 32, LANE), F32),
        ((2, C, 32, LANE), F32),
        ((S, 8, LANE), F32),
        ((S, 8, LANE), F32),
        ((8, LANE), F32),
        ((C, 8, LANE), F32),
    ]
    layer_out, loss = pl.pallas_call(
        body,
        out_shape=(
            jax.ShapeDtypeStruct((4, CH, 256), BF16),
            jax.ShapeDtypeStruct((1, LANE), F32),
        ),
        in_specs=[vmem] * 5 + [pl.BlockSpec(memory_space=pl.ANY)] + [vmem] * 6,
        out_specs=(vmem, vmem),
        scratch_shapes=[pltpu.VMEM(shape, kind) for shape, kind in scratch]
        + [pltpu.SemaphoreType.DMA((EXCHANGES,))] * 2
        + [pltpu.SemaphoreType.DMA(())],
        compiler_params=pltpu.CompilerParams(
            collective_id=0, has_side_effects=True, vmem_limit_bytes=60 * 1024 * 1024
        ),
        cost_estimate=pl.CostEstimate(
            flops=20_000_000_000, bytes_accessed=5_000_000, transcendentals=10_000
        ),
    )(
        signal.transpose(1, 2, 0),
        filter_taps.T,
        skip_gain.reshape(1, CH),
        w_gate.T,
        w_out,
        catalogue,
        item_draw_counts.reshape(1, ITEMS),
        sampled_pos.reshape(1, LANE),
        neg_owner.transpose(1, 2, 0),
        neg_row.T,
        target_owner.reshape(1, LANE),
        target_row.reshape(1, LANE),
    )
    return layer_out.transpose(2, 0, 1), loss.reshape(LANE)


def solution(mesh):
    placed = (
        P("seq", None, "ch"),
        P("seq", "ch"),
        P("ch"),
        P(None, "ch"),
        P("ch", None),
        P(("seq", "ch"), None),
        P(("seq", "ch")),
        P("seq"),
        P("seq", None, None),
        P("seq", None),
        P("seq", None),
        P("seq"),
    )
    return jax.shard_map(
        per_device,
        mesh=mesh,
        in_specs=placed,
        out_specs=(P("seq", None, "ch"), P("seq")),
        check_vma=False,
    )
```

```python
import jax
import jax.numpy as jnp
from jax import lax
from jax.experimental import pallas as pl
from jax.experimental.pallas import tpu as pltpu
from jax.sharding import PartitionSpec as P

SOFTMAX_TEMP = 0.02
EPSILON = 1e-06
MESH = pl.DeviceIdType.MESH
BF16 = jnp.bfloat16
F32 = jnp.float32
I32 = jnp.int32

S = 32
C = 8
LANE = 128
CH = 96
FULL = CH * C
TOK = 1024
NEG = 64
GROUPS = 16
SLOTS = (GROUPS + 1) * LANE
ITEMS = 2048

(
    X_CONV,
    X_REQ,
    X_BACK,
    X_QUERY,
    X_FORWARD,
    X_ACROSS,
    X_SUMS,
    X_SIG,
    X_WGATE,
    X_WOUT,
    X_WGATE_MATE,
    X_WOUT_MATE,
    X_TABLE,
    X_TABLE_Y,
    X_MIX,
    X_OUT,
    X_PART,
    X_PART_Y,
    X_FIN,
    X_ROWS,
) = range(20)
X_LAYER = X_ROWS + GROUPS // 2 + 2
CHUNKS = GROUPS // 2
EARLY = 6
HALF = GROUPS // 2
X_WAY = X_LAYER + 8
EXCHANGES = X_WAY + 8
SIDE = 4
TGT_LANES = (0, 16, 64, 80)
TGT_BLOCKS = tuple(tuple(range(first, first + 16, 2)) for first in (1, 17, 0, 16))


def iota(shape, dim):
    return lax.broadcasted_iota(I32, shape, dim)


def onehot(mask):
    return jnp.where(mask, 1.0, 0.0).astype(BF16)


def dot(a, b, ca=1, cb=0):
    return lax.dot_general(a, b, (((ca,), (cb,)), ((), ())), preferred_element_type=F32)


def split_parts(value, count):
    parts = []
    for _ in range(count):
        piece = value.astype(BF16)
        parts.append(piece)
        value = value - piece.astype(F32)
    return parts


def body(
    sig,
    taps_t,
    gain,
    wg_own,
    w_out,
    cat_hbm,
    cnt,
    spos,
    nown,
    nrow,
    town,
    trow,
    out_ref,
    loss_ref,
    cat,
    sig_send,
    sig_all,
    msgf,
    msg1,
    rcv1,
    rf,
    xpad,
    x4,
    acc,
    msg2,
    rcv2,
    wg_all,
    wo_all,
    wo_t,
    gate_t,
    mix_send,
    mix_all,
    lo_send,
    lo_all,
    q_own,
    q_stage,
    q_all,
    req_msg,
    req_all,
    ohs,
    inner,
    total,
    keys,
    vals,
    tab_own,
    tab_all,
    tab_t,
    cat_t,
    rows_send,
    rows_all,
    row_scale,
    row_log,
    ohp,
    oht,
    slot_pos,
    part,
    part_all,
    sums,
    sums_all,
    fin,
    fin_all,
    send_sem,
    recv_sem,
    cat_sem,
):
    me_s = lax.axis_index("seq")
    me_c = lax.axis_index("ch")
    me_z, me_y = me_s // SIDE, lax.rem(me_s, SIDE)
    me_x, core = me_c // 2, lax.rem(me_c, 2)
    me_v = me_y * 2 + core
    layers = S // SIDE

    def beside(y, x):
        return (me_z * SIDE + y, x * 2 + core)

    def split_peer(along_x, p):
        seq = jnp.where(along_x, me_s, me_z * SIDE + p // 2)
        return (seq, jnp.where(along_x, p, me_x * 2 + lax.rem(p, 2)))

    def copy_to(x, device, src, dst, x_recv=None):
        return pltpu.make_async_remote_copy(
            src_ref=src,
            dst_ref=dst,
            send_sem=send_sem.at[x],
            recv_sem=recv_sem.at[x if x_recv is None else x_recv],
            device_id=device,
            device_id_type=MESH,
        )

    def arrived(x, like):
        copy_to(x, (me_s, me_c), like, like).wait_recv()

    def sent(x, like):
        copy_to(x, (me_s, me_c), like, like).wait_send()

    def over(n, me, fn):
        def step(d, carry):
            fn(lax.rem(me + d, n))
            return carry

        lax.fori_loop(1, n, step, 0)

    def start_seq(x, src_of, dst):
        over(S, me_s, lambda p: copy_to(x, (p, me_c), src_of(p), dst.at[me_s]).start())

    def start_ch(x, src_of, dst):
        over(C, me_c, lambda p: copy_to(x, (me_s, p), src_of(p), dst.at[me_c]).start())

    def wait_seq(x, dst):
        arrived(x, dst.at[pl.ds(0, S - 1)])

    def wait_ch(x, dst):
        arrived(x, dst.at[pl.ds(0, C - 1)])

    def sent_seq(x, dst):
        sent(x, dst.at[pl.ds(0, S - 1)])

    def sent_ch(x, dst):
        sent(x, dst.at[pl.ds(0, C - 1)])

    barrier = pltpu.get_barrier_semaphore()

    def greet_seq(peer):
        pl.semaphore_signal(barrier, inc=1, device_id=(peer, me_c), device_id_type=MESH)

    def greet_ch(peer):
        pl.semaphore_signal(barrier, inc=1, device_id=(me_s, peer), device_id_type=MESH)

    over(S, me_s, greet_seq)
    over(C, me_c, greet_ch)
    for y in range(SIDE):

        @pl.when(me_y != y)
        def _():
            other = (me_z * SIDE + y, me_x * 2 + 1 - core)
            pl.semaphore_signal(barrier, inc=1, device_id=other, device_id_type=MESH)

        @pl.when((me_y != y) | (me_x != me_y))
        def _():
            pl.semaphore_signal(barrier, inc=1, device_id=beside(y, me_y), device_id_type=MESH)

    on_diagonal = me_x == me_y

    cat_copy = pltpu.make_async_copy(cat_hbm, cat, cat_sem)
    cat_copy.start()

    for q in range(8):
        piece = sig[q % 4, :, (q // 4) * LANE : (q // 4 + 1) * LANE]
        sig_send[q] = piece
        for k in range(3):
            msgf[pl.ds(k * 8 + q, S, stride=32), :] = piece[k * 32 : (k + 1) * 32].astype(F32)
    for il in range(2):
        for k in range(3):
            msgf[pl.ds(24 + 2 * k + il, S, stride=32), :] = taps_t[
                k * 32 : (k + 1) * 32, il * LANE : (il + 1) * LANE
            ]
    for row in range(30, 32):
        msgf[pl.ds(row, S, stride=32), :] = jnp.zeros((S, LANE), F32)
    msg1[...] = msgf[...].reshape(S, 32, LANE).astype(BF16)

    extra = SIDE - 1 + SIDE - jnp.where(on_diagonal, 1, 0)
    pl.semaphore_wait(barrier, S - 1 + C - 1 + extra)

    start_seq(X_CONV, lambda p: msg1.at[p], rcv1)
    rcv1[me_s] = msg1[me_s]
    start_ch(X_SIG, lambda p: sig_send.at[p], sig_all)
    sig_all[me_c] = sig_send[me_c]

    mate = me_c + 1 - 2 * core

    def over_x(fn):
        def step(d, carry):
            fn(lax.rem(me_c + 2 * d, C))
            return carry

        lax.fori_loop(1, SIDE, step, 0)

    def start_weight(x, x_mate, src, dst):
        over_x(lambda p: copy_to(x, (me_s, p), src, dst.at[me_c]).start())
        copy_to(x, (me_s, mate), src, dst.at[me_c], x_mate).start()
        dst[me_c] = src[...]

    def pass_weight(x, x_mate, dst):
        arrived(x, dst.at[pl.ds(0, SIDE - 1)])
        over_x(lambda p: copy_to(x_mate, (me_s, mate), dst.at[p], dst.at[p]).start())

    def wait_weight(x_mate, dst):
        arrived(x_mate, dst.at[pl.ds(0, SIDE)])

    def sent_weight(x, x_mate, dst):
        sent(x, dst.at[pl.ds(0, SIDE)])
        sent(x_mate, dst.at[pl.ds(0, SIDE - 1)])

    start_weight(X_WGATE, X_WGATE_MATE, wg_own, wg_all)
    start_weight(X_WOUT, X_WOUT_MATE, w_out, wo_all)

    upper = onehot(iota((LANE, LANE), 0) < iota((LANE, LANE), 1))
    ones = jnp.ones((LANE, LANE), BF16)
    owner_ids = iota((S, LANE), 0)

    def own_onehot(owners):
        mine = jnp.where((owners & 7) == me_c, owners >> 3, -1)
        return jnp.where(owner_ids == mine, 1.0, 0.0)

    def mark(m, carry):
        ohs[pl.ds(pl.multiple_of(m * S, S), S), :] = own_onehot(nown[m]).astype(BF16)
        return carry

    lax.fori_loop(0, 64, mark, 0, unroll=4)
    inner[...] = dot(ohs[...], upper)
    total[...] = dot(ohs[...], ones)
    key_ids = iota((LANE, LANE), 0).astype(F32)
    lane_row = iota((1, LANE), 1)

    def key_of(hot, rank, offset):
        found = jnp.sum(hot * (rank + 1.0), axis=0, keepdims=True)
        place = jnp.where(found > 0.5, found - 1.0 + offset, -1.0)
        return jnp.where(key_ids == place, 1.0, 0.0).astype(BF16)

    def value_of(hot, rows):
        high = (rows >> 8).astype(F32)
        low = (rows & 255).astype(F32)
        pieces = [hot * high, hot * low, hot * lane_row.astype(F32), hot]
        return jnp.concatenate(pieces, axis=0).astype(BF16)

    odd = lax.rem(me_s, 2)
    neg_offset = (odd * NEG).astype(F32)
    tgt_offset = ((1 - odd) * NEG + me_s - odd).astype(F32)

    def place(m, before):
        rows = pl.ds(pl.multiple_of(m * S, S), S)
        lanes = pl.ds(pl.multiple_of(m * LANE, LANE), LANE)
        hot = ohs[rows, :].astype(F32)
        keys[:, lanes] = key_of(hot, inner[rows, :] + before, neg_offset)
        vals[:, lanes] = value_of(hot, nrow[pl.ds(m, 1), :])
        return before + total[rows, :]

    lax.fori_loop(0, 64, place, jnp.zeros((S, LANE), F32), unroll=4)
    hot = own_onehot(town[...])
    rank = dot(hot.astype(BF16), upper)
    found = dot(vals[...], keys[...], 1, 1) + dot(
        value_of(hot, trow[...]), key_of(hot, rank, tgt_offset), 1, 1
    )
    high, low, pos, filled = (found[i * S : (i + 1) * S].astype(I32) for i in range(4))
    entry = (high * 256 + low) * LANE + pos
    req_msg[:, 0, :] = jnp.where(filled > 0, entry, -1)
    start_seq(X_REQ, lambda p: req_msg.at[p], req_all)
    req_all[me_s] = req_msg[me_s]

    wait_seq(X_CONV, rcv1)
    rf[...] = rcv1[...].astype(F32)
    xpad[0:16, :] = jnp.zeros((16, LANE), F32)
    later = iota((LANE, LANE), 1) >= iota((LANE, LANE), 0)
    for k in range(3):
        xpad[16:272, :] = rf[:, k * 8 : (k + 1) * 8, :].reshape(256, LANE)
        x4[...] = jnp.concatenate(
            [xpad[16 - 4 * j : 272 - 4 * j, :] for j in range(4)], axis=1
        ).astype(BF16)
        acc[...] = jnp.zeros_like(acc)
        prev = jnp.zeros((LANE, LANE), F32)
        for e in range(16):
            tiles = []
            for j in range(4):
                d = 4 * e + j
                row = 24 + 2 * k + d % 2
                chunk = jnp.broadcast_to(rf[d // 2, row : row + 1, :], (LANE, LANE))
                turned = pltpu.roll(chunk, 0, 1, stride=1, stride_axis=0)
                tiles.append(jnp.where(later, turned, prev).astype(BF16))
                prev = turned
            taps_tile = jnp.concatenate(tiles, axis=0)
            acc[16 * e :, :] += dot(x4[0 : 256 - 16 * e, :], taps_tile)
        for s in range(S):
            msgf[s * 32 + k * 8 : s * 32 + k * 8 + 8, :] = acc[s * 8 : s * 8 + 8, :]
    msg2[...] = msgf[...].reshape(S, 32, LANE).astype(BF16)
    start_seq(X_BACK, lambda p: msg2.at[p], rcv2)
    rcv2[me_s] = msg2[me_s]

    wait_seq(X_REQ, req_all)
    asked = req_all[:, 0, :]
    asked = asked.reshape(GROUPS, 2, LANE)
    even_half, odd_half = asked[:, 0, :], asked[:, 1, :]
    first_half = iota((GROUPS, LANE), 1) < NEG
    tab_own[...] = jnp.full(tab_own.shape, -1, I32)
    tab_own[0:GROUPS, :] = jnp.where(first_half, even_half, odd_half)
    tab_own[GROUPS : GROUPS + 1, :] = jnp.max(
        jnp.where(first_half, odd_half, even_half), axis=0, keepdims=True
    )
    start_ch(X_TABLE, lambda p: tab_own, tab_all.at[0])
    tab_all[0, me_c] = tab_own[...]

    def table_along_y(p):
        copy_to(X_TABLE_Y, split_peer(False, p), tab_own, tab_all.at[1, me_v]).start()

    over(C, me_v, table_along_y)
    tab_all[1, me_v] = tab_own[...]
    cat_copy.wait()

    def turn(i, carry):
        span = pl.ds(pl.multiple_of(i * 256, 256), 256)
        cat_t[0:FULL, span] = cat[span, :].T
        return carry

    lax.fori_loop(0, ITEMS // 256, turn, 0)
    cat_t[FULL : FULL + 16, :] = jnp.broadcast_to(cnt[...].astype(F32), (16, ITEMS)).astype(BF16)

    row_scale[...] = jnp.zeros_like(row_scale)
    row_log[...] = jnp.zeros_like(row_log)
    item_ids = iota((ITEMS, LANE), 0)

    def picked(group):
        return onehot(item_ids == (tab_own[pl.ds(group, 1), :] >> 7))

    def keep(found, width, group0):
        for i in range(width // LANE):
            lanes = slice(i * LANE, (i + 1) * LANE)
            for c in range(C):
                rows_send[group0 + i, c] = found[c * CH : (c + 1) * CH, lanes].astype(BF16)
            if width > LANE:
                mine = jnp.where(group0 < HALF, me_c, me_v)
                rows_all[group0 + i, mine] = rows_send[group0 + i, mine]
        square = jnp.sum(found[0:FULL] * found[0:FULL], axis=0, keepdims=True)
        scale = lax.rsqrt(square / FULL + EPSILON) / (FULL * SOFTMAX_TEMP)
        logs = jnp.log(jnp.maximum(found[FULL : FULL + 1], 1.0))
        for i in range(width // LANE):
            row_scale[pl.ds(group0 + i, 1), :] = scale[:, i * LANE : (i + 1) * LANE]
            row_log[pl.ds(group0 + i, 1), :] = logs[:, i * LANE : (i + 1) * LANE]

    def send_rows(x, span, to, along_x):
        mine = jnp.where(along_x, me_c, me_v)

        def fn(p):
            src, dst = rows_send.at[span, p], rows_all.at[to, mine]
            copy_to(x, split_peer(along_x, p), src, dst).start()

        over(C, mine, fn)

    def chunk_at(i):
        return jnp.where(i < 2, i, jnp.where(i < EARLY, i + 2, i - 4))

    def send_chunk(h):
        send_rows(X_ROWS + h, pl.ds(2 * h, 2), pl.ds(2 * h, 2), h < CHUNKS // 2)

    def send_late():
        send_rows(X_ROWS + CHUNKS, GROUPS, GROUPS, True)

        def step(i, carry):
            send_chunk(chunk_at(i))
            return carry

        lax.fori_loop(EARLY, CHUNKS, step, 0)

    def fetch(first, last):
        def step(i, carry):
            h = chunk_at(i)
            hot = jnp.concatenate([picked(2 * h), picked(2 * h + 1)], axis=1)
            keep(dot(cat_t[...], hot), 256, 2 * h)

            @pl.when(i < EARLY)
            def _():
                send_chunk(h)

            return carry

        lax.fori_loop(first, last, step, 0)

    def fetch_targets():
        keep(dot(cat_t[...], picked(GROUPS)), LANE, GROUPS)
        rows_all[GROUPS, me_c] = rows_send[GROUPS, me_c]
        rows_all[GROUPS + 1, me_v] = rows_send[GROUPS, me_v]
        send_rows(X_ROWS + CHUNKS + 1, GROUPS, GROUPS + 1, False)

    def each_chunk(fn):
        def step(h, carry):
            fn(X_ROWS + h, rows_all.at[pl.ds(2 * h, 2), pl.ds(0, C - 1)])
            return carry

        lax.fori_loop(0, CHUNKS, step, 0)
        for i in range(2):
            fn(X_ROWS + CHUNKS + i, rows_all.at[GROUPS + i, pl.ds(0, C - 1)])

    fetch(0, 5)
    pass_weight(X_WGATE, X_WGATE_MATE, wg_all)
    wait_ch(X_SIG, sig_all)

    wait_seq(X_BACK, rcv2)
    rf[...] = rcv2[...].astype(F32)
    msgf[...] = rf[...].reshape(S * 32, LANE)
    diag = iota((CH, CH), 0) == iota((CH, CH), 1)
    gain_col = jnp.sum(jnp.where(diag, gain[...], 0.0), axis=1, keepdims=True)
    for q in range(8):
        conv = jnp.concatenate(
            [msgf[pl.ds(k * 8 + q, S, stride=32), :] for k in range(3)], axis=0
        )
        mix_send[q] = (conv + gain_col * sig_send[q].astype(F32)).astype(BF16)
    start_ch(X_MIX, lambda p: mix_send.at[p], mix_all)
    mix_all[me_c] = mix_send[me_c]
    pass_weight(X_WOUT, X_WOUT_MATE, wo_all)

    wait_weight(X_WGATE_MATE, wg_all)
    gate_t[...] = dot(wg_all[...].reshape(FULL, FULL), sig_all[...].reshape(FULL, LANE))
    fetch(5, 8)
    wait_weight(X_WOUT_MATE, wo_all)
    wo_t[...] = wo_all[...].reshape(FULL, FULL).T
    wait_ch(X_MIX, mix_all)
    mix = mix_all[...].reshape(FULL, LANE).astype(F32) * gate_t[...]
    lo_send[...] = dot(wo_t[...], mix.astype(BF16)).astype(BF16).reshape(C, CH, LANE)
    start_ch(X_OUT, lambda p: lo_send.at[p], lo_all)
    lo_all[me_c] = lo_send[me_c]

    fetch_targets()

    wait_ch(X_TABLE, tab_all.at[0])
    wait_ch(X_TABLE_Y, tab_all.at[1])
    pair_ids = iota((2 * LANE, LANE), 0)

    def slots(g, carry):
        for c in range(C):
            entry = tab_all[g // HALF, c, pl.ds(g, 1), :]
            target = jnp.where(entry < 0, -1, (entry & 127) + jnp.where(lane_row < NEG, 0, LANE))
            ohp[g, :, c * LANE : (c + 1) * LANE] = onehot(pair_ids == target)
        return carry

    lax.fori_loop(0, GROUPS, slots, 0)
    wide_ids = iota((8 * LANE, LANE), 0)
    part_of = lane_row >> 4
    for o, lane0 in enumerate(TGT_LANES):
        entry = jnp.full((1, LANE), -1, I32)
        for c in range(C):
            listed = tab_all[o % 2, c, GROUPS : GROUPS + 1, :]
            turned = pltpu.roll(listed, (16 * c - lane0) % LANE, 1)
            entry = jnp.where(part_of == c, turned, entry)
        target = jnp.where(entry < 0, -1, ((lane_row & 15) >> 1) * LANE + (entry & 127))
        oht[o] = onehot(wide_ids == target)
    tab_t[...] = jnp.full(tab_t.shape, -1.0, F32)
    tab_t[0:24, :] = jnp.where(tab_own[...] < 0, -1, tab_own[...] & 127).astype(F32)
    columns = tab_t[...].T
    pos_ids = iota((LANE, LANE), 1).astype(F32)
    for g in range(GROUPS + 1):
        slot_pos[g] = onehot(columns[:, g : g + 1] == pos_ids)

    tok_pos = spos[...]
    pos_in = tok_pos >> 2
    where_in = ((pos_in >> 7) * 4 + (tok_pos & 3)) * LANE + (pos_in & 127)
    pick = onehot(iota((TOK, LANE), 0) == where_in)

    wait_ch(X_OUT, lo_all)
    lo_t = jnp.concatenate([lo_all[q] for q in range(8)], axis=1)
    q_own[...] = dot(lo_t, pick).astype(BF16)

    def layer_at(i):
        near = (i + 1) // 2
        return lax.rem(me_z + jnp.where(lax.rem(i, 2) == 1, near, layers - near), layers)

    def along_z(fn):
        def step(i, carry):
            fn(layer_at(i))
            return carry

        lax.fori_loop(1, layers, step, 0)

    def go_on(z):
        block = z * SIDE + me_y
        first = z < layers // 2
        src = q_stage.at[z]

        def step(j, carry):
            y = jnp.where(first, j, me_x)
            x = jnp.where(first, me_x, j)
            here = (y == me_y) & (x == me_x)

            @pl.when(jnp.logical_not(here))
            def _():
                way = jnp.where(first, X_FORWARD, X_ACROSS)
                copy_to(way, beside(y, x), src, q_all.at[block], X_WAY + z).start()

            @pl.when(here)
            def _():
                q_all[block] = q_stage[z]

            return carry

        lax.fori_loop(0, SIDE, step, 0)

    q_stage[me_z] = q_own[...]
    along_z(
        lambda z: copy_to(
            X_QUERY, (z * SIDE + me_y, me_c), q_own, q_stage.at[me_z], X_LAYER + me_z
        ).start()
    )
    go_on(me_z)
    send_late()
    for q in range(8):
        out_ref[q % 4, :, (q // 4) * LANE : (q // 4 + 1) * LANE] = lo_all[q]

    def take_layer(z):
        arrived(X_LAYER + z, q_own)
        go_on(z)

    along_z(take_layer)

    def take_blocks(z):
        three = (z < layers // 2) | on_diagonal

        @pl.when(three)
        def _():
            arrived(X_WAY + z, q_all.at[pl.ds(0, SIDE - 1)])

        @pl.when(jnp.logical_not(three))
        def _():
            arrived(X_WAY + z, q_all.at[pl.ds(0, SIDE)])

    part[...] = jnp.zeros_like(part)

    def pair(g, carry):
        both = jnp.concatenate([q_all[2 * g], q_all[2 * g + 1]], axis=1)
        query = dot(both, ohp[g])
        for c in range(C):
            one = query[:, c * LANE : (c + 1) * LANE]
            rows = rows_all[g, c].astype(F32)
            place = pl.ds(lax.rem(g, HALF), 1)
            square_place = pl.ds(16 + lax.rem(g, HALF), 1)
            part[g // HALF, c, place, :] = jnp.sum(one * rows, axis=0, keepdims=True)
            part[g // HALF, c, square_place, :] = jnp.sum(one * one, axis=0, keepdims=True)
        return carry

    def take_rows(h, like):
        arrived(X_ROWS + h, like)

    def layer(i, carry):
        z = layer_at(i)
        take_rows(z, rows_all.at[pl.ds(2 * z, 2), pl.ds(0, C - 1)])
        take_blocks(z)
        pair(2 * z, 0)
        pair(2 * z + 1, 0)
        return carry

    lax.fori_loop(0, layers, layer, 0)
    for i in range(2):
        take_rows(CHUNKS + i, rows_all.at[GROUPS + i, pl.ds(0, C - 1)])
    tgt_rows = []
    for o, lane0 in enumerate(TGT_LANES):
        rows = jnp.zeros((CH, LANE), F32)
        for c in range(C):
            there = rows_all[GROUPS + o % 2, c].astype(F32)
            turned = pltpu.roll(there, (16 * c - lane0) % LANE, 1)
            rows = jnp.where(part_of == c, turned, rows)
        tgt_rows.append(rows)
    tgt_part = [[[jnp.zeros((1, LANE), F32)] * 2 for _ in range(C)] for _ in range(2)]
    for o, lane0 in enumerate(TGT_LANES):
        wide = jnp.concatenate([q_all[b] for b in TGT_BLOCKS[o]], axis=1)
        one = dot(wide, oht[o])
        for i, rows in enumerate((tgt_rows[o], one)):
            both = jnp.sum(one * rows, axis=0, keepdims=True)
            for c in range(C):
                turned = pltpu.roll(both, (lane0 - 16 * c) % LANE, 1)
                ours = (lane_row >= lane0) & (lane_row < lane0 + 16)
                tgt_part[o % 2][c][i] = jnp.where(ours, turned, tgt_part[o % 2][c][i])
    for way in range(2):
        for c in range(C):
            part[way, c, HALF : HALF + 1, :] = tgt_part[way][c][0]
            part[way, c, 16 + HALF : 17 + HALF, :] = tgt_part[way][c][1]
    start_ch(X_PART, lambda p: part.at[0, p], part_all.at[0])
    part_all[0, me_c] = part[0, me_c]

    def part_along_y(p):
        copy_to(X_PART_Y, split_peer(False, p), part.at[1, p], part_all.at[1, me_v]).start()

    over(C, me_v, part_along_y)
    part_all[1, me_v] = part[1, me_v]
    wait_ch(X_PART, part_all.at[0])
    wait_ch(X_PART_Y, part_all.at[1])
    by_x, by_y = jnp.sum(part_all[0], axis=0), jnp.sum(part_all[1], axis=0)
    whole = jnp.concatenate(
        [
            piece
            for i in (0, 16)
            for piece in (by_x[i : i + 8], by_y[i : i + 8], by_x[i + 8 : i + 16] + by_y[i + 8 : i + 16])
        ],
        axis=0,
    )
    query_scale = lax.rsqrt(whole[24:48] / FULL + EPSILON)
    logit = whole[0:24] * query_scale * row_scale[...] - row_log[...]
    filled = tab_own[...] >= 0
    exp_neg = jnp.where(filled, jnp.exp(logit), 0.0)[0:GROUPS]
    halves = [jnp.where(first_half, exp_neg, 0.0), jnp.where(first_half, 0.0, exp_neg)]
    exp_parts = jnp.concatenate([p for half in halves for p in split_parts(half, 2)], axis=0)
    tgt_logit = jnp.where(filled, logit, 0.0)[GROUPS : GROUPS + 1]
    block_of = 2 * ((lane_row & 63) >> 1) + jnp.where(lane_row < NEG, 1, 0)
    by_block = jnp.where(iota((S, LANE), 0) == block_of, tgt_logit, 0.0)
    tgt_parts = jnp.concatenate(split_parts(by_block, 3), axis=0)
    targets = dot(tgt_parts, slot_pos[GROUPS])
    targets = targets[0:S] + targets[S : 2 * S] + targets[2 * S : 3 * S]
    sums[:, 1, :] = targets
    for g in range(GROUPS):
        found = dot(exp_parts, slot_pos[g])
        sums[2 * g, 0:1, :] = found[g : g + 1] + found[16 + g : 17 + g]
        sums[2 * g + 1, 0:1, :] = found[32 + g : 33 + g] + found[48 + g : 49 + g]
    start_seq(X_SUMS, lambda p: sums.at[p], sums_all)
    sums_all[me_s] = sums[me_s]
    wait_seq(X_SUMS, sums_all)
    fin[...] = jnp.sum(sums_all[...], axis=0)
    start_ch(X_FIN, lambda p: fin, fin_all)
    fin_all[me_c] = fin[...]
    wait_ch(X_FIN, fin_all)
    last = jnp.sum(fin_all[...], axis=0)
    target_logit = last[1:2]
    loss_ref[...] = jnp.log(jnp.exp(target_logit) + last[0:1]) - target_logit

    sent_seq(X_CONV, rcv1)
    sent_seq(X_REQ, req_all)
    sent_seq(X_BACK, rcv2)
    sent(X_QUERY, q_all.at[pl.ds(0, layers - 1)])
    sent(X_FORWARD, q_all.at[pl.ds(0, 12)])

    @pl.when(on_diagonal)
    def _():
        sent(X_ACROSS, q_all.at[pl.ds(0, 12)])

    @pl.when(jnp.logical_not(on_diagonal))
    def _():
        sent(X_ACROSS, q_all.at[pl.ds(0, 16)])

    sent_seq(X_SUMS, sums_all)
    sent_ch(X_SIG, sig_all)
    sent_weight(X_WGATE, X_WGATE_MATE, wg_all)
    sent_weight(X_WOUT, X_WOUT_MATE, wo_all)
    sent_ch(X_TABLE, tab_all.at[0])
    sent_ch(X_TABLE_Y, tab_all.at[1])
    each_chunk(sent)
    sent_ch(X_MIX, mix_all)
    sent_ch(X_OUT, lo_all)
    sent_ch(X_PART, part_all.at[0])
    sent_ch(X_PART_Y, part_all.at[1])
    sent_ch(X_FIN, fin_all)


def per_device(
    signal,
    filter_taps,
    skip_gain,
    w_gate,
    w_out,
    catalogue,
    item_draw_counts,
    sampled_pos,
    neg_owner,
    neg_row,
    target_owner,
    target_row,
):
    vmem = pl.BlockSpec(memory_space=pltpu.VMEM)
    scratch = [
        ((ITEMS, FULL), BF16),
        ((C, CH, LANE), BF16),
        ((C, CH, LANE), BF16),
        ((S * 32, LANE), F32),
        ((S, 32, LANE), BF16),
        ((S, 32, LANE), BF16),
        ((S, 32, LANE), F32),
        ((272, LANE), F32),
        ((256, 512), BF16),
        ((256, LANE), F32),
        ((S, 32, LANE), BF16),
        ((S, 32, LANE), BF16),
        ((C, CH, FULL), BF16),
        ((C, CH, FULL), BF16),
        ((FULL, FULL), BF16),
        ((FULL, LANE), F32),
        ((C, CH, LANE), BF16),
        ((C, CH, LANE), BF16),
        ((C, CH, LANE), BF16),
        ((C, CH, LANE), BF16),
        ((CH, LANE), BF16),
        ((S // SIDE, CH, LANE), BF16),
        ((S, CH, LANE), BF16),
        ((S, 1, LANE), I32),
        ((S, 1, LANE), I32),
        ((64 * S, LANE), BF16),
        ((64 * S, LANE), F32),
        ((64 * S, LANE), F32),
        ((LANE, 64 * LANE), BF16),
        ((LANE, 64 * LANE), BF16),
        ((24, LANE), I32),
        ((2, C, 24, LANE), I32),
        ((LANE, LANE), F32),
        ((FULL + 16, ITEMS), BF16),
        ((GROUPS + 1, C, CH, LANE), BF16),
        ((GROUPS + 2, C, CH, LANE), BF16),
        ((24, LANE), F32),
        ((24, LANE), F32),
        ((GROUPS, 2 * LANE, C * LANE), BF16),
        ((len(TGT_LANES), 8 * LANE, LANE), BF16),
        ((GROUPS + 1, LANE, LANE), BF16),
        ((2, C, 32, LANE), F32),
        ((2, C, 32, LANE), F32),
        ((S, 2, LANE), F32),
        ((S, 2, LANE), F32),
        ((2, LANE), F32),
        ((C, 2, LANE), F32),
    ]
    layer_out, loss = pl.pallas_call(
        body,
        out_shape=(
            jax.ShapeDtypeStruct((4, CH, 256), BF16),
            jax.ShapeDtypeStruct((1, LANE), F32),
        ),
        in_specs=[vmem] * 5 + [pl.BlockSpec(memory_space=pl.ANY)] + [vmem] * 6,
        out_specs=(vmem, vmem),
        scratch_shapes=[pltpu.VMEM(shape, kind) for shape, kind in scratch]
        + [pltpu.SemaphoreType.DMA((EXCHANGES,))] * 2
        + [pltpu.SemaphoreType.DMA(())],
        compiler_params=pltpu.CompilerParams(
            collective_id=0, has_side_effects=True, vmem_limit_bytes=60 * 1024 * 1024
        ),
        cost_estimate=pl.CostEstimate(
            flops=20_000_000_000, bytes_accessed=5_000_000, transcendentals=10_000
        ),
    )(
        signal.transpose(1, 2, 0),
        filter_taps.T,
        skip_gain.reshape(1, CH),
        w_gate.T,
        w_out,
        catalogue,
        item_draw_counts.reshape(1, ITEMS),
        sampled_pos.reshape(1, LANE),
        neg_owner.transpose(1, 2, 0),
        neg_row.T,
        target_owner.reshape(1, LANE),
        target_row.reshape(1, LANE),
    )
    return layer_out.transpose(2, 0, 1), loss.reshape(LANE)


def solution(mesh):
    placed = (
        P("seq", None, "ch"),
        P("seq", "ch"),
        P("ch"),
        P(None, "ch"),
        P("ch", None),
        P(("seq", "ch"), None),
        P(("seq", "ch")),
        P("seq"),
        P("seq", None, None),
        P("seq", None),
        P("seq", None),
        P("seq"),
    )
    return jax.shard_map(
        per_device,
        mesh=mesh,
        in_specs=placed,
        out_specs=(P("seq", None, "ch"), P("seq")),
        check_vma=False,
    )
```

```python
import jax
import jax.numpy as jnp
from jax import lax
from jax.experimental import pallas as pl
from jax.experimental.pallas import tpu as pltpu
from jax.sharding import PartitionSpec as P

SOFTMAX_TEMP = 0.02
EPSILON = 1e-06
MESH = pl.DeviceIdType.MESH
BF16 = jnp.bfloat16
F32 = jnp.float32
I32 = jnp.int32

S = 32
C = 8
LANE = 128
CH = 96
FULL = CH * C
TOK = 1024
NEG = 64
GROUPS = 16
SLOTS = (GROUPS + 1) * LANE
ITEMS = 2048

(
    X_CONV,
    X_REQ,
    X_BACK,
    X_QUERY,
    X_FORWARD,
    X_ACROSS,
    X_SUMS,
    X_SIG,
    X_WGATE,
    X_WOUT,
    X_WGATE_MATE,
    X_WOUT_MATE,
    X_TABLE,
    X_TABLE_Y,
    X_MIX,
    X_OUT,
    X_PART,
    X_PART_Y,
    X_FIN,
    X_ROWS,
) = range(20)
X_LAYER = X_ROWS + GROUPS // 2 + 2
CHUNKS = GROUPS // 2
HALF = GROUPS // 2
X_WAY = X_LAYER + 8
EXCHANGES = X_WAY + 8
SIDE = 4
TGT_LANES = (0, 16, 64, 80)
TGT_BLOCKS = tuple(tuple(range(first, first + 16, 2)) for first in (1, 17, 0, 16))


def iota(shape, dim):
    return lax.broadcasted_iota(I32, shape, dim)


def onehot(mask):
    return jnp.where(mask, 1.0, 0.0).astype(BF16)


def dot(a, b, ca=1, cb=0):
    return lax.dot_general(a, b, (((ca,), (cb,)), ((), ())), preferred_element_type=F32)


def split_parts(value, count):
    parts = []
    for _ in range(count):
        piece = value.astype(BF16)
        parts.append(piece)
        value = value - piece.astype(F32)
    return parts


def body(
    sig,
    taps_t,
    gain,
    wg_own,
    w_out,
    cat_hbm,
    cnt,
    spos,
    nown,
    nrow,
    town,
    trow,
    out_ref,
    loss_ref,
    cat,
    sig_send,
    sig_all,
    msgf,
    msg1,
    rcv1,
    rf,
    xpad,
    x4,
    acc,
    msg2,
    rcv2,
    wg_all,
    wo_all,
    wo_t,
    gate_t,
    mix_send,
    mix_all,
    lo_send,
    lo_all,
    q_own,
    q_stage,
    q_all,
    req_msg,
    req_all,
    ohs,
    inner,
    total,
    keys,
    vals,
    tab_own,
    tab_all,
    tab_t,
    cat_t,
    rows_send,
    rows_all,
    row_scale,
    row_log,
    ohp,
    oht,
    slot_pos,
    part,
    part_all,
    sums,
    sums_all,
    fin,
    fin_all,
    send_sem,
    recv_sem,
    cat_sem,
):
    me_s = lax.axis_index("seq")
    me_c = lax.axis_index("ch")
    me_z, me_y = me_s // SIDE, lax.rem(me_s, SIDE)
    me_x, core = me_c // 2, lax.rem(me_c, 2)
    me_v = me_y * 2 + core
    layers = S // SIDE

    def beside(y, x):
        return (me_z * SIDE + y, x * 2 + core)

    def split_peer(along_x, p):
        seq = jnp.where(along_x, me_s, me_z * SIDE + p // 2)
        return (seq, jnp.where(along_x, p, me_x * 2 + lax.rem(p, 2)))

    def copy_to(x, device, src, dst, x_recv=None):
        return pltpu.make_async_remote_copy(
            src_ref=src,
            dst_ref=dst,
            send_sem=send_sem.at[x],
            recv_sem=recv_sem.at[x if x_recv is None else x_recv],
            device_id=device,
            device_id_type=MESH,
        )

    def arrived(x, like):
        copy_to(x, (me_s, me_c), like, like).wait_recv()

    def sent(x, like):
        copy_to(x, (me_s, me_c), like, like).wait_send()

    def over(n, me, fn):
        def step(d, carry):
            fn(lax.rem(me + d, n))
            return carry

        lax.fori_loop(1, n, step, 0, unroll=n - 1 if n == C else 4)

    def start_seq(x, src_of, dst):
        over(S, me_s, lambda p: copy_to(x, (p, me_c), src_of(p), dst.at[me_s]).start())

    def start_ch(x, src_of, dst):
        over(C, me_c, lambda p: copy_to(x, (me_s, p), src_of(p), dst.at[me_c]).start())

    def wait_seq(x, dst):
        arrived(x, dst.at[pl.ds(0, S - 1)])

    def wait_ch(x, dst):
        arrived(x, dst.at[pl.ds(0, C - 1)])

    def sent_seq(x, dst):
        sent(x, dst.at[pl.ds(0, S - 1)])

    def sent_ch(x, dst):
        sent(x, dst.at[pl.ds(0, C - 1)])

    barrier = pltpu.get_barrier_semaphore()

    def greet_seq(peer):
        pl.semaphore_signal(barrier, inc=1, device_id=(peer, me_c), device_id_type=MESH)

    def greet_ch(peer):
        pl.semaphore_signal(barrier, inc=1, device_id=(me_s, peer), device_id_type=MESH)

    over(S, me_s, greet_seq)
    over(C, me_c, greet_ch)
    for y in range(SIDE):

        @pl.when(me_y != y)
        def _():
            other = (me_z * SIDE + y, me_x * 2 + 1 - core)
            pl.semaphore_signal(barrier, inc=1, device_id=other, device_id_type=MESH)

        @pl.when((me_y != y) | (me_x != me_y))
        def _():
            pl.semaphore_signal(barrier, inc=1, device_id=beside(y, me_y), device_id_type=MESH)

    on_diagonal = me_x == me_y

    cat_copy = pltpu.make_async_copy(cat_hbm, cat, cat_sem)
    cat_copy.start()

    for q in range(8):
        piece = sig[q % 4, :, (q // 4) * LANE : (q // 4 + 1) * LANE]
        sig_send[q] = piece
        for k in range(3):
            msgf[pl.ds(k * 8 + q, S, stride=32), :] = piece[k * 32 : (k + 1) * 32].astype(F32)
    for il in range(2):
        for k in range(3):
            msgf[pl.ds(24 + 2 * k + il, S, stride=32), :] = taps_t[
                k * 32 : (k + 1) * 32, il * LANE : (il + 1) * LANE
            ]
    for row in range(30, 32):
        msgf[pl.ds(row, S, stride=32), :] = jnp.zeros((S, LANE), F32)
    msg1[...] = msgf[...].reshape(S, 32, LANE).astype(BF16)

    extra = SIDE - 1 + SIDE - jnp.where(on_diagonal, 1, 0)
    pl.semaphore_wait(barrier, S - 1 + C - 1 + extra)

    start_seq(X_CONV, lambda p: msg1.at[p], rcv1)
    rcv1[me_s] = msg1[me_s]
    start_ch(X_SIG, lambda p: sig_send.at[p], sig_all)
    sig_all[me_c] = sig_send[me_c]

    mate = me_c + 1 - 2 * core

    def over_x(fn):
        def step(d, carry):
            fn(lax.rem(me_c + 2 * d, C))
            return carry

        lax.fori_loop(1, SIDE, step, 0)

    def start_weight(x, x_mate, src, dst):
        over_x(lambda p: copy_to(x, (me_s, p), src, dst.at[me_c]).start())
        copy_to(x, (me_s, mate), src, dst.at[me_c], x_mate).start()
        dst[me_c] = src[...]

    def pass_weight(x, x_mate, dst):
        arrived(x, dst.at[pl.ds(0, SIDE - 1)])
        over_x(lambda p: copy_to(x_mate, (me_s, mate), dst.at[p], dst.at[p]).start())

    def wait_weight(x_mate, dst):
        arrived(x_mate, dst.at[pl.ds(0, SIDE)])

    def sent_weight(x, x_mate, dst):
        sent(x, dst.at[pl.ds(0, SIDE)])
        sent(x_mate, dst.at[pl.ds(0, SIDE - 1)])

    start_weight(X_WGATE, X_WGATE_MATE, wg_own, wg_all)
    start_weight(X_WOUT, X_WOUT_MATE, w_out, wo_all)

    upper = onehot(iota((LANE, LANE), 0) < iota((LANE, LANE), 1))
    ones = jnp.ones((LANE, LANE), BF16)
    owner_ids = iota((S, LANE), 0)

    def own_onehot(owners):
        mine = jnp.where((owners & 7) == me_c, owners >> 3, -1)
        return jnp.where(owner_ids == mine, 1.0, 0.0)

    def mark(m, carry):
        ohs[pl.ds(pl.multiple_of(m * S, S), S), :] = own_onehot(nown[m]).astype(BF16)
        return carry

    lax.fori_loop(0, 64, mark, 0, unroll=4)
    inner[...] = dot(ohs[...], upper)
    total[...] = dot(ohs[...], ones)
    key_ids = iota((LANE, LANE), 0).astype(F32)
    lane_row = iota((1, LANE), 1)

    def key_of(hot, rank, offset):
        found = jnp.sum(hot * (rank + 1.0), axis=0, keepdims=True)
        place = jnp.where(found > 0.5, found - 1.0 + offset, -1.0)
        return jnp.where(key_ids == place, 1.0, 0.0).astype(BF16)

    def value_of(hot, rows):
        high = (rows >> 8).astype(F32)
        low = (rows & 255).astype(F32)
        pieces = [hot * high, hot * low, hot * lane_row.astype(F32), hot]
        return jnp.concatenate(pieces, axis=0).astype(BF16)

    odd = lax.rem(me_s, 2)
    neg_offset = (odd * NEG).astype(F32)
    tgt_offset = ((1 - odd) * NEG + me_s - odd).astype(F32)

    def place(m, before):
        rows = pl.ds(pl.multiple_of(m * S, S), S)
        lanes = pl.ds(pl.multiple_of(m * LANE, LANE), LANE)
        hot = ohs[rows, :].astype(F32)
        keys[:, lanes] = key_of(hot, inner[rows, :] + before, neg_offset)
        vals[:, lanes] = value_of(hot, nrow[pl.ds(m, 1), :])
        return before + total[rows, :]

    lax.fori_loop(0, 64, place, jnp.zeros((S, LANE), F32), unroll=4)
    hot = own_onehot(town[...])
    rank = dot(hot.astype(BF16), upper)
    found = dot(vals[...], keys[...], 1, 1) + dot(
        value_of(hot, trow[...]), key_of(hot, rank, tgt_offset), 1, 1
    )
    high, low, pos, filled = (found[i * S : (i + 1) * S].astype(I32) for i in range(4))
    entry = (high * 256 + low) * LANE + pos
    req_msg[:, 0, :] = jnp.where(filled > 0, entry, -1)
    start_seq(X_REQ, lambda p: req_msg.at[p], req_all)
    req_all[me_s] = req_msg[me_s]

    wait_seq(X_CONV, rcv1)
    rf[...] = rcv1[...].astype(F32)
    xpad[0:16, :] = jnp.zeros((16, LANE), F32)
    later = iota((LANE, LANE), 1) >= iota((LANE, LANE), 0)
    for k in range(3):
        xpad[16:272, :] = rf[:, k * 8 : (k + 1) * 8, :].reshape(256, LANE)
        x4[...] = jnp.concatenate(
            [xpad[16 - 4 * j : 272 - 4 * j, :] for j in range(4)], axis=1
        ).astype(BF16)
        acc[...] = jnp.zeros_like(acc)
        prev = jnp.zeros((LANE, LANE), F32)
        for e in range(16):
            tiles = []
            for j in range(4):
                d = 4 * e + j
                row = 24 + 2 * k + d % 2
                chunk = jnp.broadcast_to(rf[d // 2, row : row + 1, :], (LANE, LANE))
                turned = pltpu.roll(chunk, 0, 1, stride=1, stride_axis=0)
                tiles.append(jnp.where(later, turned, prev).astype(BF16))
                prev = turned
            taps_tile = jnp.concatenate(tiles, axis=0)
            acc[16 * e :, :] += dot(x4[0 : 256 - 16 * e, :], taps_tile)
        for s in range(S):
            msgf[s * 32 + k * 8 : s * 32 + k * 8 + 8, :] = acc[s * 8 : s * 8 + 8, :]
    msg2[...] = msgf[...].reshape(S, 32, LANE).astype(BF16)
    start_seq(X_BACK, lambda p: msg2.at[p], rcv2)
    rcv2[me_s] = msg2[me_s]

    wait_seq(X_REQ, req_all)
    asked = req_all[:, 0, :]
    asked = asked.reshape(GROUPS, 2, LANE)
    even_half, odd_half = asked[:, 0, :], asked[:, 1, :]
    first_half = iota((GROUPS, LANE), 1) < NEG
    tab_own[...] = jnp.full(tab_own.shape, -1, I32)
    tab_own[0:GROUPS, :] = jnp.where(first_half, even_half, odd_half)
    tab_own[GROUPS : GROUPS + 1, :] = jnp.max(
        jnp.where(first_half, odd_half, even_half), axis=0, keepdims=True
    )
    start_ch(X_TABLE, lambda p: tab_own, tab_all.at[0])
    tab_all[0, me_c] = tab_own[...]

    def table_along_y(p):
        copy_to(X_TABLE_Y, split_peer(False, p), tab_own, tab_all.at[1, me_v]).start()

    over(C, me_v, table_along_y)
    tab_all[1, me_v] = tab_own[...]
    cat_copy.wait()

    def turn(i, carry):
        span = pl.ds(pl.multiple_of(i * 256, 256), 256)
        cat_t[0:FULL, span] = cat[span, :].T
        return carry

    lax.fori_loop(0, ITEMS // 256, turn, 0)
    cat_t[FULL : FULL + 16, :] = jnp.broadcast_to(cnt[...].astype(F32), (16, ITEMS)).astype(BF16)

    row_scale[...] = jnp.zeros_like(row_scale)
    row_log[...] = jnp.zeros_like(row_log)
    item_ids = iota((ITEMS, LANE), 0)

    def picked(group):
        return onehot(item_ids == (tab_own[pl.ds(group, 1), :] >> 7))

    def keep(found, width, group0):
        for i in range(width // LANE):
            lanes = slice(i * LANE, (i + 1) * LANE)
            for c in range(C):
                rows_send[group0 + i, c] = found[c * CH : (c + 1) * CH, lanes].astype(BF16)
            if width > LANE:
                mine = jnp.where(group0 < HALF, me_c, me_v)
                rows_all[group0 + i, mine] = rows_send[group0 + i, mine]
        square = jnp.sum(found[0:FULL] * found[0:FULL], axis=0, keepdims=True)
        scale = lax.rsqrt(square / FULL + EPSILON) / (FULL * SOFTMAX_TEMP)
        logs = jnp.log(jnp.maximum(found[FULL : FULL + 1], 1.0))
        for i in range(width // LANE):
            row_scale[pl.ds(group0 + i, 1), :] = scale[:, i * LANE : (i + 1) * LANE]
            row_log[pl.ds(group0 + i, 1), :] = logs[:, i * LANE : (i + 1) * LANE]

    def send_rows(x, span, to, along_x):
        mine = jnp.where(along_x, me_c, me_v)

        def fn(p):
            src, dst = rows_send.at[span, p], rows_all.at[to, mine]
            copy_to(x, split_peer(along_x, p), src, dst).start()

        over(C, mine, fn)

    def chunk_at(i):
        return jnp.where(i == 0, 0, jnp.where(i == 1, 1, jnp.where(i == 2, 4, jnp.where(i == 3, 5, jnp.where(i == 4, 6, jnp.where(i == 5, 7, jnp.where(i == 6, 2, 3)))))))

    def send_chunk(h):
        send_rows(X_ROWS + h, pl.ds(2 * h, 2), pl.ds(2 * h, 2), h < CHUNKS // 2)

    def fetch(first, last):
        def step(i, carry):
            h = chunk_at(i)
            hot = jnp.concatenate([picked(2 * h), picked(2 * h + 1)], axis=1)
            keep(dot(cat_t[...], hot), 256, 2 * h)

            @pl.when((h != 1) & (h != 2) & (h != 3))
            def _():
                send_chunk(h)

            return carry

        lax.fori_loop(first, last, step, 0)

    def fetch_targets():
        keep(dot(cat_t[...], picked(GROUPS)), LANE, GROUPS)
        rows_all[GROUPS, me_c] = rows_send[GROUPS, me_c]
        rows_all[GROUPS + 1, me_v] = rows_send[GROUPS, me_v]
        send_rows(X_ROWS + CHUNKS, GROUPS, GROUPS, True)
        send_rows(X_ROWS + CHUNKS + 1, GROUPS, GROUPS + 1, False)

    def each_chunk(fn):
        def step(h, carry):
            fn(X_ROWS + h, rows_all.at[pl.ds(2 * h, 2), pl.ds(0, C - 1)])
            return carry

        lax.fori_loop(0, CHUNKS, step, 0)
        for i in range(2):
            fn(X_ROWS + CHUNKS + i, rows_all.at[GROUPS + i, pl.ds(0, C - 1)])

    fetch(0, 5)
    pass_weight(X_WGATE, X_WGATE_MATE, wg_all)
    wait_ch(X_SIG, sig_all)

    wait_seq(X_BACK, rcv2)
    rf[...] = rcv2[...].astype(F32)
    msgf[...] = rf[...].reshape(S * 32, LANE)
    diag = iota((CH, CH), 0) == iota((CH, CH), 1)
    gain_col = jnp.sum(jnp.where(diag, gain[...], 0.0), axis=1, keepdims=True)
    for q in range(8):
        conv = jnp.concatenate(
            [msgf[pl.ds(k * 8 + q, S, stride=32), :] for k in range(3)], axis=0
        )
        mix_send[q] = (conv + gain_col * sig_send[q].astype(F32)).astype(BF16)
    start_ch(X_MIX, lambda p: mix_send.at[p], mix_all)
    mix_all[me_c] = mix_send[me_c]
    send_chunk(1)
    pass_weight(X_WOUT, X_WOUT_MATE, wo_all)

    wait_weight(X_WGATE_MATE, wg_all)
    gate_t[...] = dot(wg_all[...].reshape(FULL, FULL), sig_all[...].reshape(FULL, LANE))
    fetch(5, 8)
    wait_weight(X_WOUT_MATE, wo_all)
    wo_t[...] = wo_all[...].reshape(FULL, FULL).T
    wait_ch(X_MIX, mix_all)
    mix = mix_all[...].reshape(FULL, LANE).astype(F32) * gate_t[...]
    lo_send[...] = dot(wo_t[...], mix.astype(BF16)).astype(BF16).reshape(C, CH, LANE)
    start_ch(X_OUT, lambda p: lo_send.at[p], lo_all)
    lo_all[me_c] = lo_send[me_c]
    send_chunk(2)
    send_chunk(3)

    fetch_targets()

    wait_ch(X_TABLE, tab_all.at[0])
    wait_ch(X_TABLE_Y, tab_all.at[1])
    pair_ids = iota((2 * LANE, LANE), 0)

    def slots(g, carry):
        for c in range(C):
            entry = tab_all[g // HALF, c, pl.ds(g, 1), :]
            target = jnp.where(entry < 0, -1, (entry & 127) + jnp.where(lane_row < NEG, 0, LANE))
            ohp[g, :, c * LANE : (c + 1) * LANE] = onehot(pair_ids == target)
        return carry

    lax.fori_loop(0, GROUPS, slots, 0)
    wide_ids = iota((8 * LANE, LANE), 0)
    part_of = lane_row >> 4
    for o, lane0 in enumerate(TGT_LANES):
        entry = jnp.full((1, LANE), -1, I32)
        for c in range(C):
            listed = tab_all[o % 2, c, GROUPS : GROUPS + 1, :]
            turned = pltpu.roll(listed, (16 * c - lane0) % LANE, 1)
            entry = jnp.where(part_of == c, turned, entry)
        target = jnp.where(entry < 0, -1, ((lane_row & 15) >> 1) * LANE + (entry & 127))
        oht[o] = onehot(wide_ids == target)
    tab_t[...] = jnp.full(tab_t.shape, -1.0, F32)
    tab_t[0:24, :] = jnp.where(tab_own[...] < 0, -1, tab_own[...] & 127).astype(F32)
    columns = tab_t[...].T
    pos_ids = iota((LANE, LANE), 1).astype(F32)
    for g in range(GROUPS + 1):
        slot_pos[g] = onehot(columns[:, g : g + 1] == pos_ids)

    tok_pos = spos[...]
    pos_in = tok_pos >> 2
    where_in = ((pos_in >> 7) * 4 + (tok_pos & 3)) * LANE + (pos_in & 127)
    pick = onehot(iota((TOK, LANE), 0) == where_in)

    wait_ch(X_OUT, lo_all)
    lo_t = jnp.concatenate([lo_all[q] for q in range(8)], axis=1)
    q_own[...] = dot(lo_t, pick).astype(BF16)

    def layer_at(i):
        near = (i + 1) // 2
        return lax.rem(me_z + jnp.where(lax.rem(i, 2) == 1, near, layers - near), layers)

    def along_z(fn):
        def step(i, carry):
            fn(layer_at(i))
            return carry

        lax.fori_loop(1, layers, step, 0)

    def go_on(z):
        block = z * SIDE + me_y
        first = z < layers // 2
        src = q_stage.at[z]

        def step(j, carry):
            y = jnp.where(first, j, me_x)
            x = jnp.where(first, me_x, j)
            here = (y == me_y) & (x == me_x)

            @pl.when(jnp.logical_not(here))
            def _():
                way = jnp.where(first, X_FORWARD, X_ACROSS)
                copy_to(way, beside(y, x), src, q_all.at[block], X_WAY + z).start()

            @pl.when(here)
            def _():
                q_all[block] = q_stage[z]

            return carry

        lax.fori_loop(0, SIDE, step, 0)

    q_stage[me_z] = q_own[...]
    along_z(
        lambda z: copy_to(
            X_QUERY, (z * SIDE + me_y, me_c), q_own, q_stage.at[me_z], X_LAYER + me_z
        ).start()
    )
    go_on(me_z)
    for q in range(8):
        out_ref[q % 4, :, (q // 4) * LANE : (q // 4 + 1) * LANE] = lo_all[q]

    def take_layer(z):
        arrived(X_LAYER + z, q_own)
        go_on(z)

    along_z(take_layer)

    def take_blocks(z):
        three = (z < layers // 2) | on_diagonal

        @pl.when(three)
        def _():
            arrived(X_WAY + z, q_all.at[pl.ds(0, SIDE - 1)])

        @pl.when(jnp.logical_not(three))
        def _():
            arrived(X_WAY + z, q_all.at[pl.ds(0, SIDE)])

    part[...] = jnp.zeros_like(part)

    def pair(g, carry):
        both = jnp.concatenate([q_all[2 * g], q_all[2 * g + 1]], axis=1)
        query = dot(both, ohp[g])
        for c in range(C):
            one = query[:, c * LANE : (c + 1) * LANE]
            rows = rows_all[g, c].astype(F32)
            place = pl.ds(lax.rem(g, HALF), 1)
            square_place = pl.ds(16 + lax.rem(g, HALF), 1)
            part[g // HALF, c, place, :] = jnp.sum(one * rows, axis=0, keepdims=True)
            part[g // HALF, c, square_place, :] = jnp.sum(one * one, axis=0, keepdims=True)
        return carry

    def take_rows(h, like):
        arrived(X_ROWS + h, like)

    def layer(i, carry):
        z = layer_at(i)
        take_rows(z, rows_all.at[pl.ds(2 * z, 2), pl.ds(0, C - 1)])
        take_blocks(z)
        pair(2 * z, 0)
        pair(2 * z + 1, 0)
        return carry

    lax.fori_loop(0, layers, layer, 0)
    for i in range(2):
        take_rows(CHUNKS + i, rows_all.at[GROUPS + i, pl.ds(0, C - 1)])
    tgt_rows = []
    for o, lane0 in enumerate(TGT_LANES):
        rows = jnp.zeros((CH, LANE), F32)
        for c in range(C):
            there = rows_all[GROUPS + o % 2, c].astype(F32)
            turned = pltpu.roll(there, (16 * c - lane0) % LANE, 1)
            rows = jnp.where(part_of == c, turned, rows)
        tgt_rows.append(rows)
    tgt_part = [[[jnp.zeros((1, LANE), F32)] * 2 for _ in range(C)] for _ in range(2)]
    for o, lane0 in enumerate(TGT_LANES):
        wide = jnp.concatenate([q_all[b] for b in TGT_BLOCKS[o]], axis=1)
        one = dot(wide, oht[o])
        for i, rows in enumerate((tgt_rows[o], one)):
            both = jnp.sum(one * rows, axis=0, keepdims=True)
            for c in range(C):
                turned = pltpu.roll(both, (lane0 - 16 * c) % LANE, 1)
                ours = (lane_row >= lane0) & (lane_row < lane0 + 16)
                tgt_part[o % 2][c][i] = jnp.where(ours, turned, tgt_part[o % 2][c][i])
    for way in range(2):
        for c in range(C):
            part[way, c, HALF : HALF + 1, :] = tgt_part[way][c][0]
            part[way, c, 16 + HALF : 17 + HALF, :] = tgt_part[way][c][1]
    start_ch(X_PART, lambda p: part.at[0, p], part_all.at[0])
    part_all[0, me_c] = part[0, me_c]

    def part_along_y(p):
        copy_to(X_PART_Y, split_peer(False, p), part.at[1, p], part_all.at[1, me_v]).start()

    over(C, me_v, part_along_y)
    part_all[1, me_v] = part[1, me_v]
    wait_ch(X_PART, part_all.at[0])
    wait_ch(X_PART_Y, part_all.at[1])
    by_x, by_y = jnp.sum(part_all[0], axis=0), jnp.sum(part_all[1], axis=0)
    whole = jnp.concatenate(
        [
            piece
            for i in (0, 16)
            for piece in (by_x[i : i + 8], by_y[i : i + 8], by_x[i + 8 : i + 16] + by_y[i + 8 : i + 16])
        ],
        axis=0,
    )
    query_scale = lax.rsqrt(whole[24:48] / FULL + EPSILON)
    logit = whole[0:24] * query_scale * row_scale[...] - row_log[...]
    filled = tab_own[...] >= 0
    exp_neg = jnp.where(filled, jnp.exp(logit), 0.0)[0:GROUPS]
    halves = [jnp.where(first_half, exp_neg, 0.0), jnp.where(first_half, 0.0, exp_neg)]
    exp_parts = jnp.concatenate([p for half in halves for p in split_parts(half, 2)], axis=0)
    tgt_logit = jnp.where(filled, logit, 0.0)[GROUPS : GROUPS + 1]
    block_of = 2 * ((lane_row & 63) >> 1) + jnp.where(lane_row < NEG, 1, 0)
    by_block = jnp.where(iota((S, LANE), 0) == block_of, tgt_logit, 0.0)
    tgt_parts = jnp.concatenate(split_parts(by_block, 3), axis=0)
    targets = dot(tgt_parts, slot_pos[GROUPS])
    targets = targets[0:S] + targets[S : 2 * S] + targets[2 * S : 3 * S]
    sums[:, 1, :] = targets
    for g in range(GROUPS):
        found = dot(exp_parts, slot_pos[g])
        sums[2 * g, 0:1, :] = found[g : g + 1] + found[16 + g : 17 + g]
        sums[2 * g + 1, 0:1, :] = found[32 + g : 33 + g] + found[48 + g : 49 + g]
    start_seq(X_SUMS, lambda p: sums.at[p], sums_all)
    sums_all[me_s] = sums[me_s]
    wait_seq(X_SUMS, sums_all)
    fin[...] = jnp.sum(sums_all[...], axis=0)
    start_ch(X_FIN, lambda p: fin, fin_all)
    fin_all[me_c] = fin[...]
    wait_ch(X_FIN, fin_all)
    last = jnp.sum(fin_all[...], axis=0)
    target_logit = last[1:2]
    loss_ref[...] = jnp.log(jnp.exp(target_logit) + last[0:1]) - target_logit

    sent_seq(X_CONV, rcv1)
    sent_seq(X_REQ, req_all)
    sent_seq(X_BACK, rcv2)
    sent(X_QUERY, q_all.at[pl.ds(0, layers - 1)])
    sent(X_FORWARD, q_all.at[pl.ds(0, 12)])

    @pl.when(on_diagonal)
    def _():
        sent(X_ACROSS, q_all.at[pl.ds(0, 12)])

    @pl.when(jnp.logical_not(on_diagonal))
    def _():
        sent(X_ACROSS, q_all.at[pl.ds(0, 16)])

    sent_seq(X_SUMS, sums_all)
    sent_ch(X_SIG, sig_all)
    sent_weight(X_WGATE, X_WGATE_MATE, wg_all)
    sent_weight(X_WOUT, X_WOUT_MATE, wo_all)
    sent_ch(X_TABLE, tab_all.at[0])
    sent_ch(X_TABLE_Y, tab_all.at[1])
    each_chunk(sent)
    sent_ch(X_MIX, mix_all)
    sent_ch(X_OUT, lo_all)
    sent_ch(X_PART, part_all.at[0])
    sent_ch(X_PART_Y, part_all.at[1])
    sent_ch(X_FIN, fin_all)


def per_device(
    signal,
    filter_taps,
    skip_gain,
    w_gate,
    w_out,
    catalogue,
    item_draw_counts,
    sampled_pos,
    neg_owner,
    neg_row,
    target_owner,
    target_row,
):
    vmem = pl.BlockSpec(memory_space=pltpu.VMEM)
    scratch = [
        ((ITEMS, FULL), BF16),
        ((C, CH, LANE), BF16),
        ((C, CH, LANE), BF16),
        ((S * 32, LANE), F32),
        ((S, 32, LANE), BF16),
        ((S, 32, LANE), BF16),
        ((S, 32, LANE), F32),
        ((272, LANE), F32),
        ((256, 512), BF16),
        ((256, LANE), F32),
        ((S, 32, LANE), BF16),
        ((S, 32, LANE), BF16),
        ((C, CH, FULL), BF16),
        ((C, CH, FULL), BF16),
        ((FULL, FULL), BF16),
        ((FULL, LANE), F32),
        ((C, CH, LANE), BF16),
        ((C, CH, LANE), BF16),
        ((C, CH, LANE), BF16),
        ((C, CH, LANE), BF16),
        ((CH, LANE), BF16),
        ((S // SIDE, CH, LANE), BF16),
        ((S, CH, LANE), BF16),
        ((S, 1, LANE), I32),
        ((S, 1, LANE), I32),
        ((64 * S, LANE), BF16),
        ((64 * S, LANE), F32),
        ((64 * S, LANE), F32),
        ((LANE, 64 * LANE), BF16),
        ((LANE, 64 * LANE), BF16),
        ((24, LANE), I32),
        ((2, C, 24, LANE), I32),
        ((LANE, LANE), F32),
        ((FULL + 16, ITEMS), BF16),
        ((GROUPS + 1, C, CH, LANE), BF16),
        ((GROUPS + 2, C, CH, LANE), BF16),
        ((24, LANE), F32),
        ((24, LANE), F32),
        ((GROUPS, 2 * LANE, C * LANE), BF16),
        ((len(TGT_LANES), 8 * LANE, LANE), BF16),
        ((GROUPS + 1, LANE, LANE), BF16),
        ((2, C, 32, LANE), F32),
        ((2, C, 32, LANE), F32),
        ((S, 2, LANE), F32),
        ((S, 2, LANE), F32),
        ((2, LANE), F32),
        ((C, 2, LANE), F32),
    ]
    layer_out, loss = pl.pallas_call(
        body,
        out_shape=(
            jax.ShapeDtypeStruct((4, CH, 256), BF16),
            jax.ShapeDtypeStruct((1, LANE), F32),
        ),
        in_specs=[vmem] * 5 + [pl.BlockSpec(memory_space=pl.ANY)] + [vmem] * 6,
        out_specs=(vmem, vmem),
        scratch_shapes=[pltpu.VMEM(shape, kind) for shape, kind in scratch]
        + [pltpu.SemaphoreType.DMA((EXCHANGES,))] * 2
        + [pltpu.SemaphoreType.DMA(())],
        compiler_params=pltpu.CompilerParams(
            collective_id=0, has_side_effects=True, vmem_limit_bytes=60 * 1024 * 1024
        ),
        cost_estimate=pl.CostEstimate(
            flops=20_000_000_000, bytes_accessed=5_000_000, transcendentals=10_000
        ),
    )(
        signal.transpose(1, 2, 0),
        filter_taps.T,
        skip_gain.reshape(1, CH),
        w_gate.T,
        w_out,
        catalogue,
        item_draw_counts.reshape(1, ITEMS),
        sampled_pos.reshape(1, LANE),
        neg_owner.transpose(1, 2, 0),
        neg_row.T,
        target_owner.reshape(1, LANE),
        target_row.reshape(1, LANE),
    )
    return layer_out.transpose(2, 0, 1), loss.reshape(LANE)


def solution(mesh):
    placed = (
        P("seq", None, "ch"),
        P("seq", "ch"),
        P("ch"),
        P(None, "ch"),
        P("ch", None),
        P(("seq", "ch"), None),
        P(("seq", "ch")),
        P("seq"),
        P("seq", None, None),
        P("seq", None),
        P("seq", None),
        P("seq"),
    )
    return jax.shard_map(
        per_device,
        mesh=mesh,
        in_specs=placed,
        out_specs=(P("seq", None, "ch"), P("seq")),
        check_vma=False,
    )
```

```python
import jax
import jax.numpy as jnp
from jax import lax
from jax.experimental import pallas as pl
from jax.experimental.pallas import tpu as pltpu
from jax.sharding import PartitionSpec as P

SOFTMAX_TEMP = 0.02
EPSILON = 1e-06
MESH = pl.DeviceIdType.MESH
BF16 = jnp.bfloat16
F32 = jnp.float32
I32 = jnp.int32

S = 32
C = 8
LANE = 128
CH = 96
FULL = CH * C
TOK = 1024
NEG = 64
GROUPS = 16
SLOTS = (GROUPS + 1) * LANE
ITEMS = 2048

(
    X_CONV,
    X_REQ,
    X_BACK,
    X_QUERY,
    X_FORWARD,
    X_ACROSS,
    X_SUMS,
    X_SIG,
    X_WGATE,
    X_WOUT,
    X_WGATE_MATE,
    X_WOUT_MATE,
    X_TABLE,
    X_TABLE_Y,
    X_MIX,
    X_OUT,
    X_PART,
    X_PART_Y,
    X_FIN,
    X_ROWS,
) = range(20)
X_LAYER = X_ROWS + GROUPS // 2 + 2
CHUNKS = GROUPS // 2
HALF = GROUPS // 2
X_WAY = X_LAYER + 8
EXCHANGES = X_WAY + 8
SIDE = 4
TGT_LANES = (0, 16, 64, 80)
TGT_BLOCKS = tuple(tuple(range(first, first + 16, 2)) for first in (1, 17, 0, 16))


def iota(shape, dim):
    return lax.broadcasted_iota(I32, shape, dim)


def onehot(mask):
    return jnp.where(mask, 1.0, 0.0).astype(BF16)


def dot(a, b, ca=1, cb=0):
    return lax.dot_general(a, b, (((ca,), (cb,)), ((), ())), preferred_element_type=F32)


def split_parts(value, count):
    parts = []
    for _ in range(count):
        piece = value.astype(BF16)
        parts.append(piece)
        value = value - piece.astype(F32)
    return parts


def body(
    sig_hbm,
    taps_t_hbm,
    gain_hbm,
    wg_own_hbm,
    w_out_hbm,
    cat_hbm,
    cnt_hbm,
    spos_hbm,
    nown_hbm,
    nrow_hbm,
    town_hbm,
    trow_hbm,
    out_ref,
    loss_ref,
    sig,
    taps_t,
    gain,
    wg_own,
    w_out,
    cat,
    cnt,
    spos,
    nown,
    nrow,
    town,
    trow,
    sig_send,
    sig_all,
    msgf,
    msg1,
    rcv1,
    rf,
    xpad,
    x4,
    acc,
    msg2,
    rcv2,
    wg_all,
    wo_all,
    wo_t,
    gate_t,
    mix_send,
    mix_all,
    lo_send,
    lo_all,
    q_own,
    q_stage,
    q_all,
    req_msg,
    req_all,
    ohs,
    inner,
    total,
    keys,
    vals,
    tab_own,
    tab_all,
    tab_t,
    cat_t,
    rows_send,
    rows_all,
    row_scale,
    row_log,
    ohp,
    oht,
    slot_pos,
    part,
    part_all,
    sums,
    sums_all,
    fin,
    fin_all,
    send_sem,
    recv_sem,
    load_sem,
):
    me_s = lax.axis_index("seq")
    me_c = lax.axis_index("ch")
    me_z, me_y = me_s // SIDE, lax.rem(me_s, SIDE)
    me_x, core = me_c // 2, lax.rem(me_c, 2)
    me_v = me_y * 2 + core
    layers = S // SIDE

    def beside(y, x):
        return (me_z * SIDE + y, x * 2 + core)

    def split_peer(along_x, p):
        seq = jnp.where(along_x, me_s, me_z * SIDE + p // 2)
        return (seq, jnp.where(along_x, p, me_x * 2 + lax.rem(p, 2)))

    def copy_to(x, device, src, dst, x_recv=None):
        return pltpu.make_async_remote_copy(
            src_ref=src,
            dst_ref=dst,
            send_sem=send_sem.at[x],
            recv_sem=recv_sem.at[x if x_recv is None else x_recv],
            device_id=device,
            device_id_type=MESH,
        )

    def arrived(x, like):
        copy_to(x, (me_s, me_c), like, like).wait_recv()

    def sent(x, like):
        copy_to(x, (me_s, me_c), like, like).wait_send()

    def over(n, me, fn):
        def step(d, carry):
            fn(lax.rem(me + d, n))
            return carry

        lax.fori_loop(1, n, step, 0, unroll=n - 1 if n == C else 4)

    def start_seq(x, src_of, dst):
        over(S, me_s, lambda p: copy_to(x, (p, me_c), src_of(p), dst.at[me_s]).start())

    def start_ch(x, src_of, dst):
        over(C, me_c, lambda p: copy_to(x, (me_s, p), src_of(p), dst.at[me_c]).start())

    def wait_seq(x, dst):
        arrived(x, dst.at[pl.ds(0, S - 1)])

    def wait_ch(x, dst):
        arrived(x, dst.at[pl.ds(0, C - 1)])

    def sent_seq(x, dst):
        sent(x, dst.at[pl.ds(0, S - 1)])

    def sent_ch(x, dst):
        sent(x, dst.at[pl.ds(0, C - 1)])

    barrier = pltpu.get_barrier_semaphore()

    def greet_seq(peer):
        pl.semaphore_signal(barrier, inc=1, device_id=(peer, me_c), device_id_type=MESH)

    def greet_ch(peer):
        pl.semaphore_signal(barrier, inc=1, device_id=(me_s, peer), device_id_type=MESH)

    over(S, me_s, greet_seq)
    over(C, me_c, greet_ch)
    for y in range(SIDE):

        @pl.when(me_y != y)
        def _():
            other = (me_z * SIDE + y, me_x * 2 + 1 - core)
            pl.semaphore_signal(barrier, inc=1, device_id=other, device_id_type=MESH)

        @pl.when((me_y != y) | (me_x != me_y))
        def _():
            pl.semaphore_signal(barrier, inc=1, device_id=beside(y, me_y), device_id_type=MESH)

    on_diagonal = me_x == me_y

    far = (sig_hbm, taps_t_hbm, gain_hbm, wg_own_hbm, w_out_hbm, cat_hbm, cnt_hbm, spos_hbm, nown_hbm, nrow_hbm, town_hbm, trow_hbm)
    near = (sig, taps_t, gain, wg_own, w_out, cat, cnt, spos, nown, nrow, town, trow)
    loads = [
        pltpu.make_async_copy(src, dst, load_sem.at[i])
        for i, (src, dst) in enumerate(zip(far, near))
    ]
    for load in loads:
        load.start()
    for i in (0, 1):
        loads[i].wait()

    for q in range(8):
        piece = sig[q % 4, :, (q // 4) * LANE : (q // 4 + 1) * LANE]
        sig_send[q] = piece
        for k in range(3):
            msgf[pl.ds(k * 8 + q, S, stride=32), :] = piece[k * 32 : (k + 1) * 32].astype(F32)
    for il in range(2):
        for k in range(3):
            msgf[pl.ds(24 + 2 * k + il, S, stride=32), :] = taps_t[
                k * 32 : (k + 1) * 32, il * LANE : (il + 1) * LANE
            ]
    for row in range(30, 32):
        msgf[pl.ds(row, S, stride=32), :] = jnp.zeros((S, LANE), F32)
    msg1[...] = msgf[...].reshape(S, 32, LANE).astype(BF16)

    extra = SIDE - 1 + SIDE - jnp.where(on_diagonal, 1, 0)
    pl.semaphore_wait(barrier, S - 1 + C - 1 + extra)

    for i in (2, 3, 4, 6, 7, 8, 9, 10, 11):
        loads[i].wait()
    start_seq(X_CONV, lambda p: msg1.at[p], rcv1)
    rcv1[me_s] = msg1[me_s]
    start_ch(X_SIG, lambda p: sig_send.at[p], sig_all)
    sig_all[me_c] = sig_send[me_c]

    mate = me_c + 1 - 2 * core

    def over_x(fn):
        def step(d, carry):
            fn(lax.rem(me_c + 2 * d, C))
            return carry

        lax.fori_loop(1, SIDE, step, 0)

    def start_weight(x, x_mate, src, dst):
        over_x(lambda p: copy_to(x, (me_s, p), src, dst.at[me_c]).start())
        copy_to(x, (me_s, mate), src, dst.at[me_c], x_mate).start()
        dst[me_c] = src[...]

    def pass_weight(x, x_mate, dst):
        arrived(x, dst.at[pl.ds(0, SIDE - 1)])
        over_x(lambda p: copy_to(x_mate, (me_s, mate), dst.at[p], dst.at[p]).start())

    def wait_weight(x_mate, dst):
        arrived(x_mate, dst.at[pl.ds(0, SIDE)])

    def sent_weight(x, x_mate, dst):
        sent(x, dst.at[pl.ds(0, SIDE)])
        sent(x_mate, dst.at[pl.ds(0, SIDE - 1)])

    start_weight(X_WGATE, X_WGATE_MATE, wg_own, wg_all)
    start_weight(X_WOUT, X_WOUT_MATE, w_out, wo_all)

    upper = onehot(iota((LANE, LANE), 0) < iota((LANE, LANE), 1))
    ones = jnp.ones((LANE, LANE), BF16)
    owner_ids = iota((S, LANE), 0)

    def own_onehot(owners):
        mine = jnp.where((owners & 7) == me_c, owners >> 3, -1)
        return jnp.where(owner_ids == mine, 1.0, 0.0)

    def mark(m, carry):
        ohs[pl.ds(pl.multiple_of(m * S, S), S), :] = own_onehot(nown[m]).astype(BF16)
        return carry

    lax.fori_loop(0, 64, mark, 0, unroll=4)
    inner[...] = dot(ohs[...], upper)
    total[...] = dot(ohs[...], ones)
    key_ids = iota((LANE, LANE), 0).astype(F32)
    lane_row = iota((1, LANE), 1)

    def key_of(hot, rank, offset):
        found = jnp.sum(hot * (rank + 1.0), axis=0, keepdims=True)
        place = jnp.where(found > 0.5, found - 1.0 + offset, -1.0)
        return jnp.where(key_ids == place, 1.0, 0.0).astype(BF16)

    def value_of(hot, rows):
        high = (rows >> 8).astype(F32)
        low = (rows & 255).astype(F32)
        pieces = [hot * high, hot * low, hot * lane_row.astype(F32), hot]
        return jnp.concatenate(pieces, axis=0).astype(BF16)

    odd = lax.rem(me_s, 2)
    neg_offset = (odd * NEG).astype(F32)
    tgt_offset = ((1 - odd) * NEG + me_s - odd).astype(F32)

    def place(m, before):
        rows = pl.ds(pl.multiple_of(m * S, S), S)
        lanes = pl.ds(pl.multiple_of(m * LANE, LANE), LANE)
        hot = ohs[rows, :].astype(F32)
        keys[:, lanes] = key_of(hot, inner[rows, :] + before, neg_offset)
        vals[:, lanes] = value_of(hot, nrow[pl.ds(m, 1), :])
        return before + total[rows, :]

    lax.fori_loop(0, 64, place, jnp.zeros((S, LANE), F32), unroll=4)
    hot = own_onehot(town[...])
    rank = dot(hot.astype(BF16), upper)
    found = dot(vals[...], keys[...], 1, 1) + dot(
        value_of(hot, trow[...]), key_of(hot, rank, tgt_offset), 1, 1
    )
    high, low, pos, filled = (found[i * S : (i + 1) * S].astype(I32) for i in range(4))
    entry = (high * 256 + low) * LANE + pos
    req_msg[:, 0, :] = jnp.where(filled > 0, entry, -1)
    start_seq(X_REQ, lambda p: req_msg.at[p], req_all)
    req_all[me_s] = req_msg[me_s]

    wait_seq(X_CONV, rcv1)
    rf[...] = rcv1[...].astype(F32)
    xpad[0:16, :] = jnp.zeros((16, LANE), F32)
    later = iota((LANE, LANE), 1) >= iota((LANE, LANE), 0)
    for k in range(3):
        xpad[16:272, :] = rf[:, k * 8 : (k + 1) * 8, :].reshape(256, LANE)
        x4[...] = jnp.concatenate(
            [xpad[16 - 4 * j : 272 - 4 * j, :] for j in range(4)], axis=1
        ).astype(BF16)
        acc[...] = jnp.zeros_like(acc)
        prev = jnp.zeros((LANE, LANE), F32)
        for e in range(16):
            tiles = []
            for j in range(4):
                d = 4 * e + j
                row = 24 + 2 * k + d % 2
                chunk = jnp.broadcast_to(rf[d // 2, row : row + 1, :], (LANE, LANE))
                turned = pltpu.roll(chunk, 0, 1, stride=1, stride_axis=0)
                tiles.append(jnp.where(later, turned, prev).astype(BF16))
                prev = turned
            taps_tile = jnp.concatenate(tiles, axis=0)
            acc[16 * e :, :] += dot(x4[0 : 256 - 16 * e, :], taps_tile)
        for s in range(S):
            msgf[s * 32 + k * 8 : s * 32 + k * 8 + 8, :] = acc[s * 8 : s * 8 + 8, :]
    msg2[...] = msgf[...].reshape(S, 32, LANE).astype(BF16)
    start_seq(X_BACK, lambda p: msg2.at[p], rcv2)
    rcv2[me_s] = msg2[me_s]

    wait_seq(X_REQ, req_all)
    asked = req_all[:, 0, :]
    asked = asked.reshape(GROUPS, 2, LANE)
    even_half, odd_half = asked[:, 0, :], asked[:, 1, :]
    first_half = iota((GROUPS, LANE), 1) < NEG
    tab_own[...] = jnp.full(tab_own.shape, -1, I32)
    tab_own[0:GROUPS, :] = jnp.where(first_half, even_half, odd_half)
    tab_own[GROUPS : GROUPS + 1, :] = jnp.max(
        jnp.where(first_half, odd_half, even_half), axis=0, keepdims=True
    )
    start_ch(X_TABLE, lambda p: tab_own, tab_all.at[0])
    tab_all[0, me_c] = tab_own[...]

    def table_along_y(p):
        copy_to(X_TABLE_Y, split_peer(False, p), tab_own, tab_all.at[1, me_v]).start()

    over(C, me_v, table_along_y)
    tab_all[1, me_v] = tab_own[...]
    loads[5].wait()

    def turn(i, carry):
        span = pl.ds(pl.multiple_of(i * 256, 256), 256)
        cat_t[0:FULL, span] = cat[span, :].T
        return carry

    lax.fori_loop(0, ITEMS // 256, turn, 0)
    cat_t[FULL : FULL + 16, :] = jnp.broadcast_to(cnt[...].astype(F32), (16, ITEMS)).astype(BF16)

    row_scale[...] = jnp.zeros_like(row_scale)
    row_log[...] = jnp.zeros_like(row_log)
    item_ids = iota((ITEMS, LANE), 0)

    def picked(group):
        return onehot(item_ids == (tab_own[pl.ds(group, 1), :] >> 7))

    def keep(found, width, group0):
        for i in range(width // LANE):
            lanes = slice(i * LANE, (i + 1) * LANE)
            for c in range(C):
                rows_send[group0 + i, c] = found[c * CH : (c + 1) * CH, lanes].astype(BF16)
            if width > LANE:
                mine = jnp.where(group0 < HALF, me_c, me_v)
                rows_all[group0 + i, mine] = rows_send[group0 + i, mine]
        square = jnp.sum(found[0:FULL] * found[0:FULL], axis=0, keepdims=True)
        scale = lax.rsqrt(square / FULL + EPSILON) / (FULL * SOFTMAX_TEMP)
        logs = jnp.log(jnp.maximum(found[FULL : FULL + 1], 1.0))
        for i in range(width // LANE):
            row_scale[pl.ds(group0 + i, 1), :] = scale[:, i * LANE : (i + 1) * LANE]
            row_log[pl.ds(group0 + i, 1), :] = logs[:, i * LANE : (i + 1) * LANE]

    def send_rows(x, span, to, along_x):
        mine = jnp.where(along_x, me_c, me_v)

        def fn(p):
            src, dst = rows_send.at[span, p], rows_all.at[to, mine]
            copy_to(x, split_peer(along_x, p), src, dst).start()

        over(C, mine, fn)

    def chunk_at(i):
        return jnp.where(i == 0, 0, jnp.where(i == 1, 1, jnp.where(i == 2, 4, jnp.where(i == 3, 5, jnp.where(i == 4, 6, jnp.where(i == 5, 7, jnp.where(i == 6, 2, 3)))))))

    def send_chunk(h):
        send_rows(X_ROWS + h, pl.ds(2 * h, 2), pl.ds(2 * h, 2), h < CHUNKS // 2)

    def fetch(first, last):
        def step(i, carry):
            h = chunk_at(i)
            hot = jnp.concatenate([picked(2 * h), picked(2 * h + 1)], axis=1)
            keep(dot(cat_t[...], hot), 256, 2 * h)

            @pl.when((h != 1) & (h != 2) & (h != 3))
            def _():
                send_chunk(h)

            return carry

        lax.fori_loop(first, last, step, 0)

    def fetch_targets():
        keep(dot(cat_t[...], picked(GROUPS)), LANE, GROUPS)
        rows_all[GROUPS, me_c] = rows_send[GROUPS, me_c]
        rows_all[GROUPS + 1, me_v] = rows_send[GROUPS, me_v]
        send_rows(X_ROWS + CHUNKS, GROUPS, GROUPS, True)
        send_rows(X_ROWS + CHUNKS + 1, GROUPS, GROUPS + 1, False)

    def each_chunk(fn):
        def step(h, carry):
            fn(X_ROWS + h, rows_all.at[pl.ds(2 * h, 2), pl.ds(0, C - 1)])
            return carry

        lax.fori_loop(0, CHUNKS, step, 0)
        for i in range(2):
            fn(X_ROWS + CHUNKS + i, rows_all.at[GROUPS + i, pl.ds(0, C - 1)])

    fetch(0, 5)
    pass_weight(X_WGATE, X_WGATE_MATE, wg_all)
    wait_ch(X_SIG, sig_all)

    wait_seq(X_BACK, rcv2)
    rf[...] = rcv2[...].astype(F32)
    msgf[...] = rf[...].reshape(S * 32, LANE)
    diag = iota((CH, CH), 0) == iota((CH, CH), 1)
    gain_col = jnp.sum(jnp.where(diag, gain[...], 0.0), axis=1, keepdims=True)
    for q in range(8):
        conv = jnp.concatenate(
            [msgf[pl.ds(k * 8 + q, S, stride=32), :] for k in range(3)], axis=0
        )
        mix_send[q] = (conv + gain_col * sig_send[q].astype(F32)).astype(BF16)
    start_ch(X_MIX, lambda p: mix_send.at[p], mix_all)
    mix_all[me_c] = mix_send[me_c]
    send_chunk(1)
    pass_weight(X_WOUT, X_WOUT_MATE, wo_all)

    wait_weight(X_WGATE_MATE, wg_all)
    gate_t[...] = dot(wg_all[...].reshape(FULL, FULL), sig_all[...].reshape(FULL, LANE))
    fetch(5, 8)
    wait_weight(X_WOUT_MATE, wo_all)
    wo_t[...] = wo_all[...].reshape(FULL, FULL).T
    wait_ch(X_MIX, mix_all)
    mix = mix_all[...].reshape(FULL, LANE).astype(F32) * gate_t[...]
    lo_send[...] = dot(wo_t[...], mix.astype(BF16)).astype(BF16).reshape(C, CH, LANE)
    start_ch(X_OUT, lambda p: lo_send.at[p], lo_all)
    lo_all[me_c] = lo_send[me_c]
    send_chunk(2)
    send_chunk(3)

    fetch_targets()

    wait_ch(X_TABLE, tab_all.at[0])
    wait_ch(X_TABLE_Y, tab_all.at[1])
    pair_ids = iota((2 * LANE, LANE), 0)

    def slots(g, carry):
        for c in range(C):
            entry = tab_all[g // HALF, c, pl.ds(g, 1), :]
            target = jnp.where(entry < 0, -1, (entry & 127) + jnp.where(lane_row < NEG, 0, LANE))
            ohp[g, :, c * LANE : (c + 1) * LANE] = onehot(pair_ids == target)
        return carry

    lax.fori_loop(0, GROUPS, slots, 0)
    wide_ids = iota((8 * LANE, LANE), 0)
    part_of = lane_row >> 4
    for o, lane0 in enumerate(TGT_LANES):
        entry = jnp.full((1, LANE), -1, I32)
        for c in range(C):
            listed = tab_all[o % 2, c, GROUPS : GROUPS + 1, :]
            turned = pltpu.roll(listed, (16 * c - lane0) % LANE, 1)
            entry = jnp.where(part_of == c, turned, entry)
        target = jnp.where(entry < 0, -1, ((lane_row & 15) >> 1) * LANE + (entry & 127))
        oht[o] = onehot(wide_ids == target)
    tab_t[...] = jnp.full(tab_t.shape, -1.0, F32)
    tab_t[0:24, :] = jnp.where(tab_own[...] < 0, -1, tab_own[...] & 127).astype(F32)
    columns = tab_t[...].T
    pos_ids = iota((LANE, LANE), 1).astype(F32)
    for g in range(GROUPS + 1):
        slot_pos[g] = onehot(columns[:, g : g + 1] == pos_ids)

    tok_pos = spos[...]
    pos_in = tok_pos >> 2
    where_in = ((pos_in >> 7) * 4 + (tok_pos & 3)) * LANE + (pos_in & 127)
    pick = onehot(iota((TOK, LANE), 0) == where_in)

    wait_ch(X_OUT, lo_all)
    lo_t = jnp.concatenate([lo_all[q] for q in range(8)], axis=1)
    q_own[...] = dot(lo_t, pick).astype(BF16)

    def layer_at(i):
        near = (i + 1) // 2
        return lax.rem(me_z + jnp.where(lax.rem(i, 2) == 1, near, layers - near), layers)

    def along_z(fn):
        def step(i, carry):
            fn(layer_at(i))
            return carry

        lax.fori_loop(1, layers, step, 0)

    def go_on(z):
        block = z * SIDE + me_y
        first = z < layers // 2
        src = q_stage.at[z]

        def step(j, carry):
            y = jnp.where(first, j, me_x)
            x = jnp.where(first, me_x, j)
            here = (y == me_y) & (x == me_x)

            @pl.when(jnp.logical_not(here))
            def _():
                way = jnp.where(first, X_FORWARD, X_ACROSS)
                copy_to(way, beside(y, x), src, q_all.at[block], X_WAY + z).start()

            @pl.when(here)
            def _():
                q_all[block] = q_stage[z]

            return carry

        lax.fori_loop(0, SIDE, step, 0)

    q_stage[me_z] = q_own[...]
    along_z(
        lambda z: copy_to(
            X_QUERY, (z * SIDE + me_y, me_c), q_own, q_stage.at[me_z], X_LAYER + me_z
        ).start()
    )
    go_on(me_z)
    for q in range(8):
        out_ref[q % 4, :, (q // 4) * LANE : (q // 4 + 1) * LANE] = lo_all[q]

    def take_layer(z):
        arrived(X_LAYER + z, q_own)
        go_on(z)

    along_z(take_layer)

    def take_blocks(z):
        three = (z < layers // 2) | on_diagonal

        @pl.when(three)
        def _():
            arrived(X_WAY + z, q_all.at[pl.ds(0, SIDE - 1)])

        @pl.when(jnp.logical_not(three))
        def _():
            arrived(X_WAY + z, q_all.at[pl.ds(0, SIDE)])

    part[...] = jnp.zeros_like(part)

    def pair(g, carry):
        both = jnp.concatenate([q_all[2 * g], q_all[2 * g + 1]], axis=1)
        query = dot(both, ohp[g])
        for c in range(C):
            one = query[:, c * LANE : (c + 1) * LANE]
            rows = rows_all[g, c].astype(F32)
            place = pl.ds(lax.rem(g, HALF), 1)
            square_place = pl.ds(16 + lax.rem(g, HALF), 1)
            part[g // HALF, c, place, :] = jnp.sum(one * rows, axis=0, keepdims=True)
            part[g // HALF, c, square_place, :] = jnp.sum(one * one, axis=0, keepdims=True)
        return carry

    def take_rows(h, like):
        arrived(X_ROWS + h, like)

    def layer(i, carry):
        z = layer_at(i)
        take_rows(z, rows_all.at[pl.ds(2 * z, 2), pl.ds(0, C - 1)])
        take_blocks(z)
        pair(2 * z, 0)
        pair(2 * z + 1, 0)
        return carry

    lax.fori_loop(0, layers, layer, 0)
    for i in range(2):
        take_rows(CHUNKS + i, rows_all.at[GROUPS + i, pl.ds(0, C - 1)])
    tgt_rows = []
    for o, lane0 in enumerate(TGT_LANES):
        rows = jnp.zeros((CH, LANE), F32)
        for c in range(C):
            there = rows_all[GROUPS + o % 2, c].astype(F32)
            turned = pltpu.roll(there, (16 * c - lane0) % LANE, 1)
            rows = jnp.where(part_of == c, turned, rows)
        tgt_rows.append(rows)
    tgt_part = [[[jnp.zeros((1, LANE), F32)] * 2 for _ in range(C)] for _ in range(2)]
    for o, lane0 in enumerate(TGT_LANES):
        wide = jnp.concatenate([q_all[b] for b in TGT_BLOCKS[o]], axis=1)
        one = dot(wide, oht[o])
        for i, rows in enumerate((tgt_rows[o], one)):
            both = jnp.sum(one * rows, axis=0, keepdims=True)
            for c in range(C):
                turned = pltpu.roll(both, (lane0 - 16 * c) % LANE, 1)
                ours = (lane_row >= lane0) & (lane_row < lane0 + 16)
                tgt_part[o % 2][c][i] = jnp.where(ours, turned, tgt_part[o % 2][c][i])
    for way in range(2):
        for c in range(C):
            part[way, c, HALF : HALF + 1, :] = tgt_part[way][c][0]
            part[way, c, 16 + HALF : 17 + HALF, :] = tgt_part[way][c][1]
    start_ch(X_PART, lambda p: part.at[0, p], part_all.at[0])
    part_all[0, me_c] = part[0, me_c]

    def part_along_y(p):
        copy_to(X_PART_Y, split_peer(False, p), part.at[1, p], part_all.at[1, me_v]).start()

    over(C, me_v, part_along_y)
    part_all[1, me_v] = part[1, me_v]
    wait_ch(X_PART, part_all.at[0])
    wait_ch(X_PART_Y, part_all.at[1])
    by_x, by_y = jnp.sum(part_all[0], axis=0), jnp.sum(part_all[1], axis=0)
    whole = jnp.concatenate(
        [
            piece
            for i in (0, 16)
            for piece in (by_x[i : i + 8], by_y[i : i + 8], by_x[i + 8 : i + 16] + by_y[i + 8 : i + 16])
        ],
        axis=0,
    )
    query_scale = lax.rsqrt(whole[24:48] / FULL + EPSILON)
    logit = whole[0:24] * query_scale * row_scale[...] - row_log[...]
    filled = tab_own[...] >= 0
    exp_neg = jnp.where(filled, jnp.exp(logit), 0.0)[0:GROUPS]
    halves = [jnp.where(first_half, exp_neg, 0.0), jnp.where(first_half, 0.0, exp_neg)]
    exp_parts = jnp.concatenate([p for half in halves for p in split_parts(half, 2)], axis=0)
    tgt_logit = jnp.where(filled, logit, 0.0)[GROUPS : GROUPS + 1]
    block_of = 2 * ((lane_row & 63) >> 1) + jnp.where(lane_row < NEG, 1, 0)
    by_block = jnp.where(iota((S, LANE), 0) == block_of, tgt_logit, 0.0)
    tgt_parts = jnp.concatenate(split_parts(by_block, 3), axis=0)
    targets = dot(tgt_parts, slot_pos[GROUPS])
    targets = targets[0:S] + targets[S : 2 * S] + targets[2 * S : 3 * S]
    sums[:, 1, :] = targets
    for g in range(GROUPS):
        found = dot(exp_parts, slot_pos[g])
        sums[2 * g, 0:1, :] = found[g : g + 1] + found[16 + g : 17 + g]
        sums[2 * g + 1, 0:1, :] = found[32 + g : 33 + g] + found[48 + g : 49 + g]
    start_seq(X_SUMS, lambda p: sums.at[p], sums_all)
    sums_all[me_s] = sums[me_s]
    wait_seq(X_SUMS, sums_all)
    fin[...] = jnp.sum(sums_all[...], axis=0)
    start_ch(X_FIN, lambda p: fin, fin_all)
    fin_all[me_c] = fin[...]
    wait_ch(X_FIN, fin_all)
    last = jnp.sum(fin_all[...], axis=0)
    target_logit = last[1:2]
    loss_ref[...] = jnp.log(jnp.exp(target_logit) + last[0:1]) - target_logit

    sent_seq(X_CONV, rcv1)
    sent_seq(X_REQ, req_all)
    sent_seq(X_BACK, rcv2)
    sent(X_QUERY, q_all.at[pl.ds(0, layers - 1)])
    sent(X_FORWARD, q_all.at[pl.ds(0, 12)])

    @pl.when(on_diagonal)
    def _():
        sent(X_ACROSS, q_all.at[pl.ds(0, 12)])

    @pl.when(jnp.logical_not(on_diagonal))
    def _():
        sent(X_ACROSS, q_all.at[pl.ds(0, 16)])

    sent_seq(X_SUMS, sums_all)
    sent_ch(X_SIG, sig_all)
    sent_weight(X_WGATE, X_WGATE_MATE, wg_all)
    sent_weight(X_WOUT, X_WOUT_MATE, wo_all)
    sent_ch(X_TABLE, tab_all.at[0])
    sent_ch(X_TABLE_Y, tab_all.at[1])
    each_chunk(sent)
    sent_ch(X_MIX, mix_all)
    sent_ch(X_OUT, lo_all)
    sent_ch(X_PART, part_all.at[0])
    sent_ch(X_PART_Y, part_all.at[1])
    sent_ch(X_FIN, fin_all)


def per_device(
    signal,
    filter_taps,
    skip_gain,
    w_gate,
    w_out,
    catalogue,
    item_draw_counts,
    sampled_pos,
    neg_owner,
    neg_row,
    target_owner,
    target_row,
):
    vmem = pl.BlockSpec(memory_space=pltpu.VMEM)
    scratch = [
        ((4, CH, 256), BF16),
        ((CH, 256), F32),
        ((1, CH), F32),
        ((CH, FULL), BF16),
        ((CH, FULL), BF16),
        ((ITEMS, FULL), BF16),
        ((1, ITEMS), I32),
        ((1, LANE), I32),
        ((64, 1, LANE), I32),
        ((64, LANE), I32),
        ((1, LANE), I32),
        ((1, LANE), I32),
        ((C, CH, LANE), BF16),
        ((C, CH, LANE), BF16),
        ((S * 32, LANE), F32),
        ((S, 32, LANE), BF16),
        ((S, 32, LANE), BF16),
        ((S, 32, LANE), F32),
        ((272, LANE), F32),
        ((256, 512), BF16),
        ((256, LANE), F32),
        ((S, 32, LANE), BF16),
        ((S, 32, LANE), BF16),
        ((C, CH, FULL), BF16),
        ((C, CH, FULL), BF16),
        ((FULL, FULL), BF16),
        ((FULL, LANE), F32),
        ((C, CH, LANE), BF16),
        ((C, CH, LANE), BF16),
        ((C, CH, LANE), BF16),
        ((C, CH, LANE), BF16),
        ((CH, LANE), BF16),
        ((S // SIDE, CH, LANE), BF16),
        ((S, CH, LANE), BF16),
        ((S, 1, LANE), I32),
        ((S, 1, LANE), I32),
        ((64 * S, LANE), BF16),
        ((64 * S, LANE), F32),
        ((64 * S, LANE), F32),
        ((LANE, 64 * LANE), BF16),
        ((LANE, 64 * LANE), BF16),
        ((24, LANE), I32),
        ((2, C, 24, LANE), I32),
        ((LANE, LANE), F32),
        ((FULL + 16, ITEMS), BF16),
        ((GROUPS + 1, C, CH, LANE), BF16),
        ((GROUPS + 2, C, CH, LANE), BF16),
        ((24, LANE), F32),
        ((24, LANE), F32),
        ((GROUPS, 2 * LANE, C * LANE), BF16),
        ((len(TGT_LANES), 8 * LANE, LANE), BF16),
        ((GROUPS + 1, LANE, LANE), BF16),
        ((2, C, 32, LANE), F32),
        ((2, C, 32, LANE), F32),
        ((S, 2, LANE), F32),
        ((S, 2, LANE), F32),
        ((2, LANE), F32),
        ((C, 2, LANE), F32),
    ]
    layer_out, loss = pl.pallas_call(
        body,
        out_shape=(
            jax.ShapeDtypeStruct((4, CH, 256), BF16),
            jax.ShapeDtypeStruct((1, LANE), F32),
        ),
        in_specs=[pl.BlockSpec(memory_space=pl.ANY)] * 12,
        out_specs=(vmem, vmem),
        scratch_shapes=[pltpu.VMEM(shape, kind) for shape, kind in scratch]
        + [pltpu.SemaphoreType.DMA((EXCHANGES,))] * 2
        + [pltpu.SemaphoreType.DMA((12,))],
        compiler_params=pltpu.CompilerParams(
            collective_id=0, has_side_effects=True, vmem_limit_bytes=60 * 1024 * 1024
        ),
        cost_estimate=pl.CostEstimate(
            flops=20_000_000_000, bytes_accessed=5_000_000, transcendentals=10_000
        ),
    )(
        signal.transpose(1, 2, 0),
        filter_taps.T,
        skip_gain.reshape(1, CH),
        w_gate.T,
        w_out,
        catalogue,
        item_draw_counts.reshape(1, ITEMS),
        sampled_pos.reshape(1, LANE),
        neg_owner.transpose(1, 2, 0),
        neg_row.T,
        target_owner.reshape(1, LANE),
        target_row.reshape(1, LANE),
    )
    return layer_out.transpose(2, 0, 1), loss.reshape(LANE)


def solution(mesh):
    placed = (
        P("seq", None, "ch"),
        P("seq", "ch"),
        P("ch"),
        P(None, "ch"),
        P("ch", None),
        P(("seq", "ch"), None),
        P(("seq", "ch")),
        P("seq"),
        P("seq", None, None),
        P("seq", None),
        P("seq", None),
        P("seq"),
    )
    return jax.shard_map(
        per_device,
        mesh=mesh,
        in_specs=placed,
        out_specs=(P("seq", None, "ch"), P("seq")),
        check_vma=False,
    )
```
